32 devices in a mesh: shots: 2 (over y), gx: 4 (over z), gy: 2 (over x), gz: 2 (over core).
Axes of the slice: x: 2, y: 2, z: 4, core: 2. Of those that a mesh axis runs over, the one named last changes fastest.
Arguments:
- forward_prev: float32 [64, 128, 256], P(('shots', 'gx'), 'gy', 'gz'), parts along dimension 0, may hold values from -1.8 to 1.8
- forward_now: float32 [64, 128, 256], P(('shots', 'gx'), 'gy', 'gz'), parts along dimension 0, may hold values from -1.8 to 1.8
- adjoint_prev: float32 [64, 128, 256], P(('shots', 'gx'), 'gy', 'gz'), parts along dimension 0, may hold values from -1.8 to 1.8
- adjoint_now: float32 [64, 128, 256], P(('shots', 'gx'), 'gy', 'gz'), parts along dimension 0, may hold values from -1.8 to 1.8
- model_table: float32 [2, 8192, 2, 128], P('gz', ('gx', 'gy')), may hold values from 0 to 0.3, as said below
- tile_owner: int32 [4, 4, 2, 512, 1], P(('shots', 'gz'), 'gx', 'gy'), parts along dimension 0, may hold values from 0 to 7; in each aligned block of 512 rows (0 to 511, 512 to 1023, ..., all dimensions but the last counted through in order) at most 128 rows name the same one
- tile_slot: int32 [4, 4, 2, 512], P(('shots', 'gz'), 'gx', 'gy'), parts along dimension 0, may hold values from 0 to 1023
- source_index: int32 [6], P('shots'), parts along dimension 0, may hold values from 0 to 31
- wavelet: float32 [32], P('shots'), parts along dimension 0, may hold values from -6 to 6
- receiver_depth: int32 [64, 128], P(('shots', 'gx'), 'gy'), parts along dimension 0, may hold values from 0 to 127
- traces: float32 [16, 64, 128], P(None, ('shots', 'gx'), 'gy'), parts along dimension 1, may hold values from -6 to 6
Outputs:
- forward_final: float32 [64, 128, 256], P(('shots', 'gx'), 'gy', 'gz'), parts along dimension 0
- adjoint_final: float32 [64, 128, 256], P(('shots', 'gx'), 'gy', 'gz'), parts along dimension 0
- model_gradient: float32 [2, 16384, 2, 128], P('gz', ('shots', 'gx', 'gy')), parts along dimension 1
The draws below stay inside these ranges and needn't reach their ends.
There are 2 independent parts, one for each index of `shots`. The reference program is written for one: setup_inputs(seed, part) draws one part's arguments, and reference() takes and returns one part's arrays. A program takes and returns all parts, laid end to end along the dimension named above; an argument that names none is the same for every part. Nothing has to cross between parts.
Inputs may be any that keep to these rules, and one draw needn't show every extreme that they name: `tile_owner`: among the 512 columns of one device's block, no owner is named more than 128 times, and in every draw some owner is named exactly 128 times by some block. `model_table`: component 0 lies in 0.04 to 0.14, component 1 in 0 to 0.3.
All inputs are finite; a program needn't handle non-finite values.
Results may differ from the reference program's by a relative error of at most 0.0003.
Values sent between devices are 32-bit elements; how exact they have to be, the bound alone decides.
No kernel may reach another device: no remote copies, remote signals or barrier semaphores. Data moves between devices by JAX's collectives and lax.ppermute only.
A program may use at most 64 MiB of HBM per device.

```python
import math
import jax
import jax.numpy as jnp
import numpy as np
from jax import lax

CX = 8
CY = 64
CZ = 128
OWN_DEV = 1024
STEPS = 16
NX = 32
NY = 128
NZ = 256
COLS = 512
CAP = 128
MODEL_COLS = 8192
N_GX = 4
N_GY = 2
N_GZ = 2


def draw_model_table(key, part):
    key = jax.random.fold_in(key, 11)
    first_key, second_key = jax.random.split(key)
    slowness = jax.random.uniform(first_key, (N_GZ, MODEL_COLS, 1, CZ), jnp.float32, 0.04, 0.14)
    epsilon = jax.random.uniform(second_key, (N_GZ, MODEL_COLS, 1, CZ), jnp.float32, 0.0, 0.3)
    return jnp.concatenate([slowness, epsilon], axis=2)


def plant(values, rng, low, high):
    extent = values.shape
    spot = [jax.random.randint(jax.random.fold_in(rng, axis), (), 0, extent[axis]) for axis in range(len(extent))]
    values = values.at[tuple(spot)].set(low)
    longest = extent.index(max(extent))
    spot[longest] = (spot[longest] + 1) % extent[longest]
    return values.at[tuple(spot)].set(high)


def block_scale(own_key, extent, cuts, least, largest):
    def one(axis_at, shards_of):
        draws = jax.random.uniform(jax.random.fold_in(jax.random.fold_in(own_key, 6), axis_at), (shards_of,), jnp.float32, least / len(cuts), largest / len(cuts))
        return jnp.repeat(jnp.exp(draws), extent[axis_at] // shards_of).reshape((-1,) + (1,) * (len(extent) - axis_at - 1))

    gain = one(*cuts[0])
    for cut in cuts[1:]:
        gain = gain * one(*cut)
    return gain


def assign_block(own_key, own, number, rows, amount, top, bound, lean):
    ranking = jax.random.permutation(own_key, amount)
    heavy_load, ordinary = portions_of(amount, rows * top, bound, lean, True), portions_of(amount, rows * top, bound, lean, False)
    places = jnp.arange(amount)

    def named(tallies, rotation):
        used = int((tallies > 0).sum())
        fixed = max(1, used // 4)
        passed = fixed + (places - fixed + rotation * (used - fixed)) % max(1, amount - fixed)
        return jnp.zeros((amount,), jnp.int32).at[ranking[jnp.where(places < fixed, places, passed)]].set(jnp.asarray(tallies, jnp.int32))

    tallies = jnp.where(number % 4 == 0, named(heavy_load, number // 4), named(ordinary, number - number // 4 - 1))
    mixed = jax.random.permutation(jax.random.fold_in(own, 3), amount)
    giver, taker = mixed[0:amount // 2 * 2:2], mixed[1:amount // 2 * 2:2]
    margin = jnp.minimum(tallies[giver] - 1, bound - tallies[taker]) // 2
    margin = jnp.where((giver == ranking[0]) | (taker == ranking[0]) | (tallies[taker] == 0), 0, jnp.maximum(margin, 0))
    passed = jax.random.randint(jax.random.fold_in(own, 4), (amount // 2,), 0, 1 << 20) % (margin + 1)
    tallies = tallies.at[giver].add(-passed).at[taker].add(passed)
    members = jnp.searchsorted(jnp.cumsum(tallies), jnp.arange(rows * top), side="right").astype(jnp.int32)
    grid = members.reshape(top, rows).T
    grid = grid[jax.random.permutation(jax.random.fold_in(own, 1), rows)]
    rotation = jax.random.randint(jax.random.fold_in(own, 2), (rows, 1), 0, top)
    return jnp.take_along_axis(grid, (jnp.arange(top)[None, :] + rotation) % top, axis=1)


def portions_of(amount, total, bound, skew, full):
    portions = [(1 << 20) // math.isqrt(standing ** skew) + 1 for standing in range(1, amount + 1)]
    largest = bound if full else min(bound, max(-(-total // amount), total * portions[0] // sum(portions)))
    least = 1 if total - largest >= amount - 1 else 0
    holding, rest = [largest] + [least] * (amount - 1), total - largest - least * (amount - 1)
    while rest > 0:
        movable = [i for i in range(1, amount) if holding[i] < largest] or [i for i in range(1, amount) if holding[i] < bound]
        whole, budget = sum([portions[i] for i in movable]), rest
        for i in movable:
            addition = min(bound - holding[i], max(1, budget * portions[i] // whole), rest)
            holding[i] = holding[i] + addition
            rest = rest - addition
    return np.array(holding)


def centred(own_key, dims, scale, bound, pieces=(), kind=jnp.bfloat16):
    array = jax.random.normal(own_key, dims, jnp.float32) * scale
    if len(pieces) > 0:
        array = block_scale(own_key, dims, pieces, -0.22, 0.18) * array
    return jnp.clip(array, min=-bound, max=bound).astype(kind)


def setup_inputs(seed: int = 0, part: int = 0) -> dict:
    streams_of = jax.random.split(jax.random.key(seed), 12)
    own_keys = jax.random.split(jax.random.fold_in(streams_of[11], part), 12)
    forward_prev = centred(own_keys[0], (NX, NY, NZ), 0.3, 1.8, ((0, 4), (1, 2), (2, 2)), jnp.float32)
    forward_now = centred(own_keys[1], (NX, NY, NZ), 0.3, 1.8, ((0, 4), (1, 2), (2, 2)), jnp.float32)
    adjoint_prev = centred(own_keys[2], (NX, NY, NZ), 0.3, 1.8, ((0, 4), (1, 2), (2, 2)), jnp.float32)
    adjoint_now = centred(own_keys[3], (NX, NY, NZ), 0.3, 1.8, ((0, 4), (1, 2), (2, 2)), jnp.float32)
    model_table = draw_model_table(jax.random.fold_in(streams_of[11], 71), part)
    tile_owner_keys = jax.random.split(jax.random.fold_in(own_keys[5], 1), N_GZ * N_GX * N_GY * COLS // COLS)
    tile_owner_turns = jax.random.permutation(jax.random.fold_in(own_keys[5], 3), N_GZ * N_GX * N_GY * COLS // COLS)
    tile_owner = jax.vmap(lambda own, number: assign_block(jax.random.fold_in(own_keys[5], 2), own, number, COLS, N_GX * N_GY, 1, CAP, 2))(tile_owner_keys, tile_owner_turns).reshape((N_GZ, N_GX, N_GY, COLS, 1))
    tile_slot = plant(jax.random.randint(own_keys[6], (N_GZ, N_GX, N_GY, COLS), 0, OWN_DEV), jax.random.fold_in(own_keys[6], 1), 0, OWN_DEV - 1).astype(jnp.int32)
    source_index = jax.random.randint(own_keys[7], (3,), 0, min(NX, NY, NZ)).astype(jnp.int32)
    wavelet = centred(own_keys[8], (STEPS,), 1.0, 6.0, (), jnp.float32)
    receiver_depth = plant(jax.random.randint(own_keys[9], (NX, NY), 0, NZ // 2), jax.random.fold_in(own_keys[9], 1), 0, (NZ // 2) - 1).astype(jnp.int32)
    traces = centred(own_keys[10], (STEPS, NX, NY), 1.0, 6.0, ((1, 4), (2, 2)), jnp.float32)
    return {"forward_prev": forward_prev, "forward_now": forward_now, "adjoint_prev": adjoint_prev, "adjoint_now": adjoint_now, "model_table": model_table, "tile_owner": tile_owner, "tile_slot": tile_slot, "source_index": source_index, "wavelet": wavelet, "receiver_depth": receiver_depth, "traces": traces}


STENCIL = (-205.0 / 72.0, 8.0 / 5.0, -1.0 / 5.0, 8.0 / 315.0, -1.0 / 560.0)


def derivatives(padded, shape):
    size_x, size_y, size_z = shape

    def window(off_x, off_y, off_z):
        return padded[4 + off_x:4 + off_x + size_x, 4 + off_y:4 + off_y + size_y, 4 + off_z:4 + off_z + size_z]

    center = window(0, 0, 0)
    along_x = STENCIL[0] * center
    along_y = STENCIL[0] * center
    along_z = STENCIL[0] * center
    for offset in range(1, 5):
        along_x = along_x + STENCIL[offset] * (window(offset, 0, 0) + window(-offset, 0, 0))
        along_y = along_y + STENCIL[offset] * (window(0, offset, 0) + window(0, -offset, 0))
        along_z = along_z + STENCIL[offset] * (window(0, 0, offset) + window(0, 0, -offset))
    return along_x + along_y, along_z


def propagate(previous, current, slow_coef, aniso_coef, padded):
    horizontal, vertical = derivatives(padded, current.shape)
    laplacian = (1.0 + 2.0 * aniso_coef) * horizontal + vertical
    following = (2.0 * current - previous) + slow_coef * laplacian
    return following, laplacian, horizontal


def reference(forward_prev, forward_now, adjoint_prev, adjoint_now, model_table, tile_owner, tile_slot, source_index, wavelet, receiver_depth, traces):
    column_ids = tile_owner[..., 0] * OWN_DEV + tile_slot
    depth_half = jnp.arange(N_GZ, dtype=jnp.int32)[:, None, None, None]
    column_rows = model_table[depth_half, column_ids]
    cell_params = column_rows.reshape(N_GZ, N_GX, N_GY, CX, CY, 2, CZ).transpose(5, 1, 3, 2, 4, 0, 6).reshape(2, NX, NY, NZ)
    slow_coef = cell_params[0]
    aniso_coef = cell_params[1]
    grid_x = jnp.arange(NX, dtype=jnp.int32)[:, None, None]
    grid_y = jnp.arange(NY, dtype=jnp.int32)[None, :, None]
    grid_z = jnp.arange(NZ, dtype=jnp.int32)[None, None, :]
    source_mask = ((grid_x == source_index[0]) & (grid_y == source_index[1]) & (grid_z == source_index[2])).astype(jnp.float32)
    receiver_mask = (grid_z == receiver_depth[:, :, None]).astype(jnp.float32)

    def forward(carried, weight):
        previous, current = carried
        following, laplacian, horizontal = propagate(previous, current, slow_coef, aniso_coef, jnp.pad(current, 4))
        following = following + weight * source_mask
        return (current, following), (laplacian, horizontal)

    (_, forward_final), (laplacians, horizontals) = lax.scan(forward, (forward_prev, forward_now), wavelet)

    def backward(carried, inputs):
        previous, current, grad_slow, grad_aniso = carried
        trace_row, laplacian, horizontal = inputs
        following, _, _ = propagate(previous, current, slow_coef, aniso_coef, jnp.pad(current, 4))
        following = following + trace_row[:, :, None] * receiver_mask
        grad_slow = grad_slow + following * laplacian
        grad_aniso = grad_aniso + following * (2.0 * slow_coef * horizontal)
        return (current, following, grad_slow, grad_aniso), None

    zero_field = jnp.zeros((NX, NY, NZ), jnp.float32)
    (_, adjoint_final, grad_slow, grad_aniso), _ = lax.scan(backward, (adjoint_prev, adjoint_now, zero_field, zero_field), (traces[::-1], laplacians[::-1], horizontals[::-1]))
    gradient = jnp.stack([grad_slow, grad_aniso]).reshape(2, N_GX, CX, N_GY, CY, N_GZ, CZ).transpose(5, 1, 3, 2, 4, 0, 6).reshape(N_GZ, N_GX, N_GY, COLS, 2, CZ)
    model_gradient = jnp.zeros((N_GZ, MODEL_COLS, 2, CZ), jnp.float32).at[depth_half, column_ids].add(gradient)
    return forward_final, adjoint_final, model_gradient
```

```python
import functools

import jax
import jax.numpy as jnp
import numpy as np
from jax import lax
from jax.experimental import pallas as pl
from jax.experimental.pallas import tpu as pltpu
from jax.sharding import PartitionSpec as P

STENCIL = (-205.0 / 72.0, 8.0 / 5.0, -1.0 / 5.0, 8.0 / 315.0, -1.0 / 560.0)


def with_halo(block, sides, width):
    for axis, dim in sides:
        count = lax.axis_size(axis)
        forward = [(i, i + 1) for i in range(count - 1)]
        backward = [(target, source) for source, target in forward]
        low = lax.ppermute(
            lax.slice_in_dim(block, block.shape[dim] - width, None, axis=dim), axis, forward
        )
        high = lax.ppermute(lax.slice_in_dim(block, 0, width, axis=dim), axis, backward)
        block = jnp.concatenate([low, block, high], axis=dim)
    return block


def derivatives(padded, shape):
    size_x, size_y, size_z = shape

    def window(off_x, off_y, off_z):
        return padded[
            4 + off_x : 4 + off_x + size_x,
            4 + off_y : 4 + off_y + size_y,
            4 + off_z : 4 + off_z + size_z,
        ]

    center = window(0, 0, 0)
    along_x = STENCIL[0] * center
    along_y = STENCIL[0] * center
    along_z = STENCIL[0] * center
    for offset in range(1, 5):
        along_x = along_x + STENCIL[offset] * (window(offset, 0, 0) + window(-offset, 0, 0))
        along_y = along_y + STENCIL[offset] * (window(0, offset, 0) + window(0, -offset, 0))
        along_z = along_z + STENCIL[offset] * (window(0, 0, offset) + window(0, 0, -offset))
    return (along_x + along_y, along_z)


def propagate(previous, current, slow_coef, aniso_coef, padded):
    horizontal, vertical = derivatives(padded, current.shape)
    laplacian = (1.0 + 2.0 * aniso_coef) * horizontal + vertical
    following = 2.0 * current - previous + slow_coef * laplacian
    return (following, laplacian, horizontal)


def block_body(
    forward_prev,
    forward_now,
    adjoint_prev,
    adjoint_now,
    model_table,
    tile_owner,
    tile_slot,
    source_index,
    wavelet,
    receiver_depth,
    traces,
):
    block_x, block_y, block_z = forward_now.shape
    columns = block_x * block_y
    owners_count = lax.axis_size(("gx", "gy"))
    capacity = max(2, 2 * columns // owners_count)
    column_owner = tile_owner.reshape(columns)
    column_slot = tile_slot.reshape(columns)
    local_table = model_table[0]
    held_count = local_table.shape[0]
    one_hot = (column_owner[:, None] == jnp.arange(owners_count, dtype=jnp.int32)[None, :]).astype(
        jnp.float32
    )
    earlier = (
        jnp.arange(columns, dtype=jnp.int32)[:, None]
        > jnp.arange(columns, dtype=jnp.int32)[None, :]
    ).astype(jnp.float32)
    counted_before = jnp.dot(earlier, one_hot, precision=lax.Precision.HIGHEST)
    slot_rank = jnp.sum(counted_before * one_hot, axis=1).astype(jnp.int32)
    requests = (
        jnp.full((owners_count, capacity), -1, jnp.int32)
        .at[column_owner, slot_rank]
        .set(column_slot)
    )
    received = lax.all_to_all(requests, ("gx", "gy"), split_axis=0, concat_axis=0, tiled=True)
    clipped = jnp.clip(received, 0, held_count - 1)
    fetched = lax.all_to_all(
        local_table[clipped], ("gx", "gy"), split_axis=0, concat_axis=0, tiled=True
    )
    cell_params = (
        fetched[column_owner, slot_rank].reshape(block_x, block_y, 2, block_z).transpose(2, 0, 1, 3)
    )
    slow_coef = cell_params[0]
    aniso_coef = cell_params[1]
    grid_x = lax.axis_index("gx") * block_x + jnp.arange(block_x, dtype=jnp.int32)[:, None, None]
    grid_y = lax.axis_index("gy") * block_y + jnp.arange(block_y, dtype=jnp.int32)[None, :, None]
    grid_z = lax.axis_index("gz") * block_z + jnp.arange(block_z, dtype=jnp.int32)[None, None, :]
    source_mask = (
        (grid_x == source_index[0]) & (grid_y == source_index[1]) & (grid_z == source_index[2])
    ).astype(jnp.float32)
    receiver_mask = (grid_z == receiver_depth[:, :, None]).astype(jnp.float32)

    def forward(carried, weight):
        previous, current = carried
        padded = with_halo(current, (("gx", 0), ("gy", 1), ("gz", 2)), 4)
        following, laplacian, horizontal = propagate(
            previous, current, slow_coef, aniso_coef, padded
        )
        following = following + weight * source_mask
        return ((current, following), (laplacian, horizontal))

    (_, forward_final), (laplacians, horizontals) = lax.scan(
        forward, (forward_prev, forward_now), wavelet
    )

    def backward(carried, inputs):
        previous, current, grad_slow, grad_aniso = carried
        trace_row, laplacian, horizontal = inputs
        padded = with_halo(current, (("gx", 0), ("gy", 1), ("gz", 2)), 4)
        following, _, _ = propagate(previous, current, slow_coef, aniso_coef, padded)
        following = following + trace_row[:, :, None] * receiver_mask
        grad_slow = grad_slow + following * laplacian
        grad_aniso = grad_aniso + following * (2.0 * slow_coef * horizontal)
        return ((current, following, grad_slow, grad_aniso), None)

    zero_field = jnp.zeros((block_x, block_y, block_z), jnp.float32)
    (_, adjoint_final, grad_slow, grad_aniso), _ = lax.scan(
        backward,
        (adjoint_prev, adjoint_now, zero_field, zero_field),
        (traces[::-1], laplacians[::-1], horizontals[::-1]),
    )
    grad_cells = (
        jnp.stack([grad_slow, grad_aniso]).transpose(1, 2, 0, 3).reshape(columns, 2, block_z)
    )
    outgoing = (
        jnp.zeros((owners_count, capacity, 2, block_z), jnp.float32)
        .at[column_owner, slot_rank]
        .set(grad_cells)
    )
    returned = lax.all_to_all(outgoing, ("gx", "gy"), split_axis=0, concat_axis=0, tiled=True)
    target = jnp.where(received < 0, held_count, received).reshape(owners_count * capacity)
    model_gradient = (
        jnp.zeros((held_count, 2, block_z), jnp.float32)
        .at[target]
        .add(returned.reshape(owners_count * capacity, 2, block_z), mode="drop")
    )
    return (forward_final, adjoint_final, model_gradient[None])


BX, BY, BZ = 8, 64, 128
GX, GY = 4, 2
NXA, NYA = BX * GX, BY * GY
ZS = 16
ZE = 32
HALO = 8
OWN = slice(HALO, HALO + ZS)
SCALE = 5040.0
PADX = 4
STEPS = 16
ROUNDS = STEPS // 2
MIB = 1 << 20
F32 = jnp.float32
BF16 = jnp.bfloat16
H, IX, IY, SHOT, LINE, SX, SY, SZ = range(8)


def slabs_fit(mesh):
    names = ("shots", "gx", "gy", "gz")
    return tuple(mesh.shape[n] for n in names) == (2, GX, GY, 2)


def line_device(place):
    chip, core = divmod(place, 2)
    ix, iy = (chip, 0) if chip < GX else (2 * GX - 1 - chip, 1)
    return (ix * GY + iy) * 2 + core


def off_chip_pairs():
    count = 2 * GX * GY
    pairs = []
    for low in range(1, count, 2):
        a, b = line_device(low), line_device((low + 1) % count)
        pairs += [(a, b), (b, a)]
    return pairs


OFF_PAIRS = off_chip_pairs()
SWAP = [(0, 1), (1, 0)]


def to_sibling(x):
    return lax.ppermute(x, "gz", SWAP)


def to_off_chip(x):
    return lax.ppermute(x, ("gx", "gy", "gz"), OFF_PAIRS)


def band(size):
    out = np.zeros((size, size), np.float32)
    for offset in range(1, 5):
        value = round(STENCIL[offset] * SCALE)
        for i in range(size - offset):
            out[i, i + offset] = value
            out[i + offset, i] = value
    return out


def matrices():
    along_y = band(NYA)
    along_y = np.concatenate([along_y, along_y], 0)
    along_z = band(ZE)
    full = np.kron(np.eye(8, dtype=np.float32), along_z)
    own = np.kron(np.eye(8, dtype=np.float32), along_z[OWN])
    return [jnp.asarray(m, BF16) for m in (along_y, full, own)]


def vmem(count):
    return [pl.BlockSpec(memory_space=pltpu.VMEM)] * count


SMEM = pl.BlockSpec(memory_space=pltpu.SMEM)


def call(kernel, outs, specs, scratch=(), limit=24, flops=0, moved=0, aliases=None):
    return pl.pallas_call(
        kernel,
        out_shape=[jax.ShapeDtypeStruct(s, d) for s, d in outs],
        in_specs=specs,
        out_specs=vmem(len(outs)),
        scratch_shapes=list(scratch),
        input_output_aliases=aliases or {},
        compiler_params=pltpu.CompilerParams(vmem_limit_bytes=limit * MIB),
        cost_estimate=pl.CostEstimate(flops=flops, bytes_accessed=moved, transcendentals=0),
    )


def half_lanes(shape):
    return lax.broadcasted_iota(jnp.int32, shape, len(shape) - 1) < BY


def roll_half(x):
    return pltpu.roll(x, BY, x.ndim - 1)


def place(scal, chunk):
    chip, core = divmod(chunk, 2)
    mine = core == scal[H]
    return mine, jnp.where(scal[H] == 0, chip, GX - 1 - chip)


def pack_table(scal, table, keep, give):
    first = scal[SHOT] * 1024
    for q in range(4):
        for comp in range(2):
            rows = table[pl.ds(first + q * 256 + comp, 128, stride=2), :]
            turned = rows.T
            for chunk in range(8):
                mine, g = place(scal, chunk)
                piece = turned[chunk * ZS : (chunk + 1) * ZS][None]

                @pl.when(mine)
                def _():
                    keep[pl.ds(g, 1), q, comp * ZS : (comp + 1) * ZS, :] = piece

                @pl.when(jnp.logical_not(mine))
                def _():
                    give[pl.ds(g, 1), q, comp * ZS : (comp + 1) * ZS, :] = piece


def pack_fields(scal, *refs):
    fields, (keep, give) = refs[:4], refs[4:]
    for f in range(4):
        for i in range(4):
            pair = fields[f][2 * i : 2 * i + 2].reshape(128, 128)
            turned = pair.T
            for chunk in range(8):
                mine, g = place(scal, chunk)
                piece = turned[chunk * ZS : (chunk + 1) * ZS][None]

                @pl.when(mine)
                def _():
                    keep[pl.ds(g, 1), f, i] = piece

                @pl.when(jnp.logical_not(mine))
                def _():
                    give[pl.ds(g, 1), f, i] = piece


def unpack_small(scal, mine, other, ids_slab, ids_owner, depth, traces):
    low = half_lanes((8, 128))
    h = scal[H]
    for ix in range(GX):
        rows = slice(ix * BX, (ix + 1) * BX)
        for ref, is_mine in ((mine, True), (other, False)):
            a, b = ref[ix * GY], ref[ix * GY + 1]
            core = h if is_mine else 1 - h
            for tt in range(4):
                even = jnp.where(low, a[tt], roll_half(b[tt]))
                odd = jnp.where(low, roll_half(a[tt]), b[tt])
                traces[pl.ds(core * 8 + 2 * tt, 1), rows, :] = even[None]
                traces[pl.ds(core * 8 + 2 * tt + 1, 1), rows, :] = odd[None]
            ids = jnp.where(low, a[4], roll_half(b[4])).astype(jnp.int32)
            if is_mine:
                ids_owner[rows, :] = ids
                depth[rows, :] = jnp.where(low, roll_half(a[4]), b[4]).astype(jnp.int32)

            @pl.when(core == scal[IY])
            def _():
                ids_slab[rows, :] = ids


def gather_half(second, scal, table, ids, *refs):
    if second:
        before, out, sib, off = refs
    else:
        (out,) = refs
    half = 1 - scal[SHOT] if second else scal[SHOT]

    def column(x, carry):
        row = ids[pl.ds(x, 1), :]
        chunk = row >> 7
        local = jnp.where(((chunk >> 2) & 1) == half, ((chunk >> 3) << 2) | (chunk & 3), -1)
        lane = jnp.broadcast_to(row & 127, (8, 128))
        local = jnp.broadcast_to(local, (8, 128))
        if second:
            totals = [before[x, 8 * t : 8 * t + 8, :] for t in range(4)]
        else:
            totals = [jnp.zeros((8, 128), F32) for t in range(4)]
        for j in range(32):
            hit = local == j
            for t in range(4):
                value = jnp.take_along_axis(
                    table[j // 4, j % 4, 8 * t : 8 * t + 8, :], lane, axis=1, mode="promise_in_bounds"
                )
                totals[t] = jnp.where(hit, value, totals[t])
        for t in range(4):
            out[x, 8 * t : 8 * t + 8, :] = totals[t]
        return carry

    lax.fori_loop(0, NXA, column, 0)
    if second:
        h = scal[H]
        for comp in range(2):
            rows = slice(comp * HALO, (comp + 1) * HALO)
            sib[:, rows, :] = out[:, pl.ds(comp * ZS + HALO * (1 - h), HALO), :]
            off[:, rows, :] = out[:, pl.ds(comp * ZS + HALO * h, HALO), :]


def is_edge(scal):
    return (scal[LINE] == 0) | (scal[LINE] == 2 * GX * GY - 1)


def extend_coefs(scal, coefs, sib, off, slow, aniso):
    sib_at = (ZE - HALO) * (1 - scal[H])
    off_at = (ZE - HALO) * scal[H]
    inside = jnp.where(is_edge(scal), 0.0, 1.0)
    slow[:, OWN, :] = coefs[:, 0:ZS, :]
    slow[:, pl.ds(sib_at, HALO), :] = sib[:, 0:HALO, :]
    slow[:, pl.ds(off_at, HALO), :] = off[:, 0:HALO, :] * inside
    aniso[:, OWN, :] = 1.0 + 2.0 * coefs[:, ZS:, :]
    aniso[:, pl.ds(sib_at, HALO), :] = 1.0 + 2.0 * sib[:, HALO:, :]
    aniso[:, pl.ds(off_at, HALO), :] = 1.0 + 2.0 * off[:, HALO:, :]


def unpack_fields(scal, got, *outs):
    low = half_lanes((ZS, 128))
    h = scal[H]
    for kind in range(2):
        prev, now, sib, off = outs[4 * kind : 4 * kind + 4]
        for step, own in ((0, prev), (1, now)):
            f = 2 * kind + step
            for ix in range(GX):
                for i in range(4):
                    a, b = got[ix * GY, f, i], got[ix * GY + 1, f, i]
                    x = ix * BX + 2 * i
                    own[x] = jnp.where(low, a, roll_half(b))
                    own[x + 1] = jnp.where(low, roll_half(a), b)
            sib[step] = own[:, pl.ds(HALO * (1 - h), HALO), :]
            off[step] = own[:, pl.ds(HALO * h, HALO), :]


def ranks_of(owner, owners):
    masks = jnp.concatenate(
        [(owner[ix * BX : (ix + 1) * BX] == o).astype(F32) for ix in range(GX) for o in owners], axis=0
    )
    rows = masks.shape[0]
    first = lax.broadcasted_iota(jnp.int32, (128, 128), 0)
    second = lax.broadcasted_iota(jnp.int32, (128, 128), 1)
    before = (first < second).astype(F32).astype(BF16)
    bits = masks.astype(BF16)
    along = jnp.dot(bits, before, preferred_element_type=F32)
    sums = jnp.dot(bits, jnp.ones((128, 128), BF16), preferred_element_type=F32)
    r0 = lax.broadcasted_iota(jnp.int32, (rows, rows), 0)
    r1 = lax.broadcasted_iota(jnp.int32, (rows, rows), 1)
    earlier = (((r0 >> 3) == (r1 >> 3)) & (r1 < r0)).astype(F32).astype(BF16)
    above = jnp.dot(earlier, sums.astype(BF16), preferred_element_type=F32)
    return jnp.where(masks > 0.0, along + above, -1.0).astype(jnp.int32)


def index_kernel(scal, ids_slab, ids_owner, out, ranks, acc):
    me = scal[IX] * GY + scal[IY]
    ranks[0:256] = ranks_of(ids_slab[...] >> 10, list(range(8)))
    ranks[256:288] = ranks_of(ids_owner[...] >> 10, [me])
    acc[...] = jnp.full((256, 128), -1, jnp.int32)
    lanes = lax.broadcasted_iota(jnp.int32, (256, 128), 1)
    places = lax.broadcasted_iota(jnp.int32, (256, 128), 0)

    def combo(n, carry):
        is_slab = n < 32
        ix = jnp.where(is_slab, n >> 3, n - 32)
        found = jnp.full((256, 128), -1, jnp.int32)
        for x in range(BX):
            row = jnp.broadcast_to(ranks[pl.ds(n * BX + x, 1), :], (256, 128))
            slots = ids_owner[pl.ds(ix * BX + x, 1), :] & 1023
            column = x * 128 + lax.broadcasted_iota(jnp.int32, (1, 128), 1)
            value = jnp.broadcast_to(jnp.where(is_slab, column, slots), (256, 128))
            found = jnp.where(row == places, value, found)
        best = jnp.max(found, axis=1, keepdims=True)
        acc[...] = jnp.where(lanes == n, jnp.broadcast_to(best, (256, 128)), acc[...])
        return carry

    lax.fori_loop(0, 36, combo, 0)
    turned = acc[...].astype(F32).T[0:40].astype(jnp.int32)
    out[0] = turned[:, 0:128]
    out[1] = turned[:, 128:256]


def stencil(field, g, along_y, along_z, own):
    rows = slice(PADX + 8 * g, PADX + 8 * g + 8)
    zs = OWN if own else slice(0, ZE)
    depth = ZS if own else ZE
    whole = field[rows].reshape(8 * ZE, 128)
    high = whole.astype(BF16)
    rest = (whole - high.astype(F32)).astype(BF16)
    both = jnp.concatenate([high, rest], axis=1)
    my = jnp.dot(both, along_y[...], preferred_element_type=F32).reshape(8, ZE, 128)[:, zs]
    mz = jnp.dot(along_z[...], both, preferred_element_type=F32)
    mz = (mz[:, :128] + mz[:, 128:]).reshape(8, depth, 128)
    center = field[rows, zs, :]
    hor = my * (1.0 / SCALE) + (2.0 * STENCIL[0]) * center
    for i in range(1, 5):
        up = field[PADX + 8 * g + i : PADX + 8 * g + 8 + i, zs, :]
        down = field[PADX + 8 * g - i : PADX + 8 * g + 8 - i, zs, :]
        hor = hor + STENCIL[i] * (up + down)
    ver = mz * (1.0 / SCALE) + STENCIL[0] * center
    return center, hor, ver


def round_kernel(kind, r, scal, *refs):
    refs = list(refs)
    take = lambda n: [refs.pop(0) for _ in range(n)]
    first, later, last = r == 0, r >= ROUNDS // 2, r == ROUNDS - 1
    if kind == "u":
        (weights,) = take(1)
    else:
        traces, depth = take(2)
    own, sib, off = take(3)
    (prev,) = take(1)
    slow, aniso, along_y, along_z, along_z_own = take(5)
    if later:
        if kind == "u":
            partner_mid, partner_end = take(2)
        else:
            (partner,) = take(1)
        if r > ROUNDS // 2:
            (total_in,) = take(1)
    out_own, out_mid = take(2)
    if not last:
        out_sib, out_off = take(2)
    if later:
        (total,) = take(1)
    elif kind == "u":
        (history,) = take(1)
    e0, e1 = take(2)

    h = scal[H]
    sib_at = (ZE - HALO) * (1 - h)
    off_at = (ZE - HALO) * h
    edge = is_edge(scal)
    zero = jnp.zeros((PADX, ZE, 128), F32)
    for e in (e0, e1):
        e[0:PADX] = zero
        e[PADX + NXA :] = zero
    inner = slice(PADX, PADX + NXA)
    now = 1 if first else 0
    e0[inner, OWN, :] = own[...]
    e0[inner, pl.ds(sib_at, HALO), :] = sib[now]
    e0[inner, pl.ds(off_at, HALO), :] = jnp.where(edge, 0.0, off[now])
    if first:
        out_mid[:, OWN, :] = prev[...]
        out_mid[:, pl.ds(sib_at, HALO), :] = sib[0]
        out_mid[:, pl.ds(off_at, HALO), :] = jnp.where(edge, 0.0, off[0])
        prev = out_mid
    top = scal[LINE] * ZS - HALO

    def source(weight, depth_rows, start):
        shape = (1, depth_rows, 128)
        z = lax.broadcasted_iota(jnp.int32, shape, 1) + start
        y = lax.broadcasted_iota(jnp.int32, shape, 2)
        return jnp.where((z == scal[SZ]) & (y == scal[SY]), weight, 0.0)

    def receivers(t, g, depth_rows, start):
        z = lax.broadcasted_iota(jnp.int32, (depth_rows, 128), 0) + start
        out = []
        for x in range(8 * g, 8 * g + 8):
            at = jnp.broadcast_to(depth[x : x + 1, :], (depth_rows, 128))
            value = jnp.broadcast_to(traces[t, x : x + 1, :], (depth_rows, 128))
            out.append(jnp.where(z == at, value, 0.0)[None])
        return jnp.concatenate(out, axis=0)

    for step in range(2):
        t = 2 * r + step
        field = e1 if step else e0
        depth_rows = ZS if step else ZE
        start = top + HALO if step else top
        for g in range(4):
            xs = slice(8 * g, 8 * g + 8)
            zs = OWN if step else slice(0, ZE)
            center, hor, ver = stencil(field, g, along_y, along_z_own if step else along_z, step)
            before = e0[PADX + 8 * g : PADX + 8 * g + 8, OWN, :] if step else prev[xs]
            lap = aniso[xs, zs, :] * hor + ver
            following = 2.0 * center - before + slow[xs, zs, :] * lap
            if kind == "a":
                following = following + receivers(STEPS - 1 - t, g, depth_rows, start)
            if step:
                out_own[xs] = following
            else:
                e1[PADX + 8 * g : PADX + 8 * g + 8] = following
            if step == 0:
                hor, ver = hor[:, OWN], ver[:, OWN]
            if kind == "u" and not later:
                history[2 * step, xs] = hor
                history[2 * step + 1, xs] = ver
            if later:
                if kind == "u":
                    other = partner_mid[xs, OWN, :] if step else partner_end[xs]
                    hor_part, ver_part = hor, ver
                else:
                    other = following if step else following[:, OWN]
                    hor_part = partner[2 * (1 - step), xs]
                    ver_part = partner[2 * (1 - step) + 1, xs]
                sum_h, sum_v = other * hor_part, other * ver_part
                if step:
                    sum_h, sum_v = total[0, xs] + sum_h, total[1, xs] + sum_v
                elif r > ROUNDS // 2:
                    sum_h, sum_v = total_in[0, xs] + sum_h, total_in[1, xs] + sum_v
                total[0, xs] = sum_h
                total[1, xs] = sum_v
        if kind == "u":
            if step:
                row = out_own[pl.ds(scal[SX], 1)]
                out_own[pl.ds(scal[SX], 1)] = row + source(weights[t], ZS, start)
            else:
                row = e1[pl.ds(PADX + scal[SX], 1)]
                e1[pl.ds(PADX + scal[SX], 1)] = row + source(weights[t], ZE, start)
    out_mid[...] = e1[inner]
    if not last:
        out_sib[0] = out_own[:, pl.ds(HALO * (1 - h), HALO), :]
        out_off[0] = out_own[:, pl.ds(HALO * h, HALO), :]


def pack_out(scal, u, a, total_u, total_a, coefs, index, out, grads):
    for x in range(NXA):
        gh = total_u[0, x] + total_a[0, x]
        gv = total_u[1, x] + total_a[1, x]
        slow, aniso = coefs[x, 0:ZS, :], coefs[x, ZS:, :]
        grads[x, 0:ZS, :] = (1.0 + 2.0 * aniso) * gh + gv
        grads[x, ZS:, :] = (2.0 * slow) * gh
    low = half_lanes((ZS, 128))
    for f, field in enumerate((u, a)):
        for ix in range(GX):
            for i in range(4):
                x0, x1 = field[ix * BX + 2 * i], field[ix * BX + 2 * i + 1]
                at = 256 + (f * 4 + i) * ZS
                out[ix * GY, at : at + ZS, :] = jnp.where(low, x0, roll_half(x1))
                out[ix * GY + 1, at : at + ZS, :] = jnp.where(low, roll_half(x0), x1)

    def combo(n, carry):
        ix, o = n >> 3, n & 7
        for part in range(2):
            row = index[part, pl.ds(n, 1), :]
            lane = jnp.broadcast_to(row & 127, (8, 128))
            which = jnp.broadcast_to(row >> 7, (8, 128))
            totals = [jnp.zeros((8, 128), F32) for t in range(4)]
            for x in range(BX):
                hit = which == x
                for t in range(4):
                    value = jnp.take_along_axis(
                        grads[ix * BX + x, 8 * t : 8 * t + 8, :], lane, axis=1, mode="promise_in_bounds"
                    )
                    totals[t] = jnp.where(hit, value, totals[t])
            for t in range(4):
                at = pl.multiple_of((ix * 2 + part) * 32 + 8 * t, 8)
                out[o, pl.ds(at, 8), :] = totals[t]
        return carry

    lax.fori_loop(0, 32, combo, 0)


def finish(scal, got, other, index, u_out, a_out, model, turned, columns):
    h = scal[H]
    sources = []
    for ix in range(GX):
        chip = jnp.where(h == 0, ix, GX - 1 - ix)
        base = chip * 2 * ZS
        sources.append((got, ix, True, base + h * ZS))
        sources.append((other, ix, False, base + (1 - h) * ZS))

    def piece(ref, ix, mine, start, count):
        if mine:
            return ref[ix, pl.ds(h, 1), start : start + count, :].reshape(count, 128)
        return ref[ix, start : start + count, :]

    for f, out in enumerate((u_out, a_out)):
        for i in range(4):
            for ref, ix, mine, z0 in sources:
                turned[pl.ds(pl.multiple_of(z0, ZS), ZS), :] = piece(ref, ix, mine, 256 + (f * 4 + i) * ZS, ZS)
            out[2 * i : 2 * i + 2] = turned[...].T.reshape(2, BY, 128)
    for n in range(8):
        for comp in range(2):
            for ref, ix, mine, z0 in sources:
                rows = pl.ds(pl.multiple_of(comp * 128 + z0, ZS), ZS)
                columns[rows, n * 128 : (n + 1) * 128] = piece(ref, ix, mine, n * 32 + comp * ZS, ZS)
    values = columns[...]
    high = values.astype(BF16)
    rest = (values - high.astype(F32)).astype(BF16)
    named = jnp.concatenate(
        [index[n % 2, 32 + n // 2 : 33 + n // 2, :] for n in range(8)], axis=1
    )
    for block in range(4):
        slot = lax.broadcasted_iota(jnp.int32, (256, 1024), 0) + block * 256
        pick = (slot == jnp.broadcast_to(named, (256, 1024))).astype(F32).astype(BF16)
        dims = (((1,), (1,)), ((), ()))
        sums = lax.dot_general(pick, high, dims, preferred_element_type=F32)
        sums = sums + lax.dot_general(pick, rest, dims, preferred_element_type=F32)
        for comp in range(2):
            model[pl.ds(block * 512 + comp, 256, stride=2), :] = sums[:, comp * 128 : (comp + 1) * 128]


def by_half(h, mine, other):
    first = jnp.where(h == 0, mine, other)
    second = jnp.where(h == 0, other, mine)
    both = jnp.stack([first, second], axis=1)
    return both.reshape((GX * GY,) + mine.shape[1:])


def exchange(x):
    return lax.all_to_all(x, ("gx", "gy"), split_axis=0, concat_axis=0, tiled=True)


def slab_body(
    forward_prev,
    forward_now,
    adjoint_prev,
    adjoint_now,
    model_table,
    tile_owner,
    tile_slot,
    source_index,
    wavelet,
    receiver_depth,
    traces,
):
    h = lax.axis_index("gz")
    ix, iy = lax.axis_index("gx"), lax.axis_index("gy")
    chip = jnp.where(iy == 0, ix, 2 * GX - 1 - ix)
    line = 2 * chip + h
    scal = jnp.stack(
        [h, ix, iy, lax.axis_index("shots"), line, source_index[0], source_index[1], source_index[2]]
    ).astype(jnp.int32)

    table = model_table.reshape(2048, 128)
    keep, give = call(
        pack_table, [((4, 4, 32, 128), F32)] * 2, [SMEM] + vmem(1), moved=2 * MIB, flops=1 << 20
    )(scal, table)
    table_chunks = by_half(h, keep, to_sibling(give))
    ids = (tile_owner.reshape(BX, BY) * 1024 + tile_slot.reshape(BX, BY)).astype(F32)
    small = jnp.concatenate([ids, receiver_depth.astype(F32)], axis=1)[None]
    trace_half = lax.dynamic_slice_in_dim(traces, h * 8, 8, axis=0).reshape(4, 2, BX, BY)
    trace_half = trace_half.transpose(0, 2, 1, 3).reshape(4, BX, 128)
    small = jnp.concatenate([trace_half, small], axis=0).reshape(1, 40, 128)
    small = jnp.broadcast_to(small, (8, 40, 128))
    sent = jnp.concatenate([table_chunks.reshape(8, 128, 128), small], axis=1)
    arrived = exchange(sent)
    table_mine = arrived[:, :128].reshape(8, 4, 32, 128)
    small_mine = arrived[:, 128:].reshape(8, 5, 8, 128)
    table_other = lax.ppermute(table_mine, "shots", SWAP)
    small_other = to_sibling(small_mine)

    keep, give = call(
        pack_fields, [((4, 4, 4, ZS, 128), F32)] * 2, [SMEM] + vmem(4), moved=2 * MIB, flops=1 << 20
    )(scal, forward_prev, forward_now, adjoint_prev, adjoint_now)
    fields = exchange(by_half(h, keep, to_sibling(give)))

    ids_slab, ids_owner, depth, traces = call(
        unpack_small,
        [((NXA, 128), jnp.int32)] * 3 + [((STEPS, NXA, 128), F32)],
        [SMEM] + vmem(2),
        moved=MIB // 2,
        flops=1 << 20,
    )(scal, small_mine, small_other)
    coef_shape = ((NXA, 2 * ZS, 128), F32)
    half_shape = ((NXA, 2 * HALO, 128), F32)
    (coefs,) = call(
        functools.partial(gather_half, False), [coef_shape], [SMEM] + vmem(2), moved=MIB, flops=1 << 24
    )(scal, table_mine, ids_slab)
    coefs, coefs_sib, coefs_off = call(
        functools.partial(gather_half, True),
        [coef_shape, half_shape, half_shape],
        [SMEM] + vmem(3),
        moved=2 * MIB,
        flops=1 << 24,
    )(scal, table_other, ids_slab, coefs)
    ext_shape = ((NXA, ZE, 128), F32)
    own_shape = ((NXA, ZS, 128), F32)
    slow, aniso = call(extend_coefs, [ext_shape] * 2, [SMEM] + vmem(3), moved=2 * MIB, flops=1 << 20)(
        scal, coefs, to_sibling(coefs_sib), to_off_chip(coefs_off)
    )
    (index,) = call(
        index_kernel,
        [((2, 40, 128), jnp.int32)],
        [SMEM] + vmem(2),
        [pltpu.VMEM((288, 128), jnp.int32), pltpu.VMEM((256, 128), jnp.int32)],
        moved=MIB // 4,
        flops=1 << 24,
    )(scal, ids_slab, ids_owner)

    first_halo = ((2, NXA, HALO, 128), F32)
    unpacked = call(
        unpack_fields,
        [own_shape, own_shape, first_halo, first_halo] * 2,
        [SMEM] + vmem(1),
        moved=4 * MIB,
        flops=1 << 20,
    )(scal, fields)
    bands = matrices()
    halo = ((1, NXA, HALO, 128), F32)
    state = {}
    for n, kind in enumerate("ua"):
        prev, now, sib, off = unpacked[4 * n : 4 * n + 4]
        state[kind] = [now, to_sibling(sib), to_off_chip(off), prev]
    history, mids, ends, totals = {}, {}, {}, {}
    for r in range(ROUNDS):
        for kind in "ua":
            later, last = r >= ROUNDS // 2, r == ROUNDS - 1
            drive = [wavelet] if kind == "u" else [traces, depth]
            specs = [SMEM] + ([SMEM] if kind == "u" else vmem(2))
            args = state[kind] + [slow, aniso] + bands
            if later:
                partner = ROUNDS - 1 - r
                args += [mids[partner], ends[partner]] if kind == "u" else [history[partner]]
                if r > ROUNDS // 2:
                    args += [totals[kind]]
            specs = specs + vmem(len(args))
            outs = [own_shape, ext_shape] + ([] if last else [halo, halo])
            if later:
                outs.append(((2, NXA, ZS, 128), F32))
            elif kind == "u":
                outs.append(((4, NXA, ZS, 128), F32))
            res = call(
                functools.partial(round_kernel, kind, r),
                outs,
                specs,
                [pltpu.VMEM((NXA + 2 * PADX, ZE, 128), F32)] * 2,
                moved=4 * MIB,
                flops=1 << 24,
            )(scal, *drive, *args)
            own, mid = res[0], res[1]
            if later:
                totals[kind] = res[-1]
            elif kind == "u":
                history[r] = res[-1]
            if kind == "a":
                mids[r], ends[r] = mid, own
            if last:
                state[kind] = [own]
            else:
                state[kind] = [own, to_sibling(res[2]), to_off_chip(res[3]), mid]

    (packed,) = call(
        pack_out,
        [((8, 384, 128), F32)],
        [SMEM] + vmem(6),
        [pltpu.VMEM((NXA, 2 * ZS, 128), F32)],
        moved=4 * MIB,
        flops=1 << 24,
    )(scal, state["u"][0], state["a"][0], totals["u"], totals["a"], coefs, index)
    got = exchange(packed).reshape(GX, GY, 384, 128)
    other = to_sibling(lax.dynamic_index_in_dim(got, 1 - h, axis=1, keepdims=False))
    u, a, model = call(
        finish,
        [((BX, BY, BZ), F32)] * 2 + [((2048, 128), F32)],
        [SMEM] + vmem(3),
        [pltpu.VMEM((128, 128), F32), pltpu.VMEM((256, 1024), F32)],
        moved=4 * MIB,
        flops=1 << 28,
    )(scal, got, other, index)
    return (u, a, model.reshape(1, 1024, 2, 128))


def solution(mesh):
    in_specs = (
        P(("shots", "gx"), "gy", "gz"),
        P(("shots", "gx"), "gy", "gz"),
        P(("shots", "gx"), "gy", "gz"),
        P(("shots", "gx"), "gy", "gz"),
        P("gz", ("gx", "gy"), None, None),
        P(("shots", "gz"), "gx", "gy", None, None),
        P(("shots", "gz"), "gx", "gy", None),
        P("shots"),
        P("shots"),
        P(("shots", "gx"), "gy"),
        P(None, ("shots", "gx"), "gy"),
    )
    out_specs = (
        P(("shots", "gx"), "gy", "gz"),
        P(("shots", "gx"), "gy", "gz"),
        P("gz", ("shots", "gx", "gy"), None, None),
    )
    body = slab_body if slabs_fit(mesh) else block_body
    return jax.shard_map(body, mesh=mesh, in_specs=in_specs, out_specs=out_specs, check_vma=False)
```

```python
import functools

import jax
import jax.numpy as jnp
import numpy as np
from jax import lax
from jax.experimental import pallas as pl
from jax.experimental.pallas import tpu as pltpu
from jax.sharding import PartitionSpec as P

STENCIL = (-205.0 / 72.0, 8.0 / 5.0, -1.0 / 5.0, 8.0 / 315.0, -1.0 / 560.0)


def with_halo(block, sides, width):
    for axis, dim in sides:
        count = lax.axis_size(axis)
        forward = [(i, i + 1) for i in range(count - 1)]
        backward = [(target, source) for source, target in forward]
        low = lax.ppermute(
            lax.slice_in_dim(block, block.shape[dim] - width, None, axis=dim), axis, forward
        )
        high = lax.ppermute(lax.slice_in_dim(block, 0, width, axis=dim), axis, backward)
        block = jnp.concatenate([low, block, high], axis=dim)
    return block


def derivatives(padded, shape):
    size_x, size_y, size_z = shape

    def window(off_x, off_y, off_z):
        return padded[
            4 + off_x : 4 + off_x + size_x,
            4 + off_y : 4 + off_y + size_y,
            4 + off_z : 4 + off_z + size_z,
        ]

    center = window(0, 0, 0)
    along_x = STENCIL[0] * center
    along_y = STENCIL[0] * center
    along_z = STENCIL[0] * center
    for offset in range(1, 5):
        along_x = along_x + STENCIL[offset] * (window(offset, 0, 0) + window(-offset, 0, 0))
        along_y = along_y + STENCIL[offset] * (window(0, offset, 0) + window(0, -offset, 0))
        along_z = along_z + STENCIL[offset] * (window(0, 0, offset) + window(0, 0, -offset))
    return (along_x + along_y, along_z)


def propagate(previous, current, slow_coef, aniso_coef, padded):
    horizontal, vertical = derivatives(padded, current.shape)
    laplacian = (1.0 + 2.0 * aniso_coef) * horizontal + vertical
    following = 2.0 * current - previous + slow_coef * laplacian
    return (following, laplacian, horizontal)


def block_body(
    forward_prev,
    forward_now,
    adjoint_prev,
    adjoint_now,
    model_table,
    tile_owner,
    tile_slot,
    source_index,
    wavelet,
    receiver_depth,
    traces,
):
    block_x, block_y, block_z = forward_now.shape
    columns = block_x * block_y
    owners_count = lax.axis_size(("gx", "gy"))
    capacity = max(2, 2 * columns // owners_count)
    column_owner = tile_owner.reshape(columns)
    column_slot = tile_slot.reshape(columns)
    local_table = model_table[0]
    held_count = local_table.shape[0]
    one_hot = (column_owner[:, None] == jnp.arange(owners_count, dtype=jnp.int32)[None, :]).astype(
        jnp.float32
    )
    earlier = (
        jnp.arange(columns, dtype=jnp.int32)[:, None]
        > jnp.arange(columns, dtype=jnp.int32)[None, :]
    ).astype(jnp.float32)
    counted_before = jnp.dot(earlier, one_hot, precision=lax.Precision.HIGHEST)
    slot_rank = jnp.sum(counted_before * one_hot, axis=1).astype(jnp.int32)
    requests = (
        jnp.full((owners_count, capacity), -1, jnp.int32)
        .at[column_owner, slot_rank]
        .set(column_slot)
    )
    received = lax.all_to_all(requests, ("gx", "gy"), split_axis=0, concat_axis=0, tiled=True)
    clipped = jnp.clip(received, 0, held_count - 1)
    fetched = lax.all_to_all(
        local_table[clipped], ("gx", "gy"), split_axis=0, concat_axis=0, tiled=True
    )
    cell_params = (
        fetched[column_owner, slot_rank].reshape(block_x, block_y, 2, block_z).transpose(2, 0, 1, 3)
    )
    slow_coef = cell_params[0]
    aniso_coef = cell_params[1]
    grid_x = lax.axis_index("gx") * block_x + jnp.arange(block_x, dtype=jnp.int32)[:, None, None]
    grid_y = lax.axis_index("gy") * block_y + jnp.arange(block_y, dtype=jnp.int32)[None, :, None]
    grid_z = lax.axis_index("gz") * block_z + jnp.arange(block_z, dtype=jnp.int32)[None, None, :]
    source_mask = (
        (grid_x == source_index[0]) & (grid_y == source_index[1]) & (grid_z == source_index[2])
    ).astype(jnp.float32)
    receiver_mask = (grid_z == receiver_depth[:, :, None]).astype(jnp.float32)

    def forward(carried, weight):
        previous, current = carried
        padded = with_halo(current, (("gx", 0), ("gy", 1), ("gz", 2)), 4)
        following, laplacian, horizontal = propagate(
            previous, current, slow_coef, aniso_coef, padded
        )
        following = following + weight * source_mask
        return ((current, following), (laplacian, horizontal))

    (_, forward_final), (laplacians, horizontals) = lax.scan(
        forward, (forward_prev, forward_now), wavelet
    )

    def backward(carried, inputs):
        previous, current, grad_slow, grad_aniso = carried
        trace_row, laplacian, horizontal = inputs
        padded = with_halo(current, (("gx", 0), ("gy", 1), ("gz", 2)), 4)
        following, _, _ = propagate(previous, current, slow_coef, aniso_coef, padded)
        following = following + trace_row[:, :, None] * receiver_mask
        grad_slow = grad_slow + following * laplacian
        grad_aniso = grad_aniso + following * (2.0 * slow_coef * horizontal)
        return ((current, following, grad_slow, grad_aniso), None)

    zero_field = jnp.zeros((block_x, block_y, block_z), jnp.float32)
    (_, adjoint_final, grad_slow, grad_aniso), _ = lax.scan(
        backward,
        (adjoint_prev, adjoint_now, zero_field, zero_field),
        (traces[::-1], laplacians[::-1], horizontals[::-1]),
    )
    grad_cells = (
        jnp.stack([grad_slow, grad_aniso]).transpose(1, 2, 0, 3).reshape(columns, 2, block_z)
    )
    outgoing = (
        jnp.zeros((owners_count, capacity, 2, block_z), jnp.float32)
        .at[column_owner, slot_rank]
        .set(grad_cells)
    )
    returned = lax.all_to_all(outgoing, ("gx", "gy"), split_axis=0, concat_axis=0, tiled=True)
    target = jnp.where(received < 0, held_count, received).reshape(owners_count * capacity)
    model_gradient = (
        jnp.zeros((held_count, 2, block_z), jnp.float32)
        .at[target]
        .add(returned.reshape(owners_count * capacity, 2, block_z), mode="drop")
    )
    return (forward_final, adjoint_final, model_gradient[None])


BX, BY, BZ = 8, 64, 128
GX, GY = 4, 2
NXA, NYA = BX * GX, BY * GY
ZS = 16
ZE = 32
HALO = 8
OWN = slice(HALO, HALO + ZS)
SCALE = 5040.0
UNSCALE = 1.0
PADX = 4
STEPS = 16
ROUNDS = STEPS // 2
MIB = 1 << 20
F32 = jnp.float32
BF16 = jnp.bfloat16
H, IX, IY, SHOT, LINE, SX, SY, SZ = range(8)


def slabs_fit(mesh):
    names = ("shots", "gx", "gy", "gz")
    return tuple(mesh.shape[n] for n in names) == (2, GX, GY, 2)


def line_device(place):
    chip, core = divmod(place, 2)
    ix, iy = (chip, 0) if chip < GX else (2 * GX - 1 - chip, 1)
    return (ix * GY + iy) * 2 + core


def off_chip_pairs():
    count = 2 * GX * GY
    pairs = []
    for low in range(1, count, 2):
        a, b = line_device(low), line_device((low + 1) % count)
        pairs += [(a, b), (b, a)]
    return pairs


OFF_PAIRS = off_chip_pairs()
SWAP = [(0, 1), (1, 0)]


def to_sibling(x):
    return lax.ppermute(x, "gz", SWAP)


def to_off_chip(x):
    return lax.ppermute(x, ("gx", "gy", "gz"), OFF_PAIRS)


def spread(e):
    return [(2 * s + c, 2 * (s ^ e ^ c) + (s & 1)) for s in range(GX * GY) for c in range(2)]


def to_blocks(x, e):
    return lax.ppermute(x, ("gx", "gy", "gz"), spread(e))


FAR_FIRST = (6, 7, 4, 5, 2, 3, 0, 1)


def slab_of(scal, e):
    ix = scal[IX] ^ (e >> 1)
    core = scal[IY] ^ (e & 1) ^ scal[H]
    chip = jnp.where(scal[H] == 0, ix, GX - 1 - ix)
    return pl.multiple_of(chip * 2 * ZS + core * ZS, ZS)


def block_of(scal, e):
    return (scal[IX] * GY + scal[IY]) ^ e ^ scal[H]


def band(size):
    out = np.zeros((size, size), np.float32)
    for offset in range(1, 5):
        value = round(STENCIL[offset] * SCALE)
        for i in range(size - offset):
            out[i, i + offset] = value
            out[i + offset, i] = value
    return out


def matrices():
    along_y = band(NYA)
    along_y = np.concatenate([along_y, along_y], 0)
    along_z = band(ZE)
    full = np.kron(np.eye(8, dtype=np.float32), along_z)
    own = np.kron(np.eye(8, dtype=np.float32), along_z[OWN])
    return [jnp.asarray(m, BF16) for m in (along_y, full, own)]


def vmem(count):
    return [pl.BlockSpec(memory_space=pltpu.VMEM)] * count


SMEM = pl.BlockSpec(memory_space=pltpu.SMEM)


def call(kernel, outs, specs, scratch=(), limit=24, flops=0, moved=0, aliases=None):
    return pl.pallas_call(
        kernel,
        out_shape=[jax.ShapeDtypeStruct(s, d) for s, d in outs],
        in_specs=specs,
        out_specs=vmem(len(outs)),
        scratch_shapes=list(scratch),
        input_output_aliases=aliases or {},
        compiler_params=pltpu.CompilerParams(vmem_limit_bytes=limit * MIB),
        cost_estimate=pl.CostEstimate(flops=flops, bytes_accessed=moved, transcendentals=0),
    )


def half_lanes(shape):
    return lax.broadcasted_iota(jnp.int32, shape, len(shape) - 1) < BY


def roll_half(x):
    return pltpu.roll(x, BY, x.ndim - 1)


def place(scal, chunk):
    chip, core = divmod(chunk, 2)
    mine = core == scal[H]
    return mine, jnp.where(scal[H] == 0, chip, GX - 1 - chip)


def pack_small(owner, slot, depth, traces, out):
    for tt in range(4):
        out[tt] = jnp.concatenate([traces[2 * tt], traces[2 * tt + 1]], axis=1)
    low = half_lanes((1, 128))
    ids = owner[...] * 1024 + slot[...]
    rows = []
    for x in range(BX):
        pair = ids[:, (x // 2) * 128 : (x // 2 + 1) * 128].astype(F32)
        rows.append(roll_half(pair) if x % 2 else pair)
    rows = jnp.concatenate(rows, axis=0)
    depths = depth[...].astype(F32)
    depths = jnp.concatenate([depths, depths], axis=1)
    out[4] = jnp.where(half_lanes((8, 128)), rows, depths)


def pack_table(scal, table, keep, give):
    first = scal[SHOT] * 1024
    for q in range(4):
        for comp in range(2):
            turned = table[pl.ds(first + q * 256 + comp, 128, stride=2), :].T
            at = q * 32 + comp * ZS
            for chunk in range(8):
                mine, g = place(scal, chunk)
                piece = turned[chunk * ZS : (chunk + 1) * ZS][None]

                @pl.when(mine)
                def _():
                    keep[pl.ds(g, 1), at : at + ZS, :] = piece

                @pl.when(jnp.logical_not(mine))
                def _():
                    give[pl.ds(g, 1), at : at + ZS, :] = piece


def assemble(scal, keep, got, small, out):
    h = scal[H]
    for ix in range(GX):
        out[pl.ds(ix * GY + h, 1), 0:128, :] = keep[ix][None]
        out[pl.ds(ix * GY + 1 - h, 1), 0:128, :] = got[ix][None]
    for n in range(GX * GY):
        out[n, 128:, :] = small[...].reshape(40, 128)


def pack_fields(scal, *refs):
    fields, (keep, give) = refs[:4], refs[4:]
    for f in range(4):
        for i in range(4):
            pair = fields[f][2 * i : 2 * i + 2].reshape(128, 128)
            turned = pair.T
            for chunk in range(8):
                mine, g = place(scal, chunk)
                piece = turned[chunk * ZS : (chunk + 1) * ZS][None]

                @pl.when(mine)
                def _():
                    keep[pl.ds(g, 1), f, i] = piece

                @pl.when(jnp.logical_not(mine))
                def _():
                    give[pl.ds(g, 1), f, i] = piece


def unpack_small(scal, mine, other, ids_slab, ids_owner, depth, traces):
    low = half_lanes((8, 128))
    h = scal[H]
    for ix in range(GX):
        rows = slice(ix * BX, (ix + 1) * BX)
        for ref, is_mine in ((mine, True), (other, False)):
            a, b = ref[ix * GY], ref[ix * GY + 1]
            core = h if is_mine else 1 - h
            for tt in range(4):
                even = jnp.where(low, a[tt], roll_half(b[tt]))
                odd = jnp.where(low, roll_half(a[tt]), b[tt])
                traces[pl.ds(core * 8 + 2 * tt, 1), rows, :] = even[None]
                traces[pl.ds(core * 8 + 2 * tt + 1, 1), rows, :] = odd[None]
            ids = jnp.where(low, a[4], roll_half(b[4])).astype(jnp.int32)
            if is_mine:
                ids_owner[rows, :] = ids
                depth[rows, :] = jnp.where(low, roll_half(a[4]), b[4]).astype(jnp.int32)

            @pl.when(core == scal[IY])
            def _():
                ids_slab[rows, :] = ids


def gather_half(second, scal, table, ids, *refs):
    if second:
        before, out, sib, off = refs
    else:
        (out,) = refs
    half = 1 - scal[SHOT] if second else scal[SHOT]

    def column(x, carry):
        row = ids[pl.ds(x, 1), :]
        lane = jnp.broadcast_to(row & 127, (8, 128))
        chunk = jnp.broadcast_to(row >> 7, (8, 128))
        if second:
            totals = [before[x, 8 * t : 8 * t + 8, :] for t in range(4)]
        else:
            totals = [jnp.zeros((8, 128), F32) for t in range(4)]
        for j in range(32):
            hit = chunk == (j // 4) * 8 + half * 4 + j % 4
            for t in range(4):
                value = jnp.take_along_axis(
                    table[j // 4, j % 4, 8 * t : 8 * t + 8, :], lane, axis=1, mode="promise_in_bounds"
                )
                totals[t] = jnp.where(hit, value, totals[t])
        for t in range(4):
            out[x, 8 * t : 8 * t + 8, :] = totals[t]
        return carry

    lax.fori_loop(0, NXA, column, 0)
    if second:
        h = scal[H]
        for comp in range(2):
            rows = slice(comp * HALO, (comp + 1) * HALO)
            sib[:, rows, :] = out[:, pl.ds(comp * ZS + HALO * (1 - h), HALO), :]
            off[:, rows, :] = out[:, pl.ds(comp * ZS + HALO * h, HALO), :]


def is_edge(scal):
    return (scal[LINE] == 0) | (scal[LINE] == 2 * GX * GY - 1)


def extend_coefs(scal, coefs, sib, off, slow, aniso):
    sib_at = (ZE - HALO) * (1 - scal[H])
    off_at = (ZE - HALO) * scal[H]
    inside = jnp.where(is_edge(scal), 0.0, 1.0)
    slow[:, OWN, :] = coefs[:, 0:ZS, :]
    slow[:, pl.ds(sib_at, HALO), :] = sib[:, 0:HALO, :]
    slow[:, pl.ds(off_at, HALO), :] = off[:, 0:HALO, :] * inside
    aniso[:, OWN, :] = 1.0 + 2.0 * coefs[:, ZS:, :]
    aniso[:, pl.ds(sib_at, HALO), :] = 1.0 + 2.0 * sib[:, HALO:, :]
    aniso[:, pl.ds(off_at, HALO), :] = 1.0 + 2.0 * off[:, HALO:, :]


def unpack_fields(scal, got, *outs):
    low = half_lanes((ZS, 128))
    h = scal[H]
    for kind in range(2):
        prev, now, sib, off = outs[4 * kind : 4 * kind + 4]
        for step, own in ((0, prev), (1, now)):
            f = 2 * kind + step
            for ix in range(GX):
                for i in range(4):
                    a, b = got[ix * GY, f, i], got[ix * GY + 1, f, i]
                    x = ix * BX + 2 * i
                    own[x] = jnp.where(low, a, roll_half(b))
                    own[x + 1] = jnp.where(low, roll_half(a), b)
            sib[step] = own[:, pl.ds(HALO * (1 - h), HALO), :]
            off[step] = own[:, pl.ds(HALO * h, HALO), :]


def index_kernel(scal, ids_slab, ids_owner, out):
    me = scal[IX] * GY + scal[IY]
    sub = lax.broadcasted_iota(jnp.int32, (8, 128), 0)
    lane = lax.broadcasted_iota(jnp.int32, (8, 128), 1)
    slots = []
    masks = [(jnp.broadcast_to(ids_slab[x : x + 1, :] >> 10, (8, 128)) == sub).astype(F32) for x in range(NXA)]
    for x in range(BX):
        rows = jnp.concatenate([ids_owner[s * BX + x : s * BX + x + 1, :] for s in range(GX)] * 2, axis=0)
        masks.append((((rows >> 10) == me) & (sub < GX)).astype(F32))
        slots.append((rows & 1023).astype(F32))
    bits = jnp.concatenate(masks, axis=0).astype(BF16)
    first = lax.broadcasted_iota(jnp.int32, (128, 128), 0)
    second = lax.broadcasted_iota(jnp.int32, (128, 128), 1)
    upto = (first <= second).astype(F32).astype(BF16)
    along = jnp.dot(bits, upto, preferred_element_type=F32)
    sums = jnp.dot(bits, jnp.ones((128, 128), BF16), preferred_element_type=F32)
    r0 = lax.broadcasted_iota(jnp.int32, (64, 64), 0)
    r1 = lax.broadcasted_iota(jnp.int32, (64, 64), 1)
    earlier = (((r0 & 7) == (r1 & 7)) & (r1 < r0)).astype(F32).astype(BF16)
    for group in range(GX + 1):
        rows = slice(64 * group, 64 * group + 64)
        above = jnp.dot(earlier, sums[rows].astype(BF16), preferred_element_type=F32)
        counts = along[rows] + above
        ends = sums[rows] + above
        for part in range(2):
            r = (lane + 128 * part).astype(F32)
            at_x = jnp.zeros((8, 128), jnp.int32)
            for x in range(BX):
                at_x = at_x + (ends[8 * x : 8 * x + 8] <= r).astype(jnp.int32)

            def pick(tables, at):
                value = jnp.zeros((8, 128), F32)
                for x in range(BX):
                    taken = jnp.take_along_axis(tables[x], at, axis=1, mode="promise_in_bounds")
                    value = jnp.where(at_x == x, taken, value)
                return value

            tables = [counts[8 * x : 8 * x + 8] for x in range(BX)]
            at_y = jnp.zeros((8, 128), jnp.int32)
            for step in (64, 32, 16, 8, 4, 2, 1):
                at_y = jnp.where(pick(tables, at_y + (step - 1)) <= r, at_y + step, at_y)
            at_y = jnp.minimum(at_y, 127)
            if group < GX:
                found = at_x * 128 + at_y
            else:
                found = pick(slots, at_y).astype(jnp.int32)
            out[part, 8 * group : 8 * group + 8] = jnp.where(at_x < BX, found, -1)


def stencil(field, g, along_y, along_z, own):
    rows = slice(PADX + 8 * g, PADX + 8 * g + 8)
    zs = OWN if own else slice(0, ZE)
    depth = ZS if own else ZE
    whole = field[rows].reshape(8 * ZE, 128)
    high = whole.astype(BF16)
    rest = (whole - high.astype(F32)).astype(BF16)
    both = jnp.concatenate([high, rest], axis=1)
    my = jnp.dot(both, along_y[...], preferred_element_type=F32).reshape(8, ZE, 128)[:, zs]
    mz = jnp.dot(along_z[...], both, preferred_element_type=F32)
    mz = (mz[:, :128] + mz[:, 128:]).reshape(8, depth, 128)
    center = field[rows, zs, :]
    hor = my * (1.0 / SCALE) + (2.0 * STENCIL[0]) * center
    for i in range(1, 5):
        up = field[PADX + 8 * g + i : PADX + 8 * g + 8 + i, zs, :]
        down = field[PADX + 8 * g - i : PADX + 8 * g + 8 - i, zs, :]
        hor = hor + STENCIL[i] * (up + down)
    ver = mz * (1.0 / SCALE) + STENCIL[0] * center
    return center, hor, ver


def round_kernel(kind, r, scal, *refs):
    refs = list(refs)
    take = lambda n: [refs.pop(0) for _ in range(n)]
    first, later, last = r == 0, r >= ROUNDS // 2, r == ROUNDS - 1
    if kind == "u":
        (weights,) = take(1)
    else:
        traces, depth = take(2)
    own, sib, off = take(3)
    (prev,) = take(1)
    slow, aniso, along_y, along_z, along_z_own = take(5)
    if later:
        if kind == "u":
            partner_mid, partner_end = take(2)
        else:
            (partner,) = take(1)
        if r > ROUNDS // 2:
            (total_in,) = take(1)
    out_own, out_mid = take(2)
    if not last:
        out_sib, out_off = take(2)
    if later:
        (total,) = take(1)
    elif kind == "u":
        (history,) = take(1)
    e0, e1 = take(2)

    h = scal[H]
    sib_at = (ZE - HALO) * (1 - h)
    off_at = (ZE - HALO) * h
    edge = is_edge(scal)
    zero = jnp.zeros((PADX, ZE, 128), F32)
    for e in (e0, e1):
        e[0:PADX] = zero
        e[PADX + NXA :] = zero
    inner = slice(PADX, PADX + NXA)
    now = 1 if first else 0
    e0[inner, OWN, :] = own[...]
    e0[inner, pl.ds(sib_at, HALO), :] = sib[now]
    e0[inner, pl.ds(off_at, HALO), :] = jnp.where(edge, 0.0, off[now])
    if first:
        out_mid[:, OWN, :] = prev[...]
        out_mid[:, pl.ds(sib_at, HALO), :] = sib[0]
        out_mid[:, pl.ds(off_at, HALO), :] = jnp.where(edge, 0.0, off[0])
        prev = out_mid
    top = scal[LINE] * ZS - HALO

    def source(weight, depth_rows, start):
        shape = (1, depth_rows, 128)
        z = lax.broadcasted_iota(jnp.int32, shape, 1) + start
        y = lax.broadcasted_iota(jnp.int32, shape, 2)
        return jnp.where((z == scal[SZ]) & (y == scal[SY]), weight, 0.0)

    def receivers(t, g, depth_rows, start):
        z = lax.broadcasted_iota(jnp.int32, (depth_rows, 128), 0) + start
        out = []
        for x in range(8 * g, 8 * g + 8):
            at = jnp.broadcast_to(depth[x : x + 1, :], (depth_rows, 128))
            value = jnp.broadcast_to(traces[t, x : x + 1, :], (depth_rows, 128))
            out.append(jnp.where(z == at, value, 0.0)[None])
        return jnp.concatenate(out, axis=0)

    for step in range(2):
        t = 2 * r + step
        field = e1 if step else e0
        depth_rows = ZS if step else ZE
        start = top + HALO if step else top
        for g in range(4):
            xs = slice(8 * g, 8 * g + 8)
            zs = OWN if step else slice(0, ZE)
            center, hor, ver = stencil(field, g, along_y, along_z_own if step else along_z, step)
            before = e0[PADX + 8 * g : PADX + 8 * g + 8, OWN, :] if step else prev[xs]
            lap = aniso[xs, zs, :] * hor + ver
            following = 2.0 * center - before + slow[xs, zs, :] * lap
            if kind == "a":
                following = following + receivers(STEPS - 1 - t, g, depth_rows, start)
            if step:
                out_own[xs] = following
            else:
                e1[PADX + 8 * g : PADX + 8 * g + 8] = following
            if step == 0:
                hor, ver = hor[:, OWN], ver[:, OWN]
            if kind == "u" and not later:
                history[2 * step, xs] = hor
                history[2 * step + 1, xs] = ver
            if later:
                if kind == "u":
                    other = partner_mid[xs, OWN, :] if step else partner_end[xs]
                    hor_part, ver_part = hor, ver
                else:
                    other = following if step else following[:, OWN]
                    hor_part = partner[2 * (1 - step), xs]
                    ver_part = partner[2 * (1 - step) + 1, xs]
                sum_h, sum_v = other * hor_part, other * ver_part
                if step:
                    sum_h, sum_v = total[0, xs] + sum_h, total[1, xs] + sum_v
                elif r > ROUNDS // 2:
                    sum_h, sum_v = total_in[0, xs] + sum_h, total_in[1, xs] + sum_v
                total[0, xs] = sum_h
                total[1, xs] = sum_v
        if kind == "u":
            if step:
                row = out_own[pl.ds(scal[SX], 1)]
                out_own[pl.ds(scal[SX], 1)] = row + source(weights[t], ZS, start)
            else:
                row = e1[pl.ds(PADX + scal[SX], 1)]
                e1[pl.ds(PADX + scal[SX], 1)] = row + source(weights[t], ZE, start)
    out_mid[...] = e1[inner]
    if not last:
        out_sib[0] = out_own[:, pl.ds(HALO * (1 - h), HALO), :]
        out_off[0] = out_own[:, pl.ds(HALO * h, HALO), :]


def pack_out(scal, u, a, index, total_u, total_a, coefs, *refs):
    outs, grads = refs[:8], refs[8]
    for x in range(NXA):
        gh = (total_u[0, x] + total_a[0, x]) * UNSCALE
        gv = (total_u[1, x] + total_a[1, x]) * UNSCALE
        slow, aniso = coefs[x, 0:ZS, :], coefs[x, ZS:, :]
        grads[x, 0:ZS, :] = (1.0 + 2.0 * aniso) * gh + gv
        grads[x, ZS:, :] = (2.0 * slow) * gh
    low = half_lanes((ZS, 128))
    for n, out in enumerate(outs):
        block = block_of(scal, FAR_FIRST[n])
        for f, field in enumerate((u, a)):
            for i in range(4):
                x = (block >> 1) * BX + 2 * i
                x0 = field[pl.ds(x, 1)].reshape(ZS, 128)
                x1 = field[pl.ds(x + 1, 1)].reshape(ZS, 128)
                piece = jnp.where(low, x0, roll_half(x1))
                upper = jnp.where(low, roll_half(x0), x1)
                at = 256 + (f * 4 + i) * ZS
                out[at : at + ZS, :] = jnp.where((block & 1) == 0, piece, upper)

        def stripe(ix, carry, out=out, block=block):
            for part in range(2):
                row = index[part, pl.ds(ix * 8 + block, 1), :]
                lane = jnp.broadcast_to(row & 127, (8, 128))
                which = jnp.broadcast_to(row >> 7, (8, 128))
                totals = [jnp.zeros((8, 128), F32) for t in range(4)]
                for x in range(BX):
                    hit = which == x
                    for t in range(4):
                        value = jnp.take_along_axis(
                            grads[ix * BX + x, 8 * t : 8 * t + 8, :], lane, axis=1, mode="promise_in_bounds"
                        )
                        totals[t] = jnp.where(hit, value, totals[t])
                for t in range(4):
                    at = pl.multiple_of((ix * 2 + part) * 32 + 8 * t, 8)
                    out[pl.ds(at, 8), :] = totals[t]
            return carry

        lax.fori_loop(0, GX, stripe, 0)


def name_slots(index, picks):
    named = jnp.concatenate([index[n % 2, 32 + n // 2 : 33 + n // 2, :] for n in range(8)], axis=1)
    for block in range(4):
        slot = lax.broadcasted_iota(jnp.int32, (256, 1024), 0) + block * 256
        pick = slot == jnp.broadcast_to(named, (256, 1024))
        picks[block * 256 : (block + 1) * 256, :] = pick.astype(F32).astype(BF16)


def finish(scal, picks, *refs):
    gots, (u_out, a_out, model, turned, columns) = refs[:8], refs[8:]
    for f, out in enumerate((u_out, a_out)):
        for i in range(4):
            for n, e in enumerate(FAR_FIRST):
                at = 256 + (f * 4 + i) * ZS
                turned[pl.ds(slab_of(scal, e), ZS), :] = gots[n][at : at + ZS, :]
            out[2 * i : 2 * i + 2] = turned[...].T.reshape(2, BY, 128)
    for n, e in enumerate(FAR_FIRST):
        for m in range(8):
            for comp in range(2):
                rows = pl.ds(pl.multiple_of(comp * 128 + slab_of(scal, e), ZS), ZS)
                at = m * 32 + comp * ZS
                columns[rows, m * 128 : (m + 1) * 128] = gots[n][at : at + ZS, :]
    values = columns[...]
    high = values.astype(BF16)
    rest = (values - high.astype(F32)).astype(BF16)
    for block in range(4):
        pick = picks[block * 256 : (block + 1) * 256, :]
        dims = (((1,), (1,)), ((), ()))
        sums = lax.dot_general(pick, high, dims, preferred_element_type=F32)
        sums = sums + lax.dot_general(pick, rest, dims, preferred_element_type=F32)
        for comp in range(2):
            model[pl.ds(block * 512 + comp, 256, stride=2), :] = sums[:, comp * 128 : (comp + 1) * 128]


def by_half(h, mine, other):
    first = jnp.where(h == 0, mine, other)
    second = jnp.where(h == 0, other, mine)
    both = jnp.stack([first, second], axis=1)
    return both.reshape((GX * GY,) + mine.shape[1:])


def exchange(x):
    return lax.all_to_all(x, ("gx", "gy"), split_axis=0, concat_axis=0, tiled=True)


def slab_body(
    forward_prev,
    forward_now,
    adjoint_prev,
    adjoint_now,
    model_table,
    tile_owner,
    tile_slot,
    source_index,
    wavelet,
    receiver_depth,
    traces,
):
    h = lax.axis_index("gz")
    ix, iy = lax.axis_index("gx"), lax.axis_index("gy")
    chip = jnp.where(iy == 0, ix, 2 * GX - 1 - ix)
    line = 2 * chip + h
    scal = jnp.stack(
        [h, ix, iy, lax.axis_index("shots"), line, source_index[0], source_index[1], source_index[2]]
    ).astype(jnp.int32)

    trace_half = lax.dynamic_slice_in_dim(traces, h * 8, 8, axis=0)
    (small,) = call(pack_small, [((5, BX, 128), F32)], vmem(4), moved=MIB // 16, flops=1 << 16)(
        tile_owner.reshape(1, BX * BY), tile_slot.reshape(1, BX * BY), receiver_depth, trace_half
    )
    keep, give = call(
        pack_table, [((GX, 128, 128), F32)] * 2, [SMEM] + vmem(1), moved=2 * MIB, flops=1 << 20
    )(scal, model_table.reshape(2048, 128))
    (sent,) = call(assemble, [((GX * GY, 168, 128), F32)], [SMEM] + vmem(3), moved=2 * MIB, flops=1 << 20)(
        scal, keep, to_sibling(give), small
    )
    arrived = exchange(sent)
    table_mine = arrived[:, :128].reshape(8, 4, 32, 128)
    small_mine = arrived[:, 128:].reshape(8, 5, BX, 128)
    table_other = lax.ppermute(table_mine, "shots", SWAP)
    small_other = to_sibling(small_mine)

    keep, give = call(
        pack_fields, [((4, 4, 4, ZS, 128), F32)] * 2, [SMEM] + vmem(4), moved=2 * MIB, flops=1 << 20
    )(scal, forward_prev, forward_now, adjoint_prev, adjoint_now)
    fields = exchange(by_half(h, keep, to_sibling(give)))

    ids_slab, ids_owner, depth, traces = call(
        unpack_small,
        [((NXA, 128), jnp.int32)] * 3 + [((STEPS, NXA, 128), F32)],
        [SMEM] + vmem(2),
        moved=MIB // 2,
        flops=1 << 20,
    )(scal, small_mine, small_other)
    coef_shape = ((NXA, 2 * ZS, 128), F32)
    half_shape = ((NXA, 2 * HALO, 128), F32)
    (coefs,) = call(
        functools.partial(gather_half, False), [coef_shape], [SMEM] + vmem(2), moved=MIB, flops=1 << 24
    )(scal, table_mine, ids_slab)
    coefs, coefs_sib, coefs_off = call(
        functools.partial(gather_half, True),
        [coef_shape, half_shape, half_shape],
        [SMEM] + vmem(3),
        moved=2 * MIB,
        flops=1 << 24,
    )(scal, table_other, ids_slab, coefs)
    ext_shape = ((NXA, ZE, 128), F32)
    own_shape = ((NXA, ZS, 128), F32)
    slow, aniso = call(extend_coefs, [ext_shape] * 2, [SMEM] + vmem(3), moved=2 * MIB, flops=1 << 20)(
        scal, coefs, to_sibling(coefs_sib), to_off_chip(coefs_off)
    )
    (index,) = call(
        index_kernel,
        [((2, 40, 128), jnp.int32)],
        [SMEM] + vmem(2),
        moved=MIB // 4,
        flops=1 << 24,
    )(scal, ids_slab, ids_owner)

    fields, index = lax.optimization_barrier((fields, index))
    first_halo = ((2, NXA, HALO, 128), F32)
    unpacked = call(
        unpack_fields,
        [own_shape, own_shape, first_halo, first_halo] * 2,
        [SMEM] + vmem(1),
        moved=4 * MIB,
        flops=1 << 20,
    )(scal, fields)
    bands = matrices()
    halo = ((1, NXA, HALO, 128), F32)
    state = {}
    for n, kind in enumerate("ua"):
        prev, now, sib, off = unpacked[4 * n : 4 * n + 4]
        state[kind] = [now, to_sibling(sib), to_off_chip(off), prev]
    history, mids, ends, totals = {}, {}, {}, {}
    for r in range(ROUNDS):
        for kind in "ua":
            later, last = r >= ROUNDS // 2, r == ROUNDS - 1
            drive = [wavelet] if kind == "u" else [traces, depth]
            specs = [SMEM] + ([SMEM] if kind == "u" else vmem(2))
            args = state[kind] + [slow, aniso] + bands
            if later:
                partner = ROUNDS - 1 - r
                args += [mids[partner], ends[partner]] if kind == "u" else [history[partner]]
                if r > ROUNDS // 2:
                    args += [totals[kind]]
            specs = specs + vmem(len(args))
            outs = [own_shape, ext_shape] + ([] if last else [halo, halo])
            if later:
                outs.append(((2, NXA, ZS, 128), F32))
            elif kind == "u":
                outs.append(((4, NXA, ZS, 128), F32))
            res = call(
                functools.partial(round_kernel, kind, r),
                outs,
                specs,
                [pltpu.VMEM((NXA + 2 * PADX, ZE, 128), F32)] * 2,
                moved=4 * MIB,
                flops=1 << 24,
            )(scal, *drive, *args)
            own, mid = res[0], res[1]
            if later:
                totals[kind] = res[-1]
            elif kind == "u":
                history[r] = res[-1]
            if kind == "a":
                mids[r], ends[r] = mid, own
            if last:
                state[kind] = [own]
            else:
                state[kind] = [own, to_sibling(res[2]), to_off_chip(res[3]), mid]

    packed = call(
        pack_out,
        [((384, 128), F32)] * 8,
        [SMEM] + vmem(6),
        [pltpu.VMEM((NXA, 2 * ZS, 128), F32)],
        moved=4 * MIB,
        flops=1 << 22,
    )(scal, state["u"][0], state["a"][0], index, totals["u"], totals["a"], coefs)
    index, _ = lax.optimization_barrier((index, packed[7]))
    (picks,) = call(name_slots, [((1024, 1024), BF16)], vmem(1), moved=4 * MIB, flops=1 << 22)(index)
    arrived = [to_blocks(x, e) for x, e in zip(packed, FAR_FIRST)]
    u, a, model = call(
        finish,
        [((BX, BY, BZ), F32)] * 2 + [((2048, 128), F32)],
        [SMEM] + vmem(9),
        [pltpu.VMEM((128, 128), F32), pltpu.VMEM((256, 1024), F32)],
        moved=4 * MIB,
        flops=1 << 28,
    )(scal, picks, *arrived)
    return (u, a, model.reshape(1, 1024, 2, 128))


def solution(mesh):
    in_specs = (
        P(("shots", "gx"), "gy", "gz"),
        P(("shots", "gx"), "gy", "gz"),
        P(("shots", "gx"), "gy", "gz"),
        P(("shots", "gx"), "gy", "gz"),
        P("gz", ("gx", "gy"), None, None),
        P(("shots", "gz"), "gx", "gy", None, None),
        P(("shots", "gz"), "gx", "gy", None),
        P("shots"),
        P("shots"),
        P(("shots", "gx"), "gy"),
        P(None, ("shots", "gx"), "gy"),
    )
    out_specs = (
        P(("shots", "gx"), "gy", "gz"),
        P(("shots", "gx"), "gy", "gz"),
        P("gz", ("shots", "gx", "gy"), None, None),
    )
    body = slab_body if slabs_fit(mesh) else block_body
    return jax.shard_map(body, mesh=mesh, in_specs=in_specs, out_specs=out_specs, check_vma=False)
```

```python
import functools

import jax
import jax.numpy as jnp
import numpy as np
from jax import lax
from jax.experimental import pallas as pl
from jax.experimental.pallas import tpu as pltpu
from jax.sharding import PartitionSpec as P

STENCIL = (-205.0 / 72.0, 8.0 / 5.0, -1.0 / 5.0, 8.0 / 315.0, -1.0 / 560.0)


def with_halo(block, sides, width):
    for axis, dim in sides:
        count = lax.axis_size(axis)
        forward = [(i, i + 1) for i in range(count - 1)]
        backward = [(target, source) for source, target in forward]
        low = lax.ppermute(
            lax.slice_in_dim(block, block.shape[dim] - width, None, axis=dim), axis, forward
        )
        high = lax.ppermute(lax.slice_in_dim(block, 0, width, axis=dim), axis, backward)
        block = jnp.concatenate([low, block, high], axis=dim)
    return block


def derivatives(padded, shape):
    size_x, size_y, size_z = shape

    def window(off_x, off_y, off_z):
        return padded[
            4 + off_x : 4 + off_x + size_x,
            4 + off_y : 4 + off_y + size_y,
            4 + off_z : 4 + off_z + size_z,
        ]

    center = window(0, 0, 0)
    along_x = STENCIL[0] * center
    along_y = STENCIL[0] * center
    along_z = STENCIL[0] * center
    for offset in range(1, 5):
        along_x = along_x + STENCIL[offset] * (window(offset, 0, 0) + window(-offset, 0, 0))
        along_y = along_y + STENCIL[offset] * (window(0, offset, 0) + window(0, -offset, 0))
        along_z = along_z + STENCIL[offset] * (window(0, 0, offset) + window(0, 0, -offset))
    return (along_x + along_y, along_z)


def propagate(previous, current, slow_coef, aniso_coef, padded):
    horizontal, vertical = derivatives(padded, current.shape)
    laplacian = (1.0 + 2.0 * aniso_coef) * horizontal + vertical
    following = 2.0 * current - previous + slow_coef * laplacian
    return (following, laplacian, horizontal)


def block_body(
    forward_prev,
    forward_now,
    adjoint_prev,
    adjoint_now,
    model_table,
    tile_owner,
    tile_slot,
    source_index,
    wavelet,
    receiver_depth,
    traces,
):
    block_x, block_y, block_z = forward_now.shape
    columns = block_x * block_y
    owners_count = lax.axis_size(("gx", "gy"))
    capacity = max(2, 2 * columns // owners_count)
    column_owner = tile_owner.reshape(columns)
    column_slot = tile_slot.reshape(columns)
    local_table = model_table[0]
    held_count = local_table.shape[0]
    one_hot = (column_owner[:, None] == jnp.arange(owners_count, dtype=jnp.int32)[None, :]).astype(
        jnp.float32
    )
    earlier = (
        jnp.arange(columns, dtype=jnp.int32)[:, None]
        > jnp.arange(columns, dtype=jnp.int32)[None, :]
    ).astype(jnp.float32)
    counted_before = jnp.dot(earlier, one_hot, precision=lax.Precision.HIGHEST)
    slot_rank = jnp.sum(counted_before * one_hot, axis=1).astype(jnp.int32)
    requests = (
        jnp.full((owners_count, capacity), -1, jnp.int32)
        .at[column_owner, slot_rank]
        .set(column_slot)
    )
    received = lax.all_to_all(requests, ("gx", "gy"), split_axis=0, concat_axis=0, tiled=True)
    clipped = jnp.clip(received, 0, held_count - 1)
    fetched = lax.all_to_all(
        local_table[clipped], ("gx", "gy"), split_axis=0, concat_axis=0, tiled=True
    )
    cell_params = (
        fetched[column_owner, slot_rank].reshape(block_x, block_y, 2, block_z).transpose(2, 0, 1, 3)
    )
    slow_coef = cell_params[0]
    aniso_coef = cell_params[1]
    grid_x = lax.axis_index("gx") * block_x + jnp.arange(block_x, dtype=jnp.int32)[:, None, None]
    grid_y = lax.axis_index("gy") * block_y + jnp.arange(block_y, dtype=jnp.int32)[None, :, None]
    grid_z = lax.axis_index("gz") * block_z + jnp.arange(block_z, dtype=jnp.int32)[None, None, :]
    source_mask = (
        (grid_x == source_index[0]) & (grid_y == source_index[1]) & (grid_z == source_index[2])
    ).astype(jnp.float32)
    receiver_mask = (grid_z == receiver_depth[:, :, None]).astype(jnp.float32)

    def forward(carried, weight):
        previous, current = carried
        padded = with_halo(current, (("gx", 0), ("gy", 1), ("gz", 2)), 4)
        following, laplacian, horizontal = propagate(
            previous, current, slow_coef, aniso_coef, padded
        )
        following = following + weight * source_mask
        return ((current, following), (laplacian, horizontal))

    (_, forward_final), (laplacians, horizontals) = lax.scan(
        forward, (forward_prev, forward_now), wavelet
    )

    def backward(carried, inputs):
        previous, current, grad_slow, grad_aniso = carried
        trace_row, laplacian, horizontal = inputs
        padded = with_halo(current, (("gx", 0), ("gy", 1), ("gz", 2)), 4)
        following, _, _ = propagate(previous, current, slow_coef, aniso_coef, padded)
        following = following + trace_row[:, :, None] * receiver_mask
        grad_slow = grad_slow + following * laplacian
        grad_aniso = grad_aniso + following * (2.0 * slow_coef * horizontal)
        return ((current, following, grad_slow, grad_aniso), None)

    zero_field = jnp.zeros((block_x, block_y, block_z), jnp.float32)
    (_, adjoint_final, grad_slow, grad_aniso), _ = lax.scan(
        backward,
        (adjoint_prev, adjoint_now, zero_field, zero_field),
        (traces[::-1], laplacians[::-1], horizontals[::-1]),
    )
    grad_cells = (
        jnp.stack([grad_slow, grad_aniso]).transpose(1, 2, 0, 3).reshape(columns, 2, block_z)
    )
    outgoing = (
        jnp.zeros((owners_count, capacity, 2, block_z), jnp.float32)
        .at[column_owner, slot_rank]
        .set(grad_cells)
    )
    returned = lax.all_to_all(outgoing, ("gx", "gy"), split_axis=0, concat_axis=0, tiled=True)
    target = jnp.where(received < 0, held_count, received).reshape(owners_count * capacity)
    model_gradient = (
        jnp.zeros((held_count, 2, block_z), jnp.float32)
        .at[target]
        .add(returned.reshape(owners_count * capacity, 2, block_z), mode="drop")
    )
    return (forward_final, adjoint_final, model_gradient[None])


BX, BY, BZ = 8, 64, 128
GX, GY = 4, 2
NXA, NYA = BX * GX, BY * GY
ZS = 16
ZE = 32
HALO = 8
OWN = slice(HALO, HALO + ZS)
SCALE = 5040.0
UNSCALE = 1.0 / SCALE
PADX = 4
EXT_SHAPE = (NXA + 2 * PADX, ZE, 128)
INNER = slice(PADX, PADX + NXA)
STEPS = 16
ROUNDS = STEPS // 2
MIB = 1 << 20
F32 = jnp.float32
BF16 = jnp.bfloat16
H, IX, IY, SHOT, LINE, SX, SY, SZ = range(8)


def slabs_fit(mesh):
    names = ("shots", "gx", "gy", "gz")
    return tuple(mesh.shape[n] for n in names) == (2, GX, GY, 2)


def line_device(place):
    chip, core = divmod(place, 2)
    ix, iy = (chip, 0) if chip < GX else (2 * GX - 1 - chip, 1)
    return (ix * GY + iy) * 2 + core


def off_chip_pairs():
    count = 2 * GX * GY
    pairs = []
    for low in range(1, count, 2):
        a, b = line_device(low), line_device((low + 1) % count)
        pairs += [(a, b), (b, a)]
    return pairs


OFF_PAIRS = off_chip_pairs()
SWAP = [(0, 1), (1, 0)]


def to_sibling(x):
    return lax.ppermute(x, "gz", SWAP)


def to_off_chip(x):
    return lax.ppermute(x, ("gx", "gy", "gz"), OFF_PAIRS)


def spread(e):
    return [(2 * s + c, 2 * (s ^ e ^ c) + (s & 1)) for s in range(GX * GY) for c in range(2)]


def to_blocks(x, e):
    return lax.ppermute(x, ("gx", "gy", "gz"), spread(e))


FAR_FIRST = (6, 7, 4, 5, 2, 3, 0, 1)


def slab_of(scal, e):
    ix = scal[IX] ^ (e >> 1)
    core = scal[IY] ^ (e & 1) ^ scal[H]
    chip = jnp.where(scal[H] == 0, ix, GX - 1 - ix)
    return pl.multiple_of(chip * 2 * ZS + core * ZS, ZS)


def block_of(scal, e):
    return (scal[IX] * GY + scal[IY]) ^ e ^ scal[H]


def band(size):
    out = np.zeros((size, size), np.float32)
    for offset in range(1, 5):
        value = round(STENCIL[offset] * SCALE)
        for i in range(size - offset):
            out[i, i + offset] = value
            out[i + offset, i] = value
    return out


def matrices():
    along_y = band(NYA)
    along_y = np.concatenate([along_y, along_y], 0)
    along_z = band(ZE)
    full = np.kron(np.eye(8, dtype=np.float32), along_z)
    own = np.kron(np.eye(8, dtype=np.float32), along_z[OWN])
    full, own = [np.concatenate([m, m], 1) for m in (full, own)]
    return [jnp.asarray(m, BF16) for m in (along_y, full, own)]


def vmem(count):
    return [pl.BlockSpec(memory_space=pltpu.VMEM)] * count


SMEM = pl.BlockSpec(memory_space=pltpu.SMEM)


def call(kernel, outs, specs, scratch=(), limit=24, flops=0, moved=0, aliases=None):
    return pl.pallas_call(
        kernel,
        out_shape=[jax.ShapeDtypeStruct(s, d) for s, d in outs],
        in_specs=specs,
        out_specs=vmem(len(outs)),
        scratch_shapes=list(scratch),
        input_output_aliases=aliases or {},
        compiler_params=pltpu.CompilerParams(vmem_limit_bytes=limit * MIB),
        cost_estimate=pl.CostEstimate(flops=flops, bytes_accessed=moved, transcendentals=0),
    )


def half_lanes(shape):
    return lax.broadcasted_iota(jnp.int32, shape, len(shape) - 1) < BY


def roll_half(x):
    return pltpu.roll(x, BY, x.ndim - 1)


def place(scal, chunk):
    chip, core = divmod(chunk, 2)
    mine = core == scal[H]
    return mine, jnp.where(scal[H] == 0, chip, GX - 1 - chip)


def pack_small(owner, slot, depth, traces, out):
    for tt in range(4):
        out[tt] = jnp.concatenate([traces[2 * tt], traces[2 * tt + 1]], axis=1)
    low = half_lanes((1, 128))
    ids = owner[...] * 1024 + slot[...]
    rows = []
    for x in range(BX):
        pair = ids[:, (x // 2) * 128 : (x // 2 + 1) * 128].astype(F32)
        rows.append(roll_half(pair) if x % 2 else pair)
    rows = jnp.concatenate(rows, axis=0)
    depths = depth[...].astype(F32)
    depths = jnp.concatenate([depths, depths], axis=1)
    out[4] = jnp.where(half_lanes((8, 128)), rows, depths)


def pack_table(scal, table, keep, give):
    first = scal[SHOT] * 1024
    for q in range(4):
        for comp in range(2):
            turned = table[pl.ds(first + q * 256 + comp, 128, stride=2), :].T
            at = q * 32 + comp * ZS
            for chunk in range(8):
                mine, g = place(scal, chunk)
                piece = turned[chunk * ZS : (chunk + 1) * ZS][None]

                @pl.when(mine)
                def _():
                    keep[pl.ds(g, 1), at : at + ZS, :] = piece

                @pl.when(jnp.logical_not(mine))
                def _():
                    give[pl.ds(g, 1), at : at + ZS, :] = piece


def assemble(scal, keep, got, small, out):
    h = scal[H]
    for ix in range(GX):
        out[pl.ds(ix * GY + h, 1), 0:128, :] = keep[ix][None]
        out[pl.ds(ix * GY + 1 - h, 1), 0:128, :] = got[ix][None]
    for n in range(GX * GY):
        out[n, 128:, :] = small[...].reshape(40, 128)


def pack_fields(scal, *refs):
    fields, (keep, give) = refs[:4], refs[4:]
    for f in range(4):
        for i in range(4):
            pair = fields[f][2 * i : 2 * i + 2].reshape(128, 128)
            turned = pair.T
            for chunk in range(8):
                mine, g = place(scal, chunk)
                piece = turned[chunk * ZS : (chunk + 1) * ZS][None]

                @pl.when(mine)
                def _():
                    keep[pl.ds(g, 1), f, i] = piece

                @pl.when(jnp.logical_not(mine))
                def _():
                    give[pl.ds(g, 1), f, i] = piece


def unpack_small(scal, wavelet, mine, other, ids_slab, ids_owner, depth, traces, pulse, pulse_depth, place):
    low = half_lanes((8, 128))
    h = scal[H]
    x_at = lax.broadcasted_iota(jnp.int32, (NXA, 128), 0)
    y_at = lax.broadcasted_iota(jnp.int32, (NXA, 128), 1)
    at_source = (x_at == scal[SX]) & (y_at == scal[SY])
    for t in range(STEPS):
        pulse[t] = jnp.where(at_source, wavelet[t], 0.0)
    pulse_depth[...] = jnp.full((NXA, 128), scal[SZ], jnp.int32)
    place[0] = jnp.full((8, 128), h, jnp.int32)
    place[1] = jnp.full((8, 128), jnp.where(is_edge(scal), 1, 0), jnp.int32)
    place[2] = jnp.full((8, 128), scal[LINE] * ZS - HALO, jnp.int32)
    for ix in range(GX):
        rows = slice(ix * BX, (ix + 1) * BX)
        for ref, is_mine in ((mine, True), (other, False)):
            a, b = ref[ix * GY], ref[ix * GY + 1]
            core = h if is_mine else 1 - h
            for tt in range(4):
                even = jnp.where(low, a[tt], roll_half(b[tt]))
                odd = jnp.where(low, roll_half(a[tt]), b[tt])
                traces[pl.ds(core * 8 + 2 * tt, 1), rows, :] = even[None]
                traces[pl.ds(core * 8 + 2 * tt + 1, 1), rows, :] = odd[None]
            ids = jnp.where(low, a[4], roll_half(b[4])).astype(jnp.int32)
            if is_mine:
                ids_owner[rows, :] = ids
                depth[rows, :] = jnp.where(low, roll_half(a[4]), b[4]).astype(jnp.int32)

            @pl.when(core == scal[IY])
            def _():
                ids_slab[rows, :] = ids


def gather_half(second, scal, table, ids, *refs):
    if second:
        before, out, sib, off = refs
    else:
        (out,) = refs
    half = 1 - scal[SHOT] if second else scal[SHOT]

    def column(x, carry):
        row = ids[pl.ds(x, 1), :]
        lane = jnp.broadcast_to(row & 127, (8, 128))
        chunk = jnp.broadcast_to(row >> 7, (8, 128))
        if second:
            totals = [before[x, 8 * t : 8 * t + 8, :] for t in range(4)]
        else:
            totals = [jnp.zeros((8, 128), F32) for t in range(4)]
        for j in range(32):
            hit = chunk == (j // 4) * 8 + half * 4 + j % 4
            for t in range(4):
                value = jnp.take_along_axis(
                    table[j // 4, j % 4, 8 * t : 8 * t + 8, :], lane, axis=1, mode="promise_in_bounds"
                )
                totals[t] = jnp.where(hit, value, totals[t])
        for t in range(4):
            out[x, 8 * t : 8 * t + 8, :] = totals[t]
        return carry

    lax.fori_loop(0, NXA, column, 0)
    if second:
        h = scal[H]
        for comp in range(2):
            rows = slice(comp * HALO, (comp + 1) * HALO)
            sib[:, rows, :] = out[:, pl.ds(comp * ZS + HALO * (1 - h), HALO), :]
            off[:, rows, :] = out[:, pl.ds(comp * ZS + HALO * h, HALO), :]


def is_edge(scal):
    return (scal[LINE] == 0) | (scal[LINE] == 2 * GX * GY - 1)


def extend_coefs(scal, coefs, sib, off, slow, aniso):
    sib_at = (ZE - HALO) * (1 - scal[H])
    off_at = (ZE - HALO) * scal[H]
    inside = jnp.where(is_edge(scal), 0.0, 1.0)
    slow[:, OWN, :] = coefs[:, 0:ZS, :] * UNSCALE
    slow[:, pl.ds(sib_at, HALO), :] = sib[:, 0:HALO, :] * UNSCALE
    slow[:, pl.ds(off_at, HALO), :] = off[:, 0:HALO, :] * (inside * UNSCALE)
    aniso[:, OWN, :] = 1.0 + 2.0 * coefs[:, ZS:, :]
    aniso[:, pl.ds(sib_at, HALO), :] = 1.0 + 2.0 * sib[:, HALO:, :]
    aniso[:, pl.ds(off_at, HALO), :] = 1.0 + 2.0 * off[:, HALO:, :]


def unpack_fields(scal, got, *outs):
    low = half_lanes((ZS, 128))
    h = scal[H]
    for kind in range(2):
        prev, now, sib, off = outs[4 * kind : 4 * kind + 4]
        for step, own in ((0, prev), (1, now)):
            f = 2 * kind + step
            for ix in range(GX):
                for i in range(4):
                    a, b = got[ix * GY, f, i], got[ix * GY + 1, f, i]
                    x = ix * BX + 2 * i
                    own[x] = jnp.where(low, a, roll_half(b))
                    own[x + 1] = jnp.where(low, roll_half(a), b)
            sib[step] = own[:, pl.ds(HALO * (1 - h), HALO), :]
            off[step] = own[:, pl.ds(HALO * h, HALO), :]


def index_kernel(scal, ids_slab, ids_owner, out):
    me = scal[IX] * GY + scal[IY]
    sub = lax.broadcasted_iota(jnp.int32, (8, 128), 0)
    lane = lax.broadcasted_iota(jnp.int32, (8, 128), 1)
    slots = []
    masks = [(jnp.broadcast_to(ids_slab[x : x + 1, :] >> 10, (8, 128)) == sub).astype(F32) for x in range(NXA)]
    for x in range(BX):
        rows = jnp.concatenate([ids_owner[s * BX + x : s * BX + x + 1, :] for s in range(GX)] * 2, axis=0)
        masks.append((((rows >> 10) == me) & (sub < GX)).astype(F32))
        slots.append((rows & 1023).astype(F32))
    bits = jnp.concatenate(masks, axis=0).astype(BF16)
    first = lax.broadcasted_iota(jnp.int32, (128, 128), 0)
    second = lax.broadcasted_iota(jnp.int32, (128, 128), 1)
    upto = (first <= second).astype(F32).astype(BF16)
    along = jnp.dot(bits, upto, preferred_element_type=F32)
    sums = jnp.dot(bits, jnp.ones((128, 128), BF16), preferred_element_type=F32)
    r0 = lax.broadcasted_iota(jnp.int32, (64, 64), 0)
    r1 = lax.broadcasted_iota(jnp.int32, (64, 64), 1)
    earlier = (((r0 & 7) == (r1 & 7)) & (r1 < r0)).astype(F32).astype(BF16)
    for group in range(GX + 1):
        rows = slice(64 * group, 64 * group + 64)
        above = jnp.dot(earlier, sums[rows].astype(BF16), preferred_element_type=F32)
        counts = along[rows] + above
        ends = sums[rows] + above
        for part in range(2):
            r = (lane + 128 * part).astype(F32)
            at_x = jnp.zeros((8, 128), jnp.int32)
            for x in range(BX):
                at_x = at_x + (ends[8 * x : 8 * x + 8] <= r).astype(jnp.int32)

            def pick(tables, at):
                value = jnp.zeros((8, 128), F32)
                for x in range(BX):
                    taken = jnp.take_along_axis(tables[x], at, axis=1, mode="promise_in_bounds")
                    value = jnp.where(at_x == x, taken, value)
                return value

            tables = [counts[8 * x : 8 * x + 8] for x in range(BX)]
            at_y = jnp.zeros((8, 128), jnp.int32)
            for step in (64, 32, 16, 8, 4, 2, 1):
                at_y = jnp.where(pick(tables, at_y + (step - 1)) <= r, at_y + step, at_y)
            at_y = jnp.minimum(at_y, 127)
            if group < GX:
                found = at_x * 128 + at_y
            else:
                found = pick(slots, at_y).astype(jnp.int32)
            out[part, 8 * group : 8 * group + 8] = jnp.where(at_x < BX, found, -1)


def bands_of(field, g, along_y, along_z, own):
    first = PADX + 8 * g
    depth = ZS if own else ZE
    whole = field[first : first + 8].reshape(8 * ZE, 128)
    high = whole.astype(BF16)
    rest = (whole - high.astype(F32)).astype(BF16)
    my = jnp.dot(jnp.concatenate([high, rest], axis=1), along_y[...], preferred_element_type=F32)
    mz = jnp.dot(along_z[...], jnp.concatenate([high, rest], axis=0), preferred_element_type=F32)
    return my.reshape(8, ZE, 128), mz.reshape(8, depth, 128)


def round_scratch():
    return [pltpu.VMEM(EXT_SHAPE, F32)]


def round_kernel(kind, r, *refs):
    refs = list(refs)
    take = lambda n: [refs.pop(0) for _ in range(n)]
    first, later, last = r == 0, r >= ROUNDS // 2, r == ROUNDS - 1
    place, drive, depth, own, sib, off, prev, slow, aniso, along_y, along_z, along_z_own = take(12)
    if later:
        if kind == "u":
            partner_mid, partner_end = take(2)
        else:
            (partner,) = take(1)
        if r > ROUNDS // 2:
            (total_in,) = take(1)
    out_own, out_mid = take(2)
    if not last:
        out_sib, out_off = take(2)
    if later:
        (total,) = take(1)
    elif kind == "u":
        (history,) = take(1)
    (e0,) = take(1)
    e1 = out_mid

    core_0 = place[0] == 0
    inside = place[1] == 0
    zero = jnp.zeros((PADX, ZE, 128), F32)
    for e in (e0, e1):
        e[0:PADX] = zero
        e[PADX + NXA :] = zero

    def extend(e, own, n):
        for x in range(NXA):
            near, far = sib[n, x], jnp.where(inside, off[n, x], 0.0)
            e[PADX + x, 0:HALO] = jnp.where(core_0, far, near)
            e[PADX + x, OWN] = own[x]
            e[PADX + x, HALO + ZS :] = jnp.where(core_0, near, far)

    if first:
        extend(e0, own, 1)
        extend(e1, prev, 0)
        prev = e1
    else:
        extend(e0, own, 0)
    base = jnp.concatenate([place[2]] * (ZE // 8), axis=0) + lax.broadcasted_iota(jnp.int32, (ZE, 128), 0)

    def bands(step, g):
        if step:
            return bands_of(e1, g, along_y, along_z_own, True)
        return bands_of(e0, g, along_y, along_z, False)

    items = [(step, g) for step in range(2) for g in range(4)]
    ahead = bands(*items[0])
    for k, (step, g) in enumerate(items):
        my, mz = ahead
        if k + 1 < len(items):
            ahead = bands(*items[k + 1])
        t = 2 * r + step if kind == "u" else STEPS - 1 - (2 * r + step)
        field = e1 if step else e0
        zs = OWN if step else slice(0, ZE)
        count = ZS if step else ZE
        z = base[zs]
        for n in range(8):
            x = 8 * g + n
            at = PADX + x
            center = field[at, zs, :]
            hor = my[n, zs] + (2.0 * SCALE * STENCIL[0]) * center
            for i in range(1, 5):
                hor = hor + (SCALE * STENCIL[i]) * (field[at + i, zs, :] + field[at - i, zs, :])
            ver = mz[n] + (SCALE * STENCIL[0]) * center
            before = e0[at, OWN, :] if step else prev[at]
            lap = aniso[x, zs, :] * hor + ver
            following = 2.0 * center - before + slow[x, zs, :] * lap
            at_z = jnp.broadcast_to(depth[x : x + 1, :], (count, 128))
            value = jnp.broadcast_to(drive[t, x : x + 1, :], (count, 128))
            following = following + jnp.where(z == at_z, value, 0.0)
            if step:
                out_own[x] = following
                if not last:
                    low, high = following[:HALO], following[HALO:]
                    out_sib[0, x] = jnp.where(core_0, high, low)
                    out_off[0, x] = jnp.where(core_0, low, high)
            else:
                e1[at] = following
                hor, ver = hor[OWN], ver[OWN]
            if kind == "u" and not later:
                history[2 * step, x] = hor
                history[2 * step + 1, x] = ver
            if later:
                if kind == "u":
                    other = partner_mid[at, OWN, :] if step else partner_end[x]
                else:
                    other = following if step else following[OWN]
                    hor = partner[2 * (1 - step), x]
                    ver = partner[2 * (1 - step) + 1, x]
                sum_h, sum_v = other * hor, other * ver
                if step:
                    sum_h, sum_v = total[0, x] + sum_h, total[1, x] + sum_v
                elif r > ROUNDS // 2:
                    sum_h, sum_v = total_in[0, x] + sum_h, total_in[1, x] + sum_v
                total[0, x] = sum_h
                total[1, x] = sum_v


def pack_out(scal, u, a, index, total_u, total_a, coefs, *refs):
    outs, grads = refs[:8], refs[8]
    for x in range(NXA):
        gh = (total_u[0, x] + total_a[0, x]) * UNSCALE
        gv = (total_u[1, x] + total_a[1, x]) * UNSCALE
        slow, aniso = coefs[x, 0:ZS, :], coefs[x, ZS:, :]
        grads[x, 0:ZS, :] = (1.0 + 2.0 * aniso) * gh + gv
        grads[x, ZS:, :] = (2.0 * slow) * gh
    low = half_lanes((ZS, 128))
    for n, out in enumerate(outs):
        block = block_of(scal, FAR_FIRST[n])
        for f, field in enumerate((u, a)):
            for i in range(4):
                x = (block >> 1) * BX + 2 * i
                x0 = field[pl.ds(x, 1)].reshape(ZS, 128)
                x1 = field[pl.ds(x + 1, 1)].reshape(ZS, 128)
                piece = jnp.where(low, x0, roll_half(x1))
                upper = jnp.where(low, roll_half(x0), x1)
                at = 256 + (f * 4 + i) * ZS
                out[at : at + ZS, :] = jnp.where((block & 1) == 0, piece, upper)

        def stripe(ix, carry, out=out, block=block):
            for part in range(2):
                row = index[part, pl.ds(ix * 8 + block, 1), :]
                lane = jnp.broadcast_to(row & 127, (8, 128))
                which = jnp.broadcast_to(row >> 7, (8, 128))
                totals = [jnp.zeros((8, 128), F32) for t in range(4)]
                for x in range(BX):
                    hit = which == x
                    for t in range(4):
                        value = jnp.take_along_axis(
                            grads[ix * BX + x, 8 * t : 8 * t + 8, :], lane, axis=1, mode="promise_in_bounds"
                        )
                        totals[t] = jnp.where(hit, value, totals[t])
                for t in range(4):
                    at = pl.multiple_of((ix * 2 + part) * 32 + 8 * t, 8)
                    out[pl.ds(at, 8), :] = totals[t]
            return carry

        lax.fori_loop(0, GX, stripe, 0)


def name_slots(index, picks):
    named = jnp.concatenate([index[n % 2, 32 + n // 2 : 33 + n // 2, :] for n in range(8)], axis=1)
    for block in range(4):
        slot = lax.broadcasted_iota(jnp.int32, (256, 1024), 0) + block * 256
        pick = slot == jnp.broadcast_to(named, (256, 1024))
        picks[block * 256 : (block + 1) * 256, :] = pick.astype(F32).astype(BF16)


def finish(scal, picks, *refs):
    gots, (u_out, a_out, model, turned, columns) = refs[:8], refs[8:]
    for f, out in enumerate((u_out, a_out)):
        for i in range(4):
            for n, e in enumerate(FAR_FIRST):
                at = 256 + (f * 4 + i) * ZS
                turned[pl.ds(slab_of(scal, e), ZS), :] = gots[n][at : at + ZS, :]
            out[2 * i : 2 * i + 2] = turned[...].T.reshape(2, BY, 128)
    for n, e in enumerate(FAR_FIRST):
        for m in range(8):
            for comp in range(2):
                rows = pl.ds(pl.multiple_of(comp * 128 + slab_of(scal, e), ZS), ZS)
                at = m * 32 + comp * ZS
                columns[rows, m * 128 : (m + 1) * 128] = gots[n][at : at + ZS, :]
    values = columns[...]
    high = values.astype(BF16)
    rest = (values - high.astype(F32)).astype(BF16)
    for block in range(4):
        pick = picks[block * 256 : (block + 1) * 256, :]
        dims = (((1,), (1,)), ((), ()))
        sums = lax.dot_general(pick, high, dims, preferred_element_type=F32)
        sums = sums + lax.dot_general(pick, rest, dims, preferred_element_type=F32)
        for comp in range(2):
            model[pl.ds(block * 512 + comp, 256, stride=2), :] = sums[:, comp * 128 : (comp + 1) * 128]


def by_half(h, mine, other):
    first = jnp.where(h == 0, mine, other)
    second = jnp.where(h == 0, other, mine)
    both = jnp.stack([first, second], axis=1)
    return both.reshape((GX * GY,) + mine.shape[1:])


def exchange(x):
    return lax.all_to_all(x, ("gx", "gy"), split_axis=0, concat_axis=0, tiled=True)


def slab_body(
    forward_prev,
    forward_now,
    adjoint_prev,
    adjoint_now,
    model_table,
    tile_owner,
    tile_slot,
    source_index,
    wavelet,
    receiver_depth,
    traces,
):
    h = lax.axis_index("gz")
    ix, iy = lax.axis_index("gx"), lax.axis_index("gy")
    chip = jnp.where(iy == 0, ix, 2 * GX - 1 - ix)
    line = 2 * chip + h
    scal = jnp.stack(
        [h, ix, iy, lax.axis_index("shots"), line, source_index[0], source_index[1], source_index[2]]
    ).astype(jnp.int32)

    trace_half = lax.dynamic_slice_in_dim(traces, h * 8, 8, axis=0)
    (small,) = call(pack_small, [((5, BX, 128), F32)], vmem(4), moved=MIB // 16, flops=1 << 16)(
        tile_owner.reshape(1, BX * BY), tile_slot.reshape(1, BX * BY), receiver_depth, trace_half
    )
    keep, give = call(
        pack_table, [((GX, 128, 128), F32)] * 2, [SMEM] + vmem(1), moved=2 * MIB, flops=1 << 20
    )(scal, model_table.reshape(2048, 128))
    (sent,) = call(assemble, [((GX * GY, 168, 128), F32)], [SMEM] + vmem(3), moved=2 * MIB, flops=1 << 20)(
        scal, keep, to_sibling(give), small
    )
    arrived = exchange(sent)
    table_mine = arrived[:, :128].reshape(8, 4, 32, 128)
    small_mine = arrived[:, 128:].reshape(8, 5, BX, 128)
    table_other = lax.ppermute(table_mine, "shots", SWAP)
    small_other = to_sibling(small_mine)

    keep, give = call(
        pack_fields, [((4, 4, 4, ZS, 128), F32)] * 2, [SMEM] + vmem(4), moved=2 * MIB, flops=1 << 20
    )(scal, forward_prev, forward_now, adjoint_prev, adjoint_now)
    fields = exchange(by_half(h, keep, to_sibling(give)))

    plane, drive = ((NXA, 128), jnp.int32), ((STEPS, NXA, 128), F32)
    ids_slab, ids_owner, depth, traces, pulse, pulse_depth, place_info = call(
        unpack_small,
        [plane] * 3 + [drive, drive, plane, ((3, 8, 128), jnp.int32)],
        [SMEM] * 2 + vmem(2),
        moved=MIB // 2,
        flops=1 << 20,
    )(scal, wavelet, small_mine, small_other)
    coef_shape = ((NXA, 2 * ZS, 128), F32)
    half_shape = ((NXA, 2 * HALO, 128), F32)
    (coefs,) = call(
        functools.partial(gather_half, False), [coef_shape], [SMEM] + vmem(2), moved=MIB, flops=1 << 24
    )(scal, table_mine, ids_slab)
    coefs, coefs_sib, coefs_off = call(
        functools.partial(gather_half, True),
        [coef_shape, half_shape, half_shape],
        [SMEM] + vmem(3),
        moved=2 * MIB,
        flops=1 << 24,
    )(scal, table_other, ids_slab, coefs)
    ext_shape = ((NXA, ZE, 128), F32)
    own_shape = ((NXA, ZS, 128), F32)
    slow, aniso = call(extend_coefs, [ext_shape] * 2, [SMEM] + vmem(3), moved=2 * MIB, flops=1 << 20)(
        scal, coefs, to_sibling(coefs_sib), to_off_chip(coefs_off)
    )
    (index,) = call(
        index_kernel,
        [((2, 40, 128), jnp.int32)],
        [SMEM] + vmem(2),
        moved=MIB // 4,
        flops=1 << 24,
    )(scal, ids_slab, ids_owner)

    fields, index = lax.optimization_barrier((fields, index))
    first_halo = ((2, NXA, HALO, 128), F32)
    unpacked = call(
        unpack_fields,
        [own_shape, own_shape, first_halo, first_halo] * 2,
        [SMEM] + vmem(1),
        moved=4 * MIB,
        flops=1 << 20,
    )(scal, fields)
    bands = matrices()
    halo = ((1, NXA, HALO, 128), F32)
    state = {}
    for n, kind in enumerate("ua"):
        prev, now, sib, off = unpacked[4 * n : 4 * n + 4]
        state[kind] = [now, to_sibling(sib), to_off_chip(off), prev]
    history, mids, ends, totals = {}, {}, {}, {}
    for r in range(ROUNDS):
        for kind in "ua":
            later, last = r >= ROUNDS // 2, r == ROUNDS - 1
            args = [place_info] + ([pulse, pulse_depth] if kind == "u" else [traces, depth])
            args += state[kind] + [slow, aniso] + bands
            if later:
                partner = ROUNDS - 1 - r
                args += [mids[partner], ends[partner]] if kind == "u" else [history[partner]]
                if r > ROUNDS // 2:
                    args += [totals[kind]]
            outs = [own_shape, (EXT_SHAPE, F32)] + ([] if last else [halo, halo])
            if later:
                outs.append(((2, NXA, ZS, 128), F32))
            elif kind == "u":
                outs.append(((4, NXA, ZS, 128), F32))
            res = call(
                functools.partial(round_kernel, kind, r),
                outs,
                vmem(len(args)),
                round_scratch(),
                moved=4 * MIB,
                flops=1 << 24,
            )(*args)
            own, mid = res[0], res[1]
            if later:
                totals[kind] = res[-1]
            elif kind == "u":
                history[r] = res[-1]
            if kind == "a":
                mids[r], ends[r] = mid, own
            if last:
                state[kind] = [own]
            else:
                state[kind] = [own, to_sibling(res[2]), to_off_chip(res[3]), mid]

    packed = call(
        pack_out,
        [((384, 128), F32)] * 8,
        [SMEM] + vmem(6),
        [pltpu.VMEM((NXA, 2 * ZS, 128), F32)],
        moved=4 * MIB,
        flops=1 << 22,
    )(scal, state["u"][0], state["a"][0], index, totals["u"], totals["a"], coefs)
    index, _ = lax.optimization_barrier((index, packed[7]))
    (picks,) = call(name_slots, [((1024, 1024), BF16)], vmem(1), moved=4 * MIB, flops=1 << 22)(index)
    arrived = [to_blocks(x, e) for x, e in zip(packed, FAR_FIRST)]
    u, a, model = call(
        finish,
        [((BX, BY, BZ), F32)] * 2 + [((2048, 128), F32)],
        [SMEM] + vmem(9),
        [pltpu.VMEM((128, 128), F32), pltpu.VMEM((256, 1024), F32)],
        moved=4 * MIB,
        flops=1 << 28,
    )(scal, picks, *arrived)
    return (u, a, model.reshape(1, 1024, 2, 128))


def solution(mesh):
    in_specs = (
        P(("shots", "gx"), "gy", "gz"),
        P(("shots", "gx"), "gy", "gz"),
        P(("shots", "gx"), "gy", "gz"),
        P(("shots", "gx"), "gy", "gz"),
        P("gz", ("gx", "gy"), None, None),
        P(("shots", "gz"), "gx", "gy", None, None),
        P(("shots", "gz"), "gx", "gy", None),
        P("shots"),
        P("shots"),
        P(("shots", "gx"), "gy"),
        P(None, ("shots", "gx"), "gy"),
    )
    out_specs = (
        P(("shots", "gx"), "gy", "gz"),
        P(("shots", "gx"), "gy", "gz"),
        P("gz", ("shots", "gx", "gy"), None, None),
    )
    body = slab_body if slabs_fit(mesh) else block_body
    return jax.shard_map(body, mesh=mesh, in_specs=in_specs, out_specs=out_specs, check_vma=False)
```

```python
import functools

import jax
import jax.numpy as jnp
import numpy as np
from jax import lax
from jax.experimental import pallas as pl
from jax.experimental.pallas import tpu as pltpu
from jax.sharding import PartitionSpec as P

STENCIL = (-205.0 / 72.0, 8.0 / 5.0, -1.0 / 5.0, 8.0 / 315.0, -1.0 / 560.0)


def with_halo(block, sides, width):
    for axis, dim in sides:
        count = lax.axis_size(axis)
        forward = [(i, i + 1) for i in range(count - 1)]
        backward = [(target, source) for source, target in forward]
        low = lax.ppermute(
            lax.slice_in_dim(block, block.shape[dim] - width, None, axis=dim), axis, forward
        )
        high = lax.ppermute(lax.slice_in_dim(block, 0, width, axis=dim), axis, backward)
        block = jnp.concatenate([low, block, high], axis=dim)
    return block


def derivatives(padded, shape):
    size_x, size_y, size_z = shape

    def window(off_x, off_y, off_z):
        return padded[
            4 + off_x : 4 + off_x + size_x,
            4 + off_y : 4 + off_y + size_y,
            4 + off_z : 4 + off_z + size_z,
        ]

    center = window(0, 0, 0)
    along_x = STENCIL[0] * center
    along_y = STENCIL[0] * center
    along_z = STENCIL[0] * center
    for offset in range(1, 5):
        along_x = along_x + STENCIL[offset] * (window(offset, 0, 0) + window(-offset, 0, 0))
        along_y = along_y + STENCIL[offset] * (window(0, offset, 0) + window(0, -offset, 0))
        along_z = along_z + STENCIL[offset] * (window(0, 0, offset) + window(0, 0, -offset))
    return (along_x + along_y, along_z)


def propagate(previous, current, slow_coef, aniso_coef, padded):
    horizontal, vertical = derivatives(padded, current.shape)
    laplacian = (1.0 + 2.0 * aniso_coef) * horizontal + vertical
    following = 2.0 * current - previous + slow_coef * laplacian
    return (following, laplacian, horizontal)


def block_body(
    forward_prev,
    forward_now,
    adjoint_prev,
    adjoint_now,
    model_table,
    tile_owner,
    tile_slot,
    source_index,
    wavelet,
    receiver_depth,
    traces,
):
    block_x, block_y, block_z = forward_now.shape
    columns = block_x * block_y
    owners_count = lax.axis_size(("gx", "gy"))
    capacity = max(2, 2 * columns // owners_count)
    column_owner = tile_owner.reshape(columns)
    column_slot = tile_slot.reshape(columns)
    local_table = model_table[0]
    held_count = local_table.shape[0]
    one_hot = (column_owner[:, None] == jnp.arange(owners_count, dtype=jnp.int32)[None, :]).astype(
        jnp.float32
    )
    earlier = (
        jnp.arange(columns, dtype=jnp.int32)[:, None]
        > jnp.arange(columns, dtype=jnp.int32)[None, :]
    ).astype(jnp.float32)
    counted_before = jnp.dot(earlier, one_hot, precision=lax.Precision.HIGHEST)
    slot_rank = jnp.sum(counted_before * one_hot, axis=1).astype(jnp.int32)
    requests = (
        jnp.full((owners_count, capacity), -1, jnp.int32)
        .at[column_owner, slot_rank]
        .set(column_slot)
    )
    received = lax.all_to_all(requests, ("gx", "gy"), split_axis=0, concat_axis=0, tiled=True)
    clipped = jnp.clip(received, 0, held_count - 1)
    fetched = lax.all_to_all(
        local_table[clipped], ("gx", "gy"), split_axis=0, concat_axis=0, tiled=True
    )
    cell_params = (
        fetched[column_owner, slot_rank].reshape(block_x, block_y, 2, block_z).transpose(2, 0, 1, 3)
    )
    slow_coef = cell_params[0]
    aniso_coef = cell_params[1]
    grid_x = lax.axis_index("gx") * block_x + jnp.arange(block_x, dtype=jnp.int32)[:, None, None]
    grid_y = lax.axis_index("gy") * block_y + jnp.arange(block_y, dtype=jnp.int32)[None, :, None]
    grid_z = lax.axis_index("gz") * block_z + jnp.arange(block_z, dtype=jnp.int32)[None, None, :]
    source_mask = (
        (grid_x == source_index[0]) & (grid_y == source_index[1]) & (grid_z == source_index[2])
    ).astype(jnp.float32)
    receiver_mask = (grid_z == receiver_depth[:, :, None]).astype(jnp.float32)

    def forward(carried, weight):
        previous, current = carried
        padded = with_halo(current, (("gx", 0), ("gy", 1), ("gz", 2)), 4)
        following, laplacian, horizontal = propagate(
            previous, current, slow_coef, aniso_coef, padded
        )
        following = following + weight * source_mask
        return ((current, following), (laplacian, horizontal))

    (_, forward_final), (laplacians, horizontals) = lax.scan(
        forward, (forward_prev, forward_now), wavelet
    )

    def backward(carried, inputs):
        previous, current, grad_slow, grad_aniso = carried
        trace_row, laplacian, horizontal = inputs
        padded = with_halo(current, (("gx", 0), ("gy", 1), ("gz", 2)), 4)
        following, _, _ = propagate(previous, current, slow_coef, aniso_coef, padded)
        following = following + trace_row[:, :, None] * receiver_mask
        grad_slow = grad_slow + following * laplacian
        grad_aniso = grad_aniso + following * (2.0 * slow_coef * horizontal)
        return ((current, following, grad_slow, grad_aniso), None)

    zero_field = jnp.zeros((block_x, block_y, block_z), jnp.float32)
    (_, adjoint_final, grad_slow, grad_aniso), _ = lax.scan(
        backward,
        (adjoint_prev, adjoint_now, zero_field, zero_field),
        (traces[::-1], laplacians[::-1], horizontals[::-1]),
    )
    grad_cells = (
        jnp.stack([grad_slow, grad_aniso]).transpose(1, 2, 0, 3).reshape(columns, 2, block_z)
    )
    outgoing = (
        jnp.zeros((owners_count, capacity, 2, block_z), jnp.float32)
        .at[column_owner, slot_rank]
        .set(grad_cells)
    )
    returned = lax.all_to_all(outgoing, ("gx", "gy"), split_axis=0, concat_axis=0, tiled=True)
    target = jnp.where(received < 0, held_count, received).reshape(owners_count * capacity)
    model_gradient = (
        jnp.zeros((held_count, 2, block_z), jnp.float32)
        .at[target]
        .add(returned.reshape(owners_count * capacity, 2, block_z), mode="drop")
    )
    return (forward_final, adjoint_final, model_gradient[None])


BX, BY, BZ = 8, 64, 128
GX, GY = 4, 2
NXA, NYA = BX * GX, BY * GY
ZS = 16
ZE = 32
HALO = 8
OWN = slice(HALO, HALO + ZS)
SCALE = 5040.0
UNSCALE = 1.0 / SCALE
PADX = 4
EXT_SHAPE = (NXA + 2 * PADX, ZE, 128)
INNER = slice(PADX, PADX + NXA)
STEPS = 16
ROUNDS = STEPS // 2
MIB = 1 << 20
F32 = jnp.float32
BF16 = jnp.bfloat16
H, IX, IY, SHOT, LINE, SX, SY, SZ = range(8)


def slabs_fit(mesh):
    names = ("shots", "gx", "gy", "gz")
    return tuple(mesh.shape[n] for n in names) == (2, GX, GY, 2)


def line_device(place):
    chip, core = divmod(place, 2)
    ix, iy = (chip, 0) if chip < GX else (2 * GX - 1 - chip, 1)
    return (ix * GY + iy) * 2 + core


def off_chip_pairs():
    count = 2 * GX * GY
    pairs = []
    for low in range(1, count, 2):
        a, b = line_device(low), line_device((low + 1) % count)
        pairs += [(a, b), (b, a)]
    return pairs


OFF_PAIRS = off_chip_pairs()
SWAP = [(0, 1), (1, 0)]


def to_sibling(x):
    return lax.ppermute(x, "gz", SWAP)


def to_off_chip(x):
    return lax.ppermute(x, ("gx", "gy", "gz"), OFF_PAIRS)


def spread(e):
    return [(2 * s + c, 2 * (s ^ e ^ c) + (s & 1)) for s in range(GX * GY) for c in range(2)]


def to_blocks(x, e):
    return lax.ppermute(x, ("gx", "gy", "gz"), spread(e))


FAR_FIRST = (6, 7, 4, 5, 2, 3, 0, 1)


def slab_of(scal, e):
    ix = scal[IX] ^ (e >> 1)
    core = scal[IY] ^ (e & 1) ^ scal[H]
    chip = jnp.where(scal[H] == 0, ix, GX - 1 - ix)
    return pl.multiple_of(chip * 2 * ZS + core * ZS, ZS)


def block_of(scal, e):
    return (scal[IX] * GY + scal[IY]) ^ e ^ scal[H]


def band(size):
    out = np.zeros((size, size), np.float32)
    for offset in range(1, 5):
        value = round(STENCIL[offset] * SCALE)
        for i in range(size - offset):
            out[i, i + offset] = value
            out[i + offset, i] = value
    return out


def matrices():
    along_y = band(NYA)
    along_y = np.concatenate([along_y, along_y], 0)
    along_z = band(ZE)
    full = np.kron(np.eye(8, dtype=np.float32), along_z)
    own = np.kron(np.eye(8, dtype=np.float32), along_z[OWN])
    full, own = [np.concatenate([m, m], 1) for m in (full, own)]
    return [jnp.asarray(m, BF16) for m in (along_y, full, own)]


def vmem(count):
    return [pl.BlockSpec(memory_space=pltpu.VMEM)] * count


SMEM = pl.BlockSpec(memory_space=pltpu.SMEM)


def call(kernel, outs, specs, scratch=(), limit=24, flops=0, moved=0, aliases=None):
    return pl.pallas_call(
        kernel,
        out_shape=[jax.ShapeDtypeStruct(s, d) for s, d in outs],
        in_specs=specs,
        out_specs=vmem(len(outs)),
        scratch_shapes=list(scratch),
        input_output_aliases=aliases or {},
        compiler_params=pltpu.CompilerParams(vmem_limit_bytes=limit * MIB),
        cost_estimate=pl.CostEstimate(flops=flops, bytes_accessed=moved, transcendentals=0),
    )


def half_lanes(shape):
    return lax.broadcasted_iota(jnp.int32, shape, len(shape) - 1) < BY


def roll_half(x):
    return pltpu.roll(x, BY, x.ndim - 1)


def place(scal, chunk):
    chip, core = divmod(chunk, 2)
    mine = core == scal[H]
    return mine, jnp.where(scal[H] == 0, chip, GX - 1 - chip)


def pack_small(owner, slot, depth, traces, out):
    for tt in range(4):
        out[tt] = jnp.concatenate([traces[2 * tt], traces[2 * tt + 1]], axis=1)
    low = half_lanes((1, 128))
    ids = owner[...] * 1024 + slot[...]
    rows = []
    for x in range(BX):
        pair = ids[:, (x // 2) * 128 : (x // 2 + 1) * 128].astype(F32)
        rows.append(roll_half(pair) if x % 2 else pair)
    rows = jnp.concatenate(rows, axis=0)
    depths = depth[...].astype(F32)
    depths = jnp.concatenate([depths, depths], axis=1)
    out[4] = jnp.where(half_lanes((8, 128)), rows, depths)


def pack_table(scal, table, keep, give):
    for q in range(4):
        for comp in range(2):
            turned = table[pl.ds(q * 256 + comp, 128, stride=2), :].T
            at = q * 32 + comp * ZS
            for chunk in range(8):
                mine, g = place(scal, chunk)
                piece = turned[chunk * ZS : (chunk + 1) * ZS][None]

                @pl.when(mine)
                def _():
                    keep[pl.ds(g, 1), at : at + ZS, :] = piece

                @pl.when(jnp.logical_not(mine))
                def _():
                    give[pl.ds(g, 1), at : at + ZS, :] = piece


def assemble(scal, keep, got, small, out):
    h = scal[H]
    for ix in range(GX):
        out[pl.ds(ix * GY + h, 1), 0:128, :] = keep[ix][None]
        out[pl.ds(ix * GY + 1 - h, 1), 0:128, :] = got[ix][None]
    for n in range(GX * GY):
        out[n, 128:, :] = small[...].reshape(40, 128)


def pack_fields(scal, *refs):
    fields, (keep, give) = refs[:4], refs[4:]
    for f in range(4):
        for i in range(4):
            pair = fields[f][2 * i : 2 * i + 2].reshape(128, 128)
            turned = pair.T
            for chunk in range(8):
                mine, g = place(scal, chunk)
                piece = turned[chunk * ZS : (chunk + 1) * ZS][None]

                @pl.when(mine)
                def _():
                    keep[pl.ds(g, 1), f, i] = piece

                @pl.when(jnp.logical_not(mine))
                def _():
                    give[pl.ds(g, 1), f, i] = piece


def unpack_small(scal, wavelet, mine, other, ids_slab, ids_owner, depth, traces, pulse, pulse_depth, place):
    low = half_lanes((8, 128))
    h = scal[H]
    x_at = lax.broadcasted_iota(jnp.int32, (NXA, 128), 0)
    y_at = lax.broadcasted_iota(jnp.int32, (NXA, 128), 1)
    at_source = (x_at == scal[SX]) & (y_at == scal[SY])
    for t in range(STEPS):
        pulse[t] = jnp.where(at_source, wavelet[t], 0.0)
    pulse_depth[...] = jnp.full((NXA, 128), scal[SZ], jnp.int32)
    place[0] = jnp.full((8, 128), h, jnp.int32)
    place[1] = jnp.full((8, 128), jnp.where(is_edge(scal), 1, 0), jnp.int32)
    place[2] = jnp.full((8, 128), scal[LINE] * ZS - HALO, jnp.int32)
    for ix in range(GX):
        rows = slice(ix * BX, (ix + 1) * BX)
        for ref, is_mine in ((mine, True), (other, False)):
            a, b = ref[ix * GY], ref[ix * GY + 1]
            core = h if is_mine else 1 - h
            for tt in range(4):
                even = jnp.where(low, a[tt], roll_half(b[tt]))
                odd = jnp.where(low, roll_half(a[tt]), b[tt])
                traces[pl.ds(core * 8 + 2 * tt, 1), rows, :] = even[None]
                traces[pl.ds(core * 8 + 2 * tt + 1, 1), rows, :] = odd[None]
            ids = jnp.where(low, a[4], roll_half(b[4])).astype(jnp.int32)
            if is_mine:
                ids_owner[rows, :] = ids
                depth[rows, :] = jnp.where(low, roll_half(a[4]), b[4]).astype(jnp.int32)

            @pl.when(core == scal[IY])
            def _():
                ids_slab[rows, :] = ids


def gather_half(second, scal, table, ids, *refs):
    if second:
        before, out, sib, off = refs
    else:
        (out,) = refs
    half = 1 - scal[SHOT] if second else scal[SHOT]

    def column(x, carry):
        row = ids[pl.ds(x, 1), :]
        lane = jnp.broadcast_to(row & 127, (8, 128))
        chunk = jnp.broadcast_to(row >> 7, (8, 128))
        if second:
            totals = [before[x, 8 * t : 8 * t + 8, :] for t in range(4)]
        else:
            totals = [jnp.zeros((8, 128), F32) for t in range(4)]
        for j in range(32):
            hit = chunk == (j // 4) * 8 + half * 4 + j % 4
            for t in range(4):
                value = jnp.take_along_axis(
                    table[j // 4, j % 4, 8 * t : 8 * t + 8, :], lane, axis=1, mode="promise_in_bounds"
                )
                totals[t] = jnp.where(hit, value, totals[t])
        for t in range(4):
            out[x, 8 * t : 8 * t + 8, :] = totals[t]
        return carry

    lax.fori_loop(0, NXA, column, 0)
    if second:
        h = scal[H]
        for comp in range(2):
            rows = slice(comp * HALO, (comp + 1) * HALO)
            sib[:, rows, :] = out[:, pl.ds(comp * ZS + HALO * (1 - h), HALO), :]
            off[:, rows, :] = out[:, pl.ds(comp * ZS + HALO * h, HALO), :]


def is_edge(scal):
    return (scal[LINE] == 0) | (scal[LINE] == 2 * GX * GY - 1)


def extend_coefs(scal, coefs, sib, off, slow, aniso):
    sib_at = (ZE - HALO) * (1 - scal[H])
    off_at = (ZE - HALO) * scal[H]
    inside = jnp.where(is_edge(scal), 0.0, 1.0)
    slow[:, OWN, :] = coefs[:, 0:ZS, :] * UNSCALE
    slow[:, pl.ds(sib_at, HALO), :] = sib[:, 0:HALO, :] * UNSCALE
    slow[:, pl.ds(off_at, HALO), :] = off[:, 0:HALO, :] * (inside * UNSCALE)
    aniso[:, OWN, :] = 1.0 + 2.0 * coefs[:, ZS:, :]
    aniso[:, pl.ds(sib_at, HALO), :] = 1.0 + 2.0 * sib[:, HALO:, :]
    aniso[:, pl.ds(off_at, HALO), :] = 1.0 + 2.0 * off[:, HALO:, :]


def unpack_fields(scal, got, *outs):
    low = half_lanes((ZS, 128))
    h = scal[H]
    for kind in range(2):
        prev, now, sib, off = outs[4 * kind : 4 * kind + 4]
        for step, own in ((0, prev), (1, now)):
            f = 2 * kind + step
            for ix in range(GX):
                for i in range(4):
                    a, b = got[ix * GY, f, i], got[ix * GY + 1, f, i]
                    x = ix * BX + 2 * i
                    own[x] = jnp.where(low, a, roll_half(b))
                    own[x + 1] = jnp.where(low, roll_half(a), b)
            sib[step] = own[:, pl.ds(HALO * (1 - h), HALO), :]
            off[step] = own[:, pl.ds(HALO * h, HALO), :]


def index_kernel(scal, ids_slab, ids_owner, out):
    me = scal[IX] * GY + scal[IY]
    sub = lax.broadcasted_iota(jnp.int32, (8, 128), 0)
    lane = lax.broadcasted_iota(jnp.int32, (8, 128), 1)
    slots = []
    masks = [(jnp.broadcast_to(ids_slab[x : x + 1, :] >> 10, (8, 128)) == sub).astype(F32) for x in range(NXA)]
    for x in range(BX):
        rows = jnp.concatenate([ids_owner[s * BX + x : s * BX + x + 1, :] for s in range(GX)] * 2, axis=0)
        masks.append((((rows >> 10) == me) & (sub < GX)).astype(F32))
        slots.append((rows & 1023).astype(F32))
    bits = jnp.concatenate(masks, axis=0).astype(BF16)
    first = lax.broadcasted_iota(jnp.int32, (128, 128), 0)
    second = lax.broadcasted_iota(jnp.int32, (128, 128), 1)
    upto = (first <= second).astype(F32).astype(BF16)
    along = jnp.dot(bits, upto, preferred_element_type=F32)
    sums = jnp.dot(bits, jnp.ones((128, 128), BF16), preferred_element_type=F32)
    r0 = lax.broadcasted_iota(jnp.int32, (64, 64), 0)
    r1 = lax.broadcasted_iota(jnp.int32, (64, 64), 1)
    earlier = (((r0 & 7) == (r1 & 7)) & (r1 < r0)).astype(F32).astype(BF16)
    for group in range(GX + 1):
        rows = slice(64 * group, 64 * group + 64)
        above = jnp.dot(earlier, sums[rows].astype(BF16), preferred_element_type=F32)
        counts = along[rows] + above
        ends = sums[rows] + above
        for part in range(2):
            r = (lane + 128 * part).astype(F32)
            at_x = jnp.zeros((8, 128), jnp.int32)
            for x in range(BX):
                at_x = at_x + (ends[8 * x : 8 * x + 8] <= r).astype(jnp.int32)

            def pick(tables, at):
                value = jnp.zeros((8, 128), F32)
                for x in range(BX):
                    taken = jnp.take_along_axis(tables[x], at, axis=1, mode="promise_in_bounds")
                    value = jnp.where(at_x == x, taken, value)
                return value

            tables = [counts[8 * x : 8 * x + 8] for x in range(BX)]
            at_y = jnp.zeros((8, 128), jnp.int32)
            for step in (64, 32, 16, 8, 4, 2, 1):
                at_y = jnp.where(pick(tables, at_y + (step - 1)) <= r, at_y + step, at_y)
            at_y = jnp.minimum(at_y, 127)
            if group < GX:
                found = at_x * 128 + at_y
            else:
                found = pick(slots, at_y).astype(jnp.int32)
            out[part, 8 * group : 8 * group + 8] = jnp.where(at_x < BX, found, -1)


def bands_of(field, g, along_y, along_z, own):
    first = PADX + 8 * g
    depth = ZS if own else ZE
    whole = field[first : first + 8].reshape(8 * ZE, 128)
    high = whole.astype(BF16)
    rest = (whole - high.astype(F32)).astype(BF16)
    my = jnp.dot(jnp.concatenate([high, rest], axis=1), along_y[...], preferred_element_type=F32)
    mz = jnp.dot(along_z[...], jnp.concatenate([high, rest], axis=0), preferred_element_type=F32)
    return my.reshape(8, ZE, 128), mz.reshape(8, depth, 128)


def round_scratch():
    return [pltpu.VMEM(EXT_SHAPE, F32)]


def round_kernel(kind, r, *refs):
    refs = list(refs)
    take = lambda n: [refs.pop(0) for _ in range(n)]
    first, later, last = r == 0, r >= ROUNDS // 2, r == ROUNDS - 1
    place, drive, depth, own, sib, off, prev, slow, aniso, along_y, along_z, along_z_own = take(12)
    if later:
        if kind == "u":
            partner_mid, partner_end = take(2)
        else:
            (partner,) = take(1)
        if r > ROUNDS // 2:
            (total_in,) = take(1)
    out_own, out_mid = take(2)
    if not last:
        out_sib, out_off = take(2)
    if later:
        (total,) = take(1)
    elif kind == "u":
        (history,) = take(1)
    (e0,) = take(1)
    e1 = out_mid

    core_0 = place[0] == 0
    inside = place[1] == 0
    zero = jnp.zeros((PADX, ZE, 128), F32)
    for e in (e0, e1):
        e[0:PADX] = zero
        e[PADX + NXA :] = zero

    def extend(e, own, n):
        for x in range(NXA):
            near, far = sib[n, x], jnp.where(inside, off[n, x], 0.0)
            e[PADX + x, 0:HALO] = jnp.where(core_0, far, near)
            e[PADX + x, OWN] = own[x]
            e[PADX + x, HALO + ZS :] = jnp.where(core_0, near, far)

    if first:
        extend(e0, own, 1)
        extend(e1, prev, 0)
        prev = e1
    else:
        extend(e0, own, 0)
    base = jnp.concatenate([place[2]] * (ZE // 8), axis=0) + lax.broadcasted_iota(jnp.int32, (ZE, 128), 0)

    def bands(step, g):
        if step:
            return bands_of(e1, g, along_y, along_z_own, True)
        return bands_of(e0, g, along_y, along_z, False)

    items = [(step, g) for step in range(2) for g in range(4)]
    ahead = bands(*items[0])
    for k, (step, g) in enumerate(items):
        my, mz = ahead
        if k + 1 < len(items):
            ahead = bands(*items[k + 1])
        t = 2 * r + step if kind == "u" else STEPS - 1 - (2 * r + step)
        field = e1 if step else e0
        zs = OWN if step else slice(0, ZE)
        count = ZS if step else ZE
        z = base[zs]
        for n in range(8):
            x = 8 * g + n
            at = PADX + x
            center = field[at, zs, :]
            hor = my[n, zs] + (2.0 * SCALE * STENCIL[0]) * center
            for i in range(1, 5):
                hor = hor + (SCALE * STENCIL[i]) * (field[at + i, zs, :] + field[at - i, zs, :])
            ver = mz[n] + (SCALE * STENCIL[0]) * center
            before = e0[at, OWN, :] if step else prev[at]
            lap = aniso[x, zs, :] * hor + ver
            following = 2.0 * center - before + slow[x, zs, :] * lap
            at_z = jnp.broadcast_to(depth[x : x + 1, :], (count, 128))
            value = jnp.broadcast_to(drive[t, x : x + 1, :], (count, 128))
            following = following + jnp.where(z == at_z, value, 0.0)
            if step:
                out_own[x] = following
                if not last:
                    low, high = following[:HALO], following[HALO:]
                    out_sib[0, x] = jnp.where(core_0, high, low)
                    out_off[0, x] = jnp.where(core_0, low, high)
            else:
                e1[at] = following
                hor, ver = hor[OWN], ver[OWN]
            if kind == "u" and not later:
                history[2 * step, x] = hor
                history[2 * step + 1, x] = ver
            if later:
                if kind == "u":
                    other = partner_mid[at, OWN, :] if step else partner_end[x]
                else:
                    other = following if step else following[OWN]
                    hor = partner[2 * (1 - step), x]
                    ver = partner[2 * (1 - step) + 1, x]
                sum_h, sum_v = other * hor, other * ver
                if step:
                    sum_h, sum_v = total[0, x] + sum_h, total[1, x] + sum_v
                elif r > ROUNDS // 2:
                    sum_h, sum_v = total_in[0, x] + sum_h, total_in[1, x] + sum_v
                total[0, x] = sum_h
                total[1, x] = sum_v


def pack_final(scal, u, a, *outs):
    low = half_lanes((ZS, 128))
    for n, out in enumerate(outs):
        block = block_of(scal, FAR_FIRST[n])
        for f, field in enumerate((u, a)):
            for i in range(4):
                x = (block >> 1) * BX + 2 * i
                x0 = field[pl.ds(x, 1)].reshape(ZS, 128)
                x1 = field[pl.ds(x + 1, 1)].reshape(ZS, 128)
                piece = jnp.where(low, x0, roll_half(x1))
                upper = jnp.where(low, roll_half(x0), x1)
                out[f, i] = jnp.where((block & 1) == 0, piece, upper)


def pack_grads(scal, index, total_u, total_a, coefs, *refs):
    outs, grads = refs[:8], refs[8]
    for x in range(NXA):
        gh = (total_u[0, x] + total_a[0, x]) * UNSCALE
        gv = (total_u[1, x] + total_a[1, x]) * UNSCALE
        slow, aniso = coefs[x, 0:ZS, :], coefs[x, ZS:, :]
        grads[x, 0:ZS, :] = (1.0 + 2.0 * aniso) * gh + gv
        grads[x, ZS:, :] = (2.0 * slow) * gh
    for n, out in enumerate(outs):
        block = block_of(scal, FAR_FIRST[n])

        def stripe(ix, carry, out=out, block=block):
            for part in range(2):
                row = index[part, pl.ds(ix * 8 + block, 1), :]
                lane = jnp.broadcast_to(row & 127, (8, 128))
                which = jnp.broadcast_to(row >> 7, (8, 128))
                totals = [jnp.zeros((8, 128), F32) for t in range(4)]
                for x in range(BX):
                    hit = which == x
                    for t in range(4):
                        value = jnp.take_along_axis(
                            grads[ix * BX + x, 8 * t : 8 * t + 8, :], lane, axis=1, mode="promise_in_bounds"
                        )
                        totals[t] = jnp.where(hit, value, totals[t])
                for t in range(4):
                    out[ix * 2 + part, 8 * t : 8 * t + 8, :] = totals[t]
            return carry

        lax.fori_loop(0, GX, stripe, 0)


def name_slots(index, picks):
    named = jnp.concatenate([index[n % 2, 32 + n // 2 : 33 + n // 2, :] for n in range(8)], axis=1)
    for block in range(4):
        slot = lax.broadcasted_iota(jnp.int32, (256, 1024), 0) + block * 256
        pick = slot == jnp.broadcast_to(named, (256, 1024))
        picks[block * 256 : (block + 1) * 256, :] = pick.astype(F32).astype(BF16)


def finish_fields(scal, *refs):
    gots, (u_out, a_out, turned) = refs[:8], refs[8:]
    for f, out in enumerate((u_out, a_out)):
        for i in range(4):
            for n, e in enumerate(FAR_FIRST):
                turned[f * 4 + i, pl.ds(slab_of(scal, e), ZS), :] = gots[n][f, i]
            out[2 * i : 2 * i + 2] = turned[f * 4 + i].T.reshape(2, BY, 128)


def finish_model(scal, picks, *refs):
    gots, (model, columns) = refs[:8], refs[8:]
    for n, e in enumerate(FAR_FIRST):
        for comp in range(2):
            rows = pl.ds(pl.multiple_of(comp * 128 + slab_of(scal, e), ZS), ZS)
            for m in range(8):
                columns[rows, m * 128 : (m + 1) * 128] = gots[n][m, comp * ZS : (comp + 1) * ZS, :]
    values = columns[...].T
    high = values.astype(BF16)
    rest = (values - high.astype(F32)).astype(BF16)
    both = jnp.concatenate([high, rest], axis=1)
    for block in range(4):
        sums = jnp.dot(picks[block * 256 : (block + 1) * 256, :], both, preferred_element_type=F32)
        sums = sums[:, :256] + sums[:, 256:]
        for comp in range(2):
            model[pl.ds(block * 512 + comp, 256, stride=2), :] = sums[:, comp * 128 : (comp + 1) * 128]


def by_half(h, mine, other):
    first = jnp.where(h == 0, mine, other)
    second = jnp.where(h == 0, other, mine)
    both = jnp.stack([first, second], axis=1)
    return both.reshape((GX * GY,) + mine.shape[1:])


def exchange(x):
    return lax.all_to_all(x, ("gx", "gy"), split_axis=0, concat_axis=0, tiled=True)


def slab_body(
    forward_prev,
    forward_now,
    adjoint_prev,
    adjoint_now,
    model_table,
    tile_owner,
    tile_slot,
    source_index,
    wavelet,
    receiver_depth,
    traces,
):
    h = lax.axis_index("gz")
    ix, iy = lax.axis_index("gx"), lax.axis_index("gy")
    chip = jnp.where(iy == 0, ix, 2 * GX - 1 - ix)
    line = 2 * chip + h
    scal = jnp.stack(
        [h, ix, iy, lax.axis_index("shots"), line, source_index[0], source_index[1], source_index[2]]
    ).astype(jnp.int32)

    trace_half = lax.dynamic_slice_in_dim(traces, h * 8, 8, axis=0)
    (small,) = call(pack_small, [((5, BX, 128), F32)], vmem(4), moved=MIB // 16, flops=1 << 16)(
        tile_owner.reshape(1, BX * BY), tile_slot.reshape(1, BX * BY), receiver_depth, trace_half
    )
    keep, give = call(
        pack_table, [((GX, 128, 128), F32)] * 2, [SMEM] + vmem(1), moved=2 * MIB, flops=1 << 20
    )(scal, lax.dynamic_slice_in_dim(model_table.reshape(2048, 128), lax.axis_index("shots") * 1024, 1024, axis=0))
    (sent,) = call(assemble, [((GX * GY, 168, 128), F32)], [SMEM] + vmem(3), moved=2 * MIB, flops=1 << 20)(
        scal, keep, to_sibling(give), small
    )
    arrived = exchange(sent)
    table_mine = arrived[:, :128].reshape(8, 4, 32, 128)
    small_mine = arrived[:, 128:].reshape(8, 5, BX, 128)
    table_other = lax.ppermute(table_mine, "shots", SWAP)
    small_other = to_sibling(small_mine)

    keep, give = call(
        pack_fields, [((4, 4, 4, ZS, 128), F32)] * 2, [SMEM] + vmem(4), moved=2 * MIB, flops=1 << 20
    )(scal, forward_prev, forward_now, adjoint_prev, adjoint_now)
    fields = exchange(by_half(h, keep, to_sibling(give)))

    plane, drive = ((NXA, 128), jnp.int32), ((STEPS, NXA, 128), F32)
    ids_slab, ids_owner, depth, traces, pulse, pulse_depth, place_info = call(
        unpack_small,
        [plane] * 3 + [drive, drive, plane, ((3, 8, 128), jnp.int32)],
        [SMEM] * 2 + vmem(2),
        moved=MIB // 2,
        flops=1 << 20,
    )(scal, wavelet, small_mine, small_other)
    coef_shape = ((NXA, 2 * ZS, 128), F32)
    half_shape = ((NXA, 2 * HALO, 128), F32)
    (coefs,) = call(
        functools.partial(gather_half, False), [coef_shape], [SMEM] + vmem(2), moved=MIB, flops=1 << 24
    )(scal, table_mine, ids_slab)
    coefs, coefs_sib, coefs_off = call(
        functools.partial(gather_half, True),
        [coef_shape, half_shape, half_shape],
        [SMEM] + vmem(3),
        moved=2 * MIB,
        flops=1 << 24,
    )(scal, table_other, ids_slab, coefs)
    ext_shape = ((NXA, ZE, 128), F32)
    own_shape = ((NXA, ZS, 128), F32)
    slow, aniso = call(extend_coefs, [ext_shape] * 2, [SMEM] + vmem(3), moved=2 * MIB, flops=1 << 20)(
        scal, coefs, to_sibling(coefs_sib), to_off_chip(coefs_off)
    )
    (index,) = call(
        index_kernel,
        [((2, 40, 128), jnp.int32)],
        [SMEM] + vmem(2),
        moved=MIB // 4,
        flops=1 << 24,
    )(scal, ids_slab, ids_owner)

    fields, index = lax.optimization_barrier((fields, index))
    first_halo = ((2, NXA, HALO, 128), F32)
    unpacked = call(
        unpack_fields,
        [own_shape, own_shape, first_halo, first_halo] * 2,
        [SMEM] + vmem(1),
        moved=4 * MIB,
        flops=1 << 20,
    )(scal, fields)
    bands = matrices()
    halo = ((1, NXA, HALO, 128), F32)
    state = {}
    for n, kind in enumerate("ua"):
        prev, now, sib, off = unpacked[4 * n : 4 * n + 4]
        state[kind] = [now, to_sibling(sib), to_off_chip(off), prev]
    history, mids, ends, totals = {}, {}, {}, {}
    for r in range(ROUNDS):
        for kind in "ua":
            later, last = r >= ROUNDS // 2, r == ROUNDS - 1
            args = [place_info] + ([pulse, pulse_depth] if kind == "u" else [traces, depth])
            args += state[kind] + [slow, aniso] + bands
            if later:
                partner = ROUNDS - 1 - r
                args += [mids[partner], ends[partner]] if kind == "u" else [history[partner]]
                if r > ROUNDS // 2:
                    args += [totals[kind]]
            outs = [own_shape, (EXT_SHAPE, F32)] + ([] if last else [halo, halo])
            if later:
                outs.append(((2, NXA, ZS, 128), F32))
            elif kind == "u":
                outs.append(((4, NXA, ZS, 128), F32))
            res = call(
                functools.partial(round_kernel, kind, r),
                outs,
                vmem(len(args)),
                round_scratch(),
                moved=4 * MIB,
                flops=1 << 24,
            )(*args)
            own, mid = res[0], res[1]
            if later:
                totals[kind] = res[-1]
            elif kind == "u":
                history[r] = res[-1]
            if kind == "a":
                mids[r], ends[r] = mid, own
            if last:
                state[kind] = [own]
            else:
                state[kind] = [own, to_sibling(res[2]), to_off_chip(res[3]), mid]

    final = call(
        pack_final, [((2, 4, ZS, 128), F32)] * 8, [SMEM] + vmem(2), moved=MIB, flops=1 << 20
    )(scal, state["u"][0], state["a"][0])
    final = [to_blocks(x, e) for x, e in zip(final, FAR_FIRST)]
    columns = call(
        pack_grads,
        [((8, 2 * ZS, 128), F32)] * 8,
        [SMEM] + vmem(4),
        [pltpu.VMEM((NXA, 2 * ZS, 128), F32)],
        moved=16 * MIB,
        flops=1 << 22,
    )(scal, index, totals["u"], totals["a"], coefs)
    index, _ = lax.optimization_barrier((index, columns[7]))
    (picks,) = call(name_slots, [((1024, 1024), BF16)], vmem(1), moved=4 * MIB, flops=1 << 22)(index)
    columns = [to_blocks(x, e) for x, e in zip(columns, FAR_FIRST)]
    u, a = call(
        finish_fields,
        [((BX, BY, BZ), F32)] * 2,
        [SMEM] + vmem(8),
        [pltpu.VMEM((8, 128, 128), F32)],
        moved=MIB,
        flops=1 << 20,
    )(scal, *final)
    (model,) = call(
        finish_model,
        [((2048, 128), F32)],
        [SMEM] + vmem(9),
        [pltpu.VMEM((256, 1024), F32)],
        moved=4 * MIB,
        flops=1 << 28,
    )(scal, picks, *columns)
    return (u, a, model.reshape(1, 1024, 2, 128))


def solution(mesh):
    in_specs = (
        P(("shots", "gx"), "gy", "gz"),
        P(("shots", "gx"), "gy", "gz"),
        P(("shots", "gx"), "gy", "gz"),
        P(("shots", "gx"), "gy", "gz"),
        P("gz", ("gx", "gy"), None, None),
        P(("shots", "gz"), "gx", "gy", None, None),
        P(("shots", "gz"), "gx", "gy", None),
        P("shots"),
        P("shots"),
        P(("shots", "gx"), "gy"),
        P(None, ("shots", "gx"), "gy"),
    )
    out_specs = (
        P(("shots", "gx"), "gy", "gz"),
        P(("shots", "gx"), "gy", "gz"),
        P("gz", ("shots", "gx", "gy"), None, None),
    )
    body = slab_body if slabs_fit(mesh) else block_body
    return jax.shard_map(body, mesh=mesh, in_specs=in_specs, out_specs=out_specs, check_vma=False)
```

```python
import functools

import jax
import jax.numpy as jnp
import numpy as np
from jax import lax
from jax.experimental import pallas as pl
from jax.experimental.pallas import tpu as pltpu
from jax.sharding import PartitionSpec as P

STENCIL = (-205.0 / 72.0, 8.0 / 5.0, -1.0 / 5.0, 8.0 / 315.0, -1.0 / 560.0)


def with_halo(block, sides, width):
    for axis, dim in sides:
        count = lax.axis_size(axis)
        forward = [(i, i + 1) for i in range(count - 1)]
        backward = [(target, source) for source, target in forward]
        low = lax.ppermute(
            lax.slice_in_dim(block, block.shape[dim] - width, None, axis=dim), axis, forward
        )
        high = lax.ppermute(lax.slice_in_dim(block, 0, width, axis=dim), axis, backward)
        block = jnp.concatenate([low, block, high], axis=dim)
    return block


def derivatives(padded, shape):
    size_x, size_y, size_z = shape

    def window(off_x, off_y, off_z):
        return padded[
            4 + off_x : 4 + off_x + size_x,
            4 + off_y : 4 + off_y + size_y,
            4 + off_z : 4 + off_z + size_z,
        ]

    center = window(0, 0, 0)
    along_x = STENCIL[0] * center
    along_y = STENCIL[0] * center
    along_z = STENCIL[0] * center
    for offset in range(1, 5):
        along_x = along_x + STENCIL[offset] * (window(offset, 0, 0) + window(-offset, 0, 0))
        along_y = along_y + STENCIL[offset] * (window(0, offset, 0) + window(0, -offset, 0))
        along_z = along_z + STENCIL[offset] * (window(0, 0, offset) + window(0, 0, -offset))
    return (along_x + along_y, along_z)


def propagate(previous, current, slow_coef, aniso_coef, padded):
    horizontal, vertical = derivatives(padded, current.shape)
    laplacian = (1.0 + 2.0 * aniso_coef) * horizontal + vertical
    following = 2.0 * current - previous + slow_coef * laplacian
    return (following, laplacian, horizontal)


def block_body(
    forward_prev,
    forward_now,
    adjoint_prev,
    adjoint_now,
    model_table,
    tile_owner,
    tile_slot,
    source_index,
    wavelet,
    receiver_depth,
    traces,
):
    block_x, block_y, block_z = forward_now.shape
    columns = block_x * block_y
    owners_count = lax.axis_size(("gx", "gy"))
    capacity = max(2, 2 * columns // owners_count)
    column_owner = tile_owner.reshape(columns)
    column_slot = tile_slot.reshape(columns)
    local_table = model_table[0]
    held_count = local_table.shape[0]
    one_hot = (column_owner[:, None] == jnp.arange(owners_count, dtype=jnp.int32)[None, :]).astype(
        jnp.float32
    )
    earlier = (
        jnp.arange(columns, dtype=jnp.int32)[:, None]
        > jnp.arange(columns, dtype=jnp.int32)[None, :]
    ).astype(jnp.float32)
    counted_before = jnp.dot(earlier, one_hot, precision=lax.Precision.HIGHEST)
    slot_rank = jnp.sum(counted_before * one_hot, axis=1).astype(jnp.int32)
    requests = (
        jnp.full((owners_count, capacity), -1, jnp.int32)
        .at[column_owner, slot_rank]
        .set(column_slot)
    )
    received = lax.all_to_all(requests, ("gx", "gy"), split_axis=0, concat_axis=0, tiled=True)
    clipped = jnp.clip(received, 0, held_count - 1)
    fetched = lax.all_to_all(
        local_table[clipped], ("gx", "gy"), split_axis=0, concat_axis=0, tiled=True
    )
    cell_params = (
        fetched[column_owner, slot_rank].reshape(block_x, block_y, 2, block_z).transpose(2, 0, 1, 3)
    )
    slow_coef = cell_params[0]
    aniso_coef = cell_params[1]
    grid_x = lax.axis_index("gx") * block_x + jnp.arange(block_x, dtype=jnp.int32)[:, None, None]
    grid_y = lax.axis_index("gy") * block_y + jnp.arange(block_y, dtype=jnp.int32)[None, :, None]
    grid_z = lax.axis_index("gz") * block_z + jnp.arange(block_z, dtype=jnp.int32)[None, None, :]
    source_mask = (
        (grid_x == source_index[0]) & (grid_y == source_index[1]) & (grid_z == source_index[2])
    ).astype(jnp.float32)
    receiver_mask = (grid_z == receiver_depth[:, :, None]).astype(jnp.float32)

    def forward(carried, weight):
        previous, current = carried
        padded = with_halo(current, (("gx", 0), ("gy", 1), ("gz", 2)), 4)
        following, laplacian, horizontal = propagate(
            previous, current, slow_coef, aniso_coef, padded
        )
        following = following + weight * source_mask
        return ((current, following), (laplacian, horizontal))

    (_, forward_final), (laplacians, horizontals) = lax.scan(
        forward, (forward_prev, forward_now), wavelet
    )

    def backward(carried, inputs):
        previous, current, grad_slow, grad_aniso = carried
        trace_row, laplacian, horizontal = inputs
        padded = with_halo(current, (("gx", 0), ("gy", 1), ("gz", 2)), 4)
        following, _, _ = propagate(previous, current, slow_coef, aniso_coef, padded)
        following = following + trace_row[:, :, None] * receiver_mask
        grad_slow = grad_slow + following * laplacian
        grad_aniso = grad_aniso + following * (2.0 * slow_coef * horizontal)
        return ((current, following, grad_slow, grad_aniso), None)

    zero_field = jnp.zeros((block_x, block_y, block_z), jnp.float32)
    (_, adjoint_final, grad_slow, grad_aniso), _ = lax.scan(
        backward,
        (adjoint_prev, adjoint_now, zero_field, zero_field),
        (traces[::-1], laplacians[::-1], horizontals[::-1]),
    )
    grad_cells = (
        jnp.stack([grad_slow, grad_aniso]).transpose(1, 2, 0, 3).reshape(columns, 2, block_z)
    )
    outgoing = (
        jnp.zeros((owners_count, capacity, 2, block_z), jnp.float32)
        .at[column_owner, slot_rank]
        .set(grad_cells)
    )
    returned = lax.all_to_all(outgoing, ("gx", "gy"), split_axis=0, concat_axis=0, tiled=True)
    target = jnp.where(received < 0, held_count, received).reshape(owners_count * capacity)
    model_gradient = (
        jnp.zeros((held_count, 2, block_z), jnp.float32)
        .at[target]
        .add(returned.reshape(owners_count * capacity, 2, block_z), mode="drop")
    )
    return (forward_final, adjoint_final, model_gradient[None])


BX, BY, BZ = 8, 64, 128
GX, GY = 4, 2
NXA, NYA = BX * GX, BY * GY
ZS = 16
ZE = 32
HALO = 8
OWN = slice(HALO, HALO + ZS)
SCALE = 5040.0
UNSCALE = 1.0 / SCALE
PADX = 4
EXT_SHAPE = (NXA + 2 * PADX, ZE, 128)
INNER = slice(PADX, PADX + NXA)
STEPS = 16
ROUNDS = STEPS // 2
MIB = 1 << 20
F32 = jnp.float32
BF16 = jnp.bfloat16
H, IX, IY, SHOT, LINE, SX, SY, SZ = range(8)


def slabs_fit(mesh):
    names = ("shots", "gx", "gy", "gz")
    return tuple(mesh.shape[n] for n in names) == (2, GX, GY, 2)


def line_device(place):
    chip, core = divmod(place, 2)
    ix, iy = (chip, 0) if chip < GX else (2 * GX - 1 - chip, 1)
    return (ix * GY + iy) * 2 + core


def off_chip_pairs():
    count = 2 * GX * GY
    pairs = []
    for low in range(1, count, 2):
        a, b = line_device(low), line_device((low + 1) % count)
        pairs += [(a, b), (b, a)]
    return pairs


OFF_PAIRS = off_chip_pairs()
SWAP = [(0, 1), (1, 0)]


def to_sibling(x):
    return lax.ppermute(x, "gz", SWAP)


def to_off_chip(x):
    return lax.ppermute(x, ("gx", "gy", "gz"), OFF_PAIRS)


def spread(e):
    return [(2 * s + c, 2 * (s ^ e ^ c) + (s & 1)) for s in range(GX * GY) for c in range(2)]


def to_blocks(x, e):
    return lax.ppermute(x, ("gx", "gy", "gz"), spread(e))


FAR_FIRST = (6, 7, 4, 5, 2, 3, 0, 1)


def slab_of(scal, e):
    ix = scal[IX] ^ (e >> 1)
    core = scal[IY] ^ (e & 1) ^ scal[H]
    chip = jnp.where(scal[H] == 0, ix, GX - 1 - ix)
    return pl.multiple_of(chip * 2 * ZS + core * ZS, ZS)


def block_of(scal, e):
    return (scal[IX] * GY + scal[IY]) ^ e ^ scal[H]


def band(size):
    out = np.zeros((size, size), np.float32)
    for offset in range(1, 5):
        value = round(STENCIL[offset] * SCALE)
        for i in range(size - offset):
            out[i, i + offset] = value
            out[i + offset, i] = value
    return out


def matrices():
    along_y = band(NYA)
    along_y = np.concatenate([along_y, along_y], 0)
    along_z = band(ZE)
    full = np.kron(np.eye(8, dtype=np.float32), along_z)
    own = np.kron(np.eye(8, dtype=np.float32), along_z[OWN])
    full, own = [np.concatenate([m, m], 1) for m in (full, own)]
    return [jnp.asarray(m, BF16) for m in (along_y, full, own)]


def vmem(count):
    return [pl.BlockSpec(memory_space=pltpu.VMEM)] * count


SMEM = pl.BlockSpec(memory_space=pltpu.SMEM)


def call(kernel, outs, specs, scratch=(), limit=24, flops=0, moved=0, aliases=None):
    return pl.pallas_call(
        kernel,
        out_shape=[jax.ShapeDtypeStruct(s, d) for s, d in outs],
        in_specs=specs,
        out_specs=vmem(len(outs)),
        scratch_shapes=list(scratch),
        input_output_aliases=aliases or {},
        compiler_params=pltpu.CompilerParams(vmem_limit_bytes=limit * MIB),
        cost_estimate=pl.CostEstimate(flops=flops, bytes_accessed=moved, transcendentals=0),
    )


def half_lanes(shape):
    return lax.broadcasted_iota(jnp.int32, shape, len(shape) - 1) < BY


def roll_half(x):
    return pltpu.roll(x, BY, x.ndim - 1)


def roll_tile(x):
    return pltpu.roll(x, HALO // 2, 0)


def place(scal, chunk):
    chip, core = divmod(chunk, 2)
    mine = core == scal[H]
    return mine, jnp.where(scal[H] == 0, chip, GX - 1 - chip)


def pack_small(owner, slot, depth, traces, out):
    for tt in range(4):
        out[tt] = jnp.concatenate([traces[2 * tt], traces[2 * tt + 1]], axis=1)
    low = half_lanes((1, 128))
    ids = owner[...] * 1024 + slot[...]
    rows = []
    for x in range(BX):
        pair = ids[:, (x // 2) * 128 : (x // 2 + 1) * 128].astype(F32)
        rows.append(roll_half(pair) if x % 2 else pair)
    rows = jnp.concatenate(rows, axis=0)
    depths = depth[...].astype(F32)
    depths = jnp.concatenate([depths, depths], axis=1)
    out[4] = jnp.where(half_lanes((8, 128)), rows, depths)


def pack_table(scal, table, keep, give):
    first = scal[SHOT] * 1024
    for q in range(4):
        for comp in range(2):
            turned = table[pl.ds(first + q * 256 + comp, 128, stride=2), :].T
            at = q * 32 + comp * ZS
            for chunk in range(8):
                mine, g = place(scal, chunk)
                piece = turned[chunk * ZS : (chunk + 1) * ZS][None]

                @pl.when(mine)
                def _():
                    keep[pl.ds(g, 1), at : at + ZS, :] = piece

                @pl.when(jnp.logical_not(mine))
                def _():
                    give[pl.ds(g, 1), at : at + ZS, :] = piece


def assemble(scal, keep, got, small, out):
    h = scal[H]
    for ix in range(GX):
        out[pl.ds(ix * GY + h, 1), 0:128, :] = keep[ix][None]
        out[pl.ds(ix * GY + 1 - h, 1), 0:128, :] = got[ix][None]
    for n in range(GX * GY):
        out[n, 128:, :] = small[...].reshape(40, 128)


def pack_fields(scal, *refs):
    fields, (keep, give) = refs[:4], refs[4:]
    for f in range(4):
        for i in range(4):
            pair = fields[f][2 * i : 2 * i + 2].reshape(128, 128)
            turned = pair.T
            for chunk in range(8):
                mine, g = place(scal, chunk)
                piece = turned[chunk * ZS : (chunk + 1) * ZS][None]

                @pl.when(mine)
                def _():
                    keep[pl.ds(g, 1), f, i] = piece

                @pl.when(jnp.logical_not(mine))
                def _():
                    give[pl.ds(g, 1), f, i] = piece


def unpack_small(scal, wavelet, mine, other, ids_slab, ids_owner, depth, traces, pulse, pulse_depth, place):
    low = half_lanes((8, 128))
    h = scal[H]
    x_at = lax.broadcasted_iota(jnp.int32, (NXA, 128), 0)
    y_at = lax.broadcasted_iota(jnp.int32, (NXA, 128), 1)
    at_source = (x_at == scal[SX]) & (y_at == scal[SY])
    for t in range(STEPS):
        pulse[t] = jnp.where(at_source, wavelet[t], 0.0)
    pulse_depth[...] = jnp.full((NXA, 128), scal[SZ], jnp.int32)
    place[0] = jnp.full((8, 128), h, jnp.int32)
    place[1] = jnp.full((8, 128), jnp.where(is_edge(scal), 1, 0), jnp.int32)
    place[2] = jnp.full((8, 128), scal[LINE] * ZS - HALO, jnp.int32)
    for ix in range(GX):
        rows = slice(ix * BX, (ix + 1) * BX)
        for ref, is_mine in ((mine, True), (other, False)):
            a, b = ref[ix * GY], ref[ix * GY + 1]
            core = h if is_mine else 1 - h
            for tt in range(4):
                even = jnp.where(low, a[tt], roll_half(b[tt]))
                odd = jnp.where(low, roll_half(a[tt]), b[tt])
                traces[pl.ds(core * 8 + 2 * tt, 1), rows, :] = even[None]
                traces[pl.ds(core * 8 + 2 * tt + 1, 1), rows, :] = odd[None]
            ids = jnp.where(low, a[4], roll_half(b[4])).astype(jnp.int32)
            if is_mine:
                ids_owner[rows, :] = ids
                depth[rows, :] = jnp.where(low, roll_half(a[4]), b[4]).astype(jnp.int32)

            @pl.when(core == scal[IY])
            def _():
                ids_slab[rows, :] = ids


def gather_half(second, scal, table, ids, *refs):
    if second:
        before, out, sib, off = refs
    else:
        (out,) = refs
    half = 1 - scal[SHOT] if second else scal[SHOT]

    def column(x, carry):
        row = ids[pl.ds(x, 1), :]
        lane = jnp.broadcast_to(row & 127, (8, 128))
        chunk = jnp.broadcast_to(row >> 7, (8, 128))
        if second:
            totals = [before[x, 8 * t : 8 * t + 8, :] for t in range(4)]
        else:
            totals = [jnp.zeros((8, 128), F32) for t in range(4)]
        for j in range(32):
            hit = chunk == (j // 4) * 8 + half * 4 + j % 4
            for t in range(4):
                value = jnp.take_along_axis(
                    table[j // 4, j % 4, 8 * t : 8 * t + 8, :], lane, axis=1, mode="promise_in_bounds"
                )
                totals[t] = jnp.where(hit, value, totals[t])
        for t in range(4):
            out[x, 8 * t : 8 * t + 8, :] = totals[t]
        return carry

    lax.fori_loop(0, NXA, column, 0)
    if second:
        h = scal[H]
        for comp in range(2):
            rows = slice(comp * HALO, (comp + 1) * HALO)
            sib[:, rows, :] = out[:, pl.ds(comp * ZS + HALO * (1 - h), HALO), :]
            off[:, rows, :] = out[:, pl.ds(comp * ZS + HALO * h, HALO), :]


def is_edge(scal):
    return (scal[LINE] == 0) | (scal[LINE] == 2 * GX * GY - 1)


def extend_coefs(scal, coefs, sib, off, slow, aniso):
    sib_at = (ZE - HALO) * (1 - scal[H])
    off_at = (ZE - HALO) * scal[H]
    inside = jnp.where(is_edge(scal), 0.0, 1.0)
    slow[:, OWN, :] = coefs[:, 0:ZS, :] * UNSCALE
    slow[:, pl.ds(sib_at, HALO), :] = sib[:, 0:HALO, :] * UNSCALE
    slow[:, pl.ds(off_at, HALO), :] = off[:, 0:HALO, :] * (inside * UNSCALE)
    aniso[:, OWN, :] = 1.0 + 2.0 * coefs[:, ZS:, :]
    aniso[:, pl.ds(sib_at, HALO), :] = 1.0 + 2.0 * sib[:, HALO:, :]
    aniso[:, pl.ds(off_at, HALO), :] = 1.0 + 2.0 * off[:, HALO:, :]


def unpack_fields(scal, got, *outs):
    low = half_lanes((ZS, 128))
    h = scal[H]
    for kind in range(2):
        prev, now, sib, off = outs[4 * kind : 4 * kind + 4]
        for step, own in ((0, prev), (1, now)):
            f = 2 * kind + step
            for ix in range(GX):
                for i in range(4):
                    a, b = got[ix * GY, f, i], got[ix * GY + 1, f, i]
                    x = ix * BX + 2 * i
                    own[x] = jnp.where(low, a, roll_half(b))
                    own[x + 1] = jnp.where(low, roll_half(a), b)
        sib[0:NXA] = now[:, pl.ds(HALO * (1 - h), HALO), :]
        off[0:NXA] = now[:, pl.ds(HALO * h, HALO), :]
        upper = lax.broadcasted_iota(jnp.int32, (HALO, 128), 0) < HALO // 2
        for x in range(NXA // 2):
            one, two = prev[x], prev[x + NXA // 2]
            start = jnp.where(upper, one[:HALO], roll_tile(two[:HALO]))
            end = jnp.where(upper, roll_tile(one[HALO:]), two[HALO:])
            sib[NXA + x] = jnp.where(h == 0, end, start)
            off[NXA + x] = jnp.where(h == 0, start, end)


def index_kernel(scal, ids_slab, ids_owner, out):
    me = scal[IX] * GY + scal[IY]
    sub = lax.broadcasted_iota(jnp.int32, (8, 128), 0)
    lane = lax.broadcasted_iota(jnp.int32, (8, 128), 1)
    slots = []
    masks = [(jnp.broadcast_to(ids_slab[x : x + 1, :] >> 10, (8, 128)) == sub).astype(F32) for x in range(NXA)]
    for x in range(BX):
        rows = jnp.concatenate([ids_owner[s * BX + x : s * BX + x + 1, :] for s in range(GX)] * 2, axis=0)
        masks.append((((rows >> 10) == me) & (sub < GX)).astype(F32))
        slots.append((rows & 1023).astype(F32))
    bits = jnp.concatenate(masks, axis=0).astype(BF16)
    first = lax.broadcasted_iota(jnp.int32, (128, 128), 0)
    second = lax.broadcasted_iota(jnp.int32, (128, 128), 1)
    upto = (first <= second).astype(F32).astype(BF16)
    along = jnp.dot(bits, upto, preferred_element_type=F32)
    sums = jnp.dot(bits, jnp.ones((128, 128), BF16), preferred_element_type=F32)
    r0 = lax.broadcasted_iota(jnp.int32, (64, 64), 0)
    r1 = lax.broadcasted_iota(jnp.int32, (64, 64), 1)
    earlier = (((r0 & 7) == (r1 & 7)) & (r1 < r0)).astype(F32).astype(BF16)
    for group in range(GX + 1):
        rows = slice(64 * group, 64 * group + 64)
        above = jnp.dot(earlier, sums[rows].astype(BF16), preferred_element_type=F32)
        counts = along[rows] + above
        ends = sums[rows] + above
        for part in range(2):
            r = (lane + 128 * part).astype(F32)
            at_x = jnp.zeros((8, 128), jnp.int32)
            for x in range(BX):
                at_x = at_x + (ends[8 * x : 8 * x + 8] <= r).astype(jnp.int32)

            def pick(tables, at):
                value = jnp.zeros((8, 128), F32)
                for x in range(BX):
                    taken = jnp.take_along_axis(tables[x], at, axis=1, mode="promise_in_bounds")
                    value = jnp.where(at_x == x, taken, value)
                return value

            tables = [counts[8 * x : 8 * x + 8] for x in range(BX)]
            at_y = jnp.zeros((8, 128), jnp.int32)
            for step in (64, 32, 16, 8, 4, 2, 1):
                at_y = jnp.where(pick(tables, at_y + (step - 1)) <= r, at_y + step, at_y)
            at_y = jnp.minimum(at_y, 127)
            if group < GX:
                found = at_x * 128 + at_y
            else:
                found = pick(slots, at_y).astype(jnp.int32)
            out[part, 8 * group : 8 * group + 8] = jnp.where(at_x < BX, found, -1)


def bands_of(field, g, along_y, along_z, own):
    first = PADX + 8 * g
    depth = ZS if own else ZE
    whole = field[first : first + 8].reshape(8 * ZE, 128)
    high = whole.astype(BF16)
    rest = (whole - high.astype(F32)).astype(BF16)
    my = jnp.dot(jnp.concatenate([high, rest], axis=1), along_y[...], preferred_element_type=F32)
    mz = jnp.dot(along_z[...], jnp.concatenate([high, rest], axis=0), preferred_element_type=F32)
    return my.reshape(8, ZE, 128), mz.reshape(8, depth, 128)


def round_scratch():
    return [pltpu.VMEM(EXT_SHAPE, F32)]


def round_kernel(kind, r, *refs):
    refs = list(refs)
    take = lambda n: [refs.pop(0) for _ in range(n)]
    first, later, last = r == 0, r >= ROUNDS // 2, r == ROUNDS - 1
    place, drive, depth, own, sib, off, prev, slow, aniso, along_y, along_z, along_z_own = take(12)
    if later:
        if kind == "u":
            partner_mid, partner_end = take(2)
        else:
            (partner,) = take(1)
        if r > ROUNDS // 2:
            (total_in,) = take(1)
    out_own, out_mid = take(2)
    if not last:
        out_sib, out_off = take(2)
    if later:
        (total,) = take(1)
    elif kind == "u":
        (history,) = take(1)
    (e0,) = take(1)
    e1 = out_mid

    core_0 = place[0] == 0
    inside = place[1] == 0
    zero = jnp.zeros((PADX, ZE, 128), F32)
    for e in (e0, e1):
        e[0:PADX] = zero
        e[PADX + NXA :] = zero

    def extend(e, own, shared):
        for x in range(NXA):
            at = NXA + x % (NXA // 2) if shared else x
            near, far = sib[at], jnp.where(inside, off[at], 0.0)
            low, high = jnp.where(core_0, far, near), jnp.where(core_0, near, far)
            if shared and x < NXA // 2:
                low = roll_tile(low)
            elif shared:
                high = roll_tile(high)
            e[PADX + x, 0:HALO] = low
            e[PADX + x, OWN] = own[x]
            e[PADX + x, HALO + ZS :] = high

    extend(e0, own, False)
    if first:
        extend(e1, prev, True)
        prev = e1
    base = jnp.concatenate([place[2]] * (ZE // 8), axis=0) + lax.broadcasted_iota(jnp.int32, (ZE, 128), 0)

    def bands(step, g):
        if step:
            return bands_of(e1, g, along_y, along_z_own, True)
        return bands_of(e0, g, along_y, along_z, False)

    items = [(step, g) for step in range(2) for g in range(4)]
    ahead = bands(*items[0])
    for k, (step, g) in enumerate(items):
        my, mz = ahead
        if k + 1 < len(items):
            ahead = bands(*items[k + 1])
        t = 2 * r + step if kind == "u" else STEPS - 1 - (2 * r + step)
        field = e1 if step else e0
        zs = OWN if step else slice(0, ZE)
        count = ZS if step else ZE
        z = base[zs]
        for n in range(8):
            x = 8 * g + n
            at = PADX + x
            center = field[at, zs, :]
            hor = my[n, zs] + (2.0 * SCALE * STENCIL[0]) * center
            for i in range(1, 5):
                hor = hor + (SCALE * STENCIL[i]) * (field[at + i, zs, :] + field[at - i, zs, :])
            ver = mz[n] + (SCALE * STENCIL[0]) * center
            before = e0[at, OWN, :] if step else prev[at]
            lap = aniso[x, zs, :] * hor + ver
            following = 2.0 * center - before + slow[x, zs, :] * lap
            at_z = jnp.broadcast_to(depth[x : x + 1, :], (count, 128))
            value = jnp.broadcast_to(drive[t, x : x + 1, :], (count, 128))
            following = following + jnp.where(z == at_z, value, 0.0)
            if step:
                out_own[x] = following
                if not last:
                    low, high = following[:HALO], following[HALO:]
                    out_sib[x] = jnp.where(core_0, high, low)
                    out_off[x] = jnp.where(core_0, low, high)
            else:
                e1[at] = following
                hor, ver = hor[OWN], ver[OWN]
            if kind == "u" and not later:
                history[2 * step, x] = hor
                history[2 * step + 1, x] = ver
            if later:
                if kind == "u":
                    other = partner_mid[at, OWN, :] if step else partner_end[x]
                else:
                    other = following if step else following[OWN]
                    hor = partner[2 * (1 - step), x]
                    ver = partner[2 * (1 - step) + 1, x]
                sum_h, sum_v = other * hor, other * ver
                if step:
                    sum_h, sum_v = total[0, x] + sum_h, total[1, x] + sum_v
                elif r > ROUNDS // 2:
                    sum_h, sum_v = total_in[0, x] + sum_h, total_in[1, x] + sum_v
                total[0, x] = sum_h
                total[1, x] = sum_v


def pack_final(scal, u, a, *outs):
    low = half_lanes((ZS, 128))
    for n, out in enumerate(outs):
        block = block_of(scal, FAR_FIRST[n])
        for f, field in enumerate((u, a)):
            for i in range(4):
                x = (block >> 1) * BX + 2 * i
                x0 = field[pl.ds(x, 1)].reshape(ZS, 128)
                x1 = field[pl.ds(x + 1, 1)].reshape(ZS, 128)
                piece = jnp.where(low, x0, roll_half(x1))
                upper = jnp.where(low, roll_half(x0), x1)
                out[f, i] = jnp.where((block & 1) == 0, piece, upper)


def pack_grads(scal, index, total_u, total_a, coefs, *refs):
    outs, grads = refs[:8], refs[8]
    for x in range(NXA):
        gh = (total_u[0, x] + total_a[0, x]) * UNSCALE
        gv = (total_u[1, x] + total_a[1, x]) * UNSCALE
        slow, aniso = coefs[x, 0:ZS, :], coefs[x, ZS:, :]
        grads[x, 0:ZS, :] = (1.0 + 2.0 * aniso) * gh + gv
        grads[x, ZS:, :] = (2.0 * slow) * gh
    for n, out in enumerate(outs):
        block = block_of(scal, FAR_FIRST[n])

        def stripe(ix, carry, out=out, block=block):
            for part in range(2):
                row = index[part, pl.ds(ix * 8 + block, 1), :]
                lane = jnp.broadcast_to(row & 127, (8, 128))
                which = jnp.broadcast_to(row >> 7, (8, 128))
                totals = [jnp.zeros((8, 128), F32) for t in range(4)]
                for x in range(BX):
                    hit = which == x
                    for t in range(4):
                        value = jnp.take_along_axis(
                            grads[ix * BX + x, 8 * t : 8 * t + 8, :], lane, axis=1, mode="promise_in_bounds"
                        )
                        totals[t] = jnp.where(hit, value, totals[t])
                for t in range(4):
                    out[ix * 2 + part, 8 * t : 8 * t + 8, :] = totals[t]
            return carry

        lax.fori_loop(0, GX, stripe, 0)


def name_slots(index, picks):
    named = jnp.concatenate([index[n % 2, 32 + n // 2 : 33 + n // 2, :] for n in range(8)], axis=1)
    for block in range(4):
        slot = lax.broadcasted_iota(jnp.int32, (256, 1024), 0) + block * 256
        pick = slot == jnp.broadcast_to(named, (256, 1024))
        picks[block * 256 : (block + 1) * 256, :] = pick.astype(F32).astype(BF16)


def finish_fields(scal, *refs):
    gots, (u_out, a_out, turned) = refs[:8], refs[8:]
    for f, out in enumerate((u_out, a_out)):
        for i in range(4):
            for n, e in enumerate(FAR_FIRST):
                turned[f * 4 + i, pl.ds(slab_of(scal, e), ZS), :] = gots[n][f, i]
            out[2 * i : 2 * i + 2] = turned[f * 4 + i].T.reshape(2, BY, 128)


def finish_model(scal, picks, *refs):
    gots, (out, columns, model, sems) = refs[:8], refs[8:]
    for n, e in enumerate(FAR_FIRST):
        for comp in range(2):
            rows = pl.ds(pl.multiple_of(comp * 128 + slab_of(scal, e), ZS), ZS)
            for m in range(8):
                columns[rows, m * 128 : (m + 1) * 128] = gots[n][m, comp * ZS : (comp + 1) * ZS, :]
    values = columns[...].T
    high = values.astype(BF16)
    rest = (values - high.astype(F32)).astype(BF16)
    both = jnp.concatenate([high, rest], axis=1)
    copies = []
    for block in range(4):
        sums = jnp.dot(picks[block * 256 : (block + 1) * 256, :], both, preferred_element_type=F32)
        sums = sums[:, :256] + sums[:, 256:]
        for comp in range(2):
            model[pl.ds(block * 512 + comp, 256, stride=2), :] = sums[:, comp * 128 : (comp + 1) * 128]
        rows = pl.ds(block * 512, 512)
        copies.append(pltpu.make_async_copy(model.at[rows], out.at[rows], sems.at[block]))
        copies[-1].start()
    for copy in copies:
        copy.wait()


def by_half(h, mine, other):
    first = jnp.where(h == 0, mine, other)
    second = jnp.where(h == 0, other, mine)
    both = jnp.stack([first, second], axis=1)
    return both.reshape((GX * GY,) + mine.shape[1:])


def exchange(x):
    return lax.all_to_all(x, ("gx", "gy"), split_axis=0, concat_axis=0, tiled=True)


def slab_body(
    forward_prev,
    forward_now,
    adjoint_prev,
    adjoint_now,
    model_table,
    tile_owner,
    tile_slot,
    source_index,
    wavelet,
    receiver_depth,
    traces,
):
    h = lax.axis_index("gz")
    ix, iy = lax.axis_index("gx"), lax.axis_index("gy")
    chip = jnp.where(iy == 0, ix, 2 * GX - 1 - ix)
    line = 2 * chip + h
    scal = jnp.stack(
        [h, ix, iy, lax.axis_index("shots"), line, source_index[0], source_index[1], source_index[2]]
    ).astype(jnp.int32)

    trace_half = lax.dynamic_slice_in_dim(traces, h * 8, 8, axis=0)
    (small,) = call(pack_small, [((5, BX, 128), F32)], vmem(4), moved=MIB // 16, flops=1 << 16)(
        tile_owner.reshape(1, BX * BY), tile_slot.reshape(1, BX * BY), receiver_depth, trace_half
    )
    keep, give = call(
        pack_table, [((GX, 128, 128), F32)] * 2, [SMEM] + vmem(1), moved=2 * MIB, flops=1 << 20
    )(scal, model_table.reshape(2048, 128))
    (sent,) = call(assemble, [((GX * GY, 168, 128), F32)], [SMEM] + vmem(3), moved=2 * MIB, flops=1 << 20)(
        scal, keep, to_sibling(give), small
    )
    arrived = exchange(sent)
    table_mine = arrived[:, :128].reshape(8, 4, 32, 128)
    small_mine = arrived[:, 128:].reshape(8, 5, BX, 128)
    table_other = lax.ppermute(table_mine, "shots", SWAP)
    small_other = to_sibling(small_mine)

    keep, give = call(
        pack_fields, [((4, 4, 4, ZS, 128), F32)] * 2, [SMEM] + vmem(4), moved=2 * MIB, flops=1 << 20
    )(scal, forward_prev, forward_now, adjoint_prev, adjoint_now)
    fields = exchange(by_half(h, keep, to_sibling(give)))

    plane, drive = ((NXA, 128), jnp.int32), ((STEPS, NXA, 128), F32)
    ids_slab, ids_owner, depth, traces, pulse, pulse_depth, place_info = call(
        unpack_small,
        [plane] * 3 + [drive, drive, plane, ((3, 8, 128), jnp.int32)],
        [SMEM] * 2 + vmem(2),
        moved=MIB // 2,
        flops=1 << 20,
    )(scal, wavelet, small_mine, small_other)
    coef_shape = ((NXA, 2 * ZS, 128), F32)
    half_shape = ((NXA, 2 * HALO, 128), F32)
    (coefs,) = call(
        functools.partial(gather_half, False), [coef_shape], [SMEM] + vmem(2), moved=MIB, flops=1 << 24
    )(scal, table_mine, ids_slab)
    coefs, coefs_sib, coefs_off = call(
        functools.partial(gather_half, True),
        [coef_shape, half_shape, half_shape],
        [SMEM] + vmem(3),
        moved=2 * MIB,
        flops=1 << 24,
    )(scal, table_other, ids_slab, coefs)
    ext_shape = ((NXA, ZE, 128), F32)
    own_shape = ((NXA, ZS, 128), F32)
    slow, aniso = call(extend_coefs, [ext_shape] * 2, [SMEM] + vmem(3), moved=2 * MIB, flops=1 << 20)(
        scal, coefs, to_sibling(coefs_sib), to_off_chip(coefs_off)
    )
    (index,) = call(
        index_kernel,
        [((2, 40, 128), jnp.int32)],
        [SMEM] + vmem(2),
        moved=MIB // 4,
        flops=1 << 24,
    )(scal, ids_slab, ids_owner)

    fields, index = lax.optimization_barrier((fields, index))
    first_halo = ((NXA + NXA // 2, HALO, 128), F32)
    unpacked = call(
        unpack_fields,
        [own_shape, own_shape, first_halo, first_halo] * 2,
        [SMEM] + vmem(1),
        moved=4 * MIB,
        flops=1 << 20,
    )(scal, fields)
    bands = matrices()
    halo = ((NXA, HALO, 128), F32)
    state = {}
    for n, kind in enumerate("ua"):
        prev, now, sib, off = unpacked[4 * n : 4 * n + 4]
        state[kind] = [now, to_sibling(sib), to_off_chip(off), prev]
    history, mids, ends, totals = {}, {}, {}, {}
    for r in range(ROUNDS):
        for kind in "ua":
            later, last = r >= ROUNDS // 2, r == ROUNDS - 1
            args = [place_info] + ([pulse, pulse_depth] if kind == "u" else [traces, depth])
            args += state[kind] + [slow, aniso] + bands
            if later:
                partner = ROUNDS - 1 - r
                args += [mids[partner], ends[partner]] if kind == "u" else [history[partner]]
                if r > ROUNDS // 2:
                    args += [totals[kind]]
            outs = [own_shape, (EXT_SHAPE, F32)] + ([] if last else [halo, halo])
            if later:
                outs.append(((2, NXA, ZS, 128), F32))
            elif kind == "u":
                outs.append(((4, NXA, ZS, 128), F32))
            res = call(
                functools.partial(round_kernel, kind, r),
                outs,
                vmem(len(args)),
                round_scratch(),
                moved=4 * MIB,
                flops=1 << 24,
            )(*args)
            own, mid = res[0], res[1]
            if later:
                totals[kind] = res[-1]
            elif kind == "u":
                history[r] = res[-1]
            if kind == "a":
                mids[r], ends[r] = mid, own
            if last:
                state[kind] = [own]
            else:
                state[kind] = [own, to_sibling(res[2]), to_off_chip(res[3]), mid]

    final = call(
        pack_final, [((2, 4, ZS, 128), F32)] * 8, [SMEM] + vmem(2), moved=MIB, flops=1 << 20
    )(scal, state["u"][0], state["a"][0])
    final = [to_blocks(x, e) for x, e in zip(final, FAR_FIRST)]
    columns = call(
        pack_grads,
        [((8, 2 * ZS, 128), F32)] * 8,
        [SMEM] + vmem(4),
        [pltpu.VMEM((NXA, 2 * ZS, 128), F32)],
        moved=16 * MIB,
        flops=1 << 22,
    )(scal, index, totals["u"], totals["a"], coefs)
    index, _ = lax.optimization_barrier((index, columns[7]))
    (picks,) = call(name_slots, [((1024, 1024), BF16)], vmem(1), moved=4 * MIB, flops=1 << 22)(index)
    columns = [to_blocks(x, e) for x, e in zip(columns, FAR_FIRST)]
    u, a = call(
        finish_fields,
        [((BX, BY, BZ), F32)] * 2,
        [SMEM] + vmem(8),
        [pltpu.VMEM((8, 128, 128), F32)],
        moved=MIB,
        flops=1 << 20,
    )(scal, *final)
    model = pl.pallas_call(
        finish_model,
        out_shape=jax.ShapeDtypeStruct((2048, 128), F32),
        in_specs=[SMEM] + vmem(9),
        out_specs=pl.BlockSpec(memory_space=pl.ANY),
        scratch_shapes=[
            pltpu.VMEM((256, 1024), F32),
            pltpu.VMEM((2048, 128), F32),
            pltpu.SemaphoreType.DMA((4,)),
        ],
        compiler_params=pltpu.CompilerParams(vmem_limit_bytes=24 * MIB),
        cost_estimate=pl.CostEstimate(flops=1 << 28, bytes_accessed=4 * MIB, transcendentals=0),
    )(scal, picks, *columns)
    return (u, a, model.reshape(1, 1024, 2, 128))


def solution(mesh):
    in_specs = (
        P(("shots", "gx"), "gy", "gz"),
        P(("shots", "gx"), "gy", "gz"),
        P(("shots", "gx"), "gy", "gz"),
        P(("shots", "gx"), "gy", "gz"),
        P("gz", ("gx", "gy"), None, None),
        P(("shots", "gz"), "gx", "gy", None, None),
        P(("shots", "gz"), "gx", "gy", None),
        P("shots"),
        P("shots"),
        P(("shots", "gx"), "gy"),
        P(None, ("shots", "gx"), "gy"),
    )
    out_specs = (
        P(("shots", "gx"), "gy", "gz"),
        P(("shots", "gx"), "gy", "gz"),
        P("gz", ("shots", "gx", "gy"), None, None),
    )
    body = slab_body if slabs_fit(mesh) else block_body
    return jax.shard_map(body, mesh=mesh, in_specs=in_specs, out_specs=out_specs, check_vma=False)
```

```python
import functools

import jax
import jax.numpy as jnp
import numpy as np
from jax import lax
from jax.experimental import pallas as pl
from jax.experimental.pallas import tpu as pltpu
from jax.sharding import PartitionSpec as P

STENCIL = (-205.0 / 72.0, 8.0 / 5.0, -1.0 / 5.0, 8.0 / 315.0, -1.0 / 560.0)


def with_halo(block, sides, width):
    for axis, dim in sides:
        count = lax.axis_size(axis)
        forward = [(i, i + 1) for i in range(count - 1)]
        backward = [(target, source) for source, target in forward]
        low = lax.ppermute(
            lax.slice_in_dim(block, block.shape[dim] - width, None, axis=dim), axis, forward
        )
        high = lax.ppermute(lax.slice_in_dim(block, 0, width, axis=dim), axis, backward)
        block = jnp.concatenate([low, block, high], axis=dim)
    return block


def derivatives(padded, shape):
    size_x, size_y, size_z = shape

    def window(off_x, off_y, off_z):
        return padded[
            4 + off_x : 4 + off_x + size_x,
            4 + off_y : 4 + off_y + size_y,
            4 + off_z : 4 + off_z + size_z,
        ]

    center = window(0, 0, 0)
    along_x = STENCIL[0] * center
    along_y = STENCIL[0] * center
    along_z = STENCIL[0] * center
    for offset in range(1, 5):
        along_x = along_x + STENCIL[offset] * (window(offset, 0, 0) + window(-offset, 0, 0))
        along_y = along_y + STENCIL[offset] * (window(0, offset, 0) + window(0, -offset, 0))
        along_z = along_z + STENCIL[offset] * (window(0, 0, offset) + window(0, 0, -offset))
    return (along_x + along_y, along_z)


def propagate(previous, current, slow_coef, aniso_coef, padded):
    horizontal, vertical = derivatives(padded, current.shape)
    laplacian = (1.0 + 2.0 * aniso_coef) * horizontal + vertical
    following = 2.0 * current - previous + slow_coef * laplacian
    return (following, laplacian, horizontal)


def block_body(
    forward_prev,
    forward_now,
    adjoint_prev,
    adjoint_now,
    model_table,
    tile_owner,
    tile_slot,
    source_index,
    wavelet,
    receiver_depth,
    traces,
):
    block_x, block_y, block_z = forward_now.shape
    columns = block_x * block_y
    owners_count = lax.axis_size(("gx", "gy"))
    capacity = max(2, 2 * columns // owners_count)
    column_owner = tile_owner.reshape(columns)
    column_slot = tile_slot.reshape(columns)
    local_table = model_table[0]
    held_count = local_table.shape[0]
    one_hot = (column_owner[:, None] == jnp.arange(owners_count, dtype=jnp.int32)[None, :]).astype(
        jnp.float32
    )
    earlier = (
        jnp.arange(columns, dtype=jnp.int32)[:, None]
        > jnp.arange(columns, dtype=jnp.int32)[None, :]
    ).astype(jnp.float32)
    counted_before = jnp.dot(earlier, one_hot, precision=lax.Precision.HIGHEST)
    slot_rank = jnp.sum(counted_before * one_hot, axis=1).astype(jnp.int32)
    requests = (
        jnp.full((owners_count, capacity), -1, jnp.int32)
        .at[column_owner, slot_rank]
        .set(column_slot)
    )
    received = lax.all_to_all(requests, ("gx", "gy"), split_axis=0, concat_axis=0, tiled=True)
    clipped = jnp.clip(received, 0, held_count - 1)
    fetched = lax.all_to_all(
        local_table[clipped], ("gx", "gy"), split_axis=0, concat_axis=0, tiled=True
    )
    cell_params = (
        fetched[column_owner, slot_rank].reshape(block_x, block_y, 2, block_z).transpose(2, 0, 1, 3)
    )
    slow_coef = cell_params[0]
    aniso_coef = cell_params[1]
    grid_x = lax.axis_index("gx") * block_x + jnp.arange(block_x, dtype=jnp.int32)[:, None, None]
    grid_y = lax.axis_index("gy") * block_y + jnp.arange(block_y, dtype=jnp.int32)[None, :, None]
    grid_z = lax.axis_index("gz") * block_z + jnp.arange(block_z, dtype=jnp.int32)[None, None, :]
    source_mask = (
        (grid_x == source_index[0]) & (grid_y == source_index[1]) & (grid_z == source_index[2])
    ).astype(jnp.float32)
    receiver_mask = (grid_z == receiver_depth[:, :, None]).astype(jnp.float32)

    def forward(carried, weight):
        previous, current = carried
        padded = with_halo(current, (("gx", 0), ("gy", 1), ("gz", 2)), 4)
        following, laplacian, horizontal = propagate(
            previous, current, slow_coef, aniso_coef, padded
        )
        following = following + weight * source_mask
        return ((current, following), (laplacian, horizontal))

    (_, forward_final), (laplacians, horizontals) = lax.scan(
        forward, (forward_prev, forward_now), wavelet
    )

    def backward(carried, inputs):
        previous, current, grad_slow, grad_aniso = carried
        trace_row, laplacian, horizontal = inputs
        padded = with_halo(current, (("gx", 0), ("gy", 1), ("gz", 2)), 4)
        following, _, _ = propagate(previous, current, slow_coef, aniso_coef, padded)
        following = following + trace_row[:, :, None] * receiver_mask
        grad_slow = grad_slow + following * laplacian
        grad_aniso = grad_aniso + following * (2.0 * slow_coef * horizontal)
        return ((current, following, grad_slow, grad_aniso), None)

    zero_field = jnp.zeros((block_x, block_y, block_z), jnp.float32)
    (_, adjoint_final, grad_slow, grad_aniso), _ = lax.scan(
        backward,
        (adjoint_prev, adjoint_now, zero_field, zero_field),
        (traces[::-1], laplacians[::-1], horizontals[::-1]),
    )
    grad_cells = (
        jnp.stack([grad_slow, grad_aniso]).transpose(1, 2, 0, 3).reshape(columns, 2, block_z)
    )
    outgoing = (
        jnp.zeros((owners_count, capacity, 2, block_z), jnp.float32)
        .at[column_owner, slot_rank]
        .set(grad_cells)
    )
    returned = lax.all_to_all(outgoing, ("gx", "gy"), split_axis=0, concat_axis=0, tiled=True)
    target = jnp.where(received < 0, held_count, received).reshape(owners_count * capacity)
    model_gradient = (
        jnp.zeros((held_count, 2, block_z), jnp.float32)
        .at[target]
        .add(returned.reshape(owners_count * capacity, 2, block_z), mode="drop")
    )
    return (forward_final, adjoint_final, model_gradient[None])


BX, BY, BZ = 8, 64, 128
GX, GY = 4, 2
NXA, NYA = BX * GX, BY * GY
ZS = 16
ZE = 32
HALO = 8
OWN = slice(HALO, HALO + ZS)
SCALE = 5040.0
UNSCALE = 1.0 / SCALE
PADX = 4
EXT_SHAPE = (NXA + 2 * PADX, ZE, 128)
INNER = slice(PADX, PADX + NXA)
STEPS = 16
ROUNDS = STEPS // 2
MIB = 1 << 20
F32 = jnp.float32
BF16 = jnp.bfloat16
H, IX, IY, SHOT, LINE, SX, SY, SZ = range(8)


def slabs_fit(mesh):
    names = ("shots", "gx", "gy", "gz")
    return tuple(mesh.shape[n] for n in names) == (2, GX, GY, 2)


def line_device(place):
    chip, core = divmod(place, 2)
    ix, iy = (chip, 0) if chip < GX else (2 * GX - 1 - chip, 1)
    return (ix * GY + iy) * 2 + core


def off_chip_pairs():
    count = 2 * GX * GY
    pairs = []
    for low in range(1, count, 2):
        a, b = line_device(low), line_device((low + 1) % count)
        pairs += [(a, b), (b, a)]
    return pairs


OFF_PAIRS = off_chip_pairs()
SWAP = [(0, 1), (1, 0)]


def to_sibling(x):
    return lax.ppermute(x, "gz", SWAP)


def to_off_chip(x):
    return lax.ppermute(x, ("gx", "gy", "gz"), OFF_PAIRS)


def spread(e):
    return [(2 * s + c, 2 * (s ^ e ^ c) + (s & 1)) for s in range(GX * GY) for c in range(2)]


def to_blocks(x, e):
    return lax.ppermute(x, ("gx", "gy", "gz"), spread(e))


FAR_FIRST = (6, 7, 4, 5, 2, 3, 0, 1)


def slab_of(scal, e):
    ix = scal[IX] ^ (e >> 1)
    core = scal[IY] ^ (e & 1) ^ scal[H]
    chip = jnp.where(scal[H] == 0, ix, GX - 1 - ix)
    return pl.multiple_of(chip * 2 * ZS + core * ZS, ZS)


def block_of(scal, e):
    return (scal[IX] * GY + scal[IY]) ^ e ^ scal[H]


def band(size):
    out = np.zeros((size, size), np.float32)
    for offset in range(1, 5):
        value = round(STENCIL[offset] * SCALE)
        for i in range(size - offset):
            out[i, i + offset] = value
            out[i + offset, i] = value
    return out


def matrices():
    along_y = band(NYA)
    along_y = np.concatenate([along_y, along_y], 0)
    along_z = band(ZE)
    full = np.kron(np.eye(8, dtype=np.float32), along_z)
    own = np.kron(np.eye(8, dtype=np.float32), along_z[OWN])
    full, own = [np.concatenate([m, m], 1) for m in (full, own)]
    return [jnp.asarray(m, BF16) for m in (along_y, full, own)]


def vmem(count):
    return [pl.BlockSpec(memory_space=pltpu.VMEM)] * count


SMEM = pl.BlockSpec(memory_space=pltpu.SMEM)


def call(kernel, outs, specs, scratch=(), limit=24, flops=0, moved=0, aliases=None):
    return pl.pallas_call(
        kernel,
        out_shape=[jax.ShapeDtypeStruct(s, d) for s, d in outs],
        in_specs=specs,
        out_specs=vmem(len(outs)),
        scratch_shapes=list(scratch),
        input_output_aliases=aliases or {},
        compiler_params=pltpu.CompilerParams(vmem_limit_bytes=limit * MIB),
        cost_estimate=pl.CostEstimate(flops=flops, bytes_accessed=moved, transcendentals=0),
    )


def half_lanes(shape):
    return lax.broadcasted_iota(jnp.int32, shape, len(shape) - 1) < BY


def roll_half(x):
    return pltpu.roll(x, BY, x.ndim - 1)


def roll_tile(x):
    return pltpu.roll(x, HALO // 2, 0)


def place(scal, chunk):
    chip, core = divmod(chunk, 2)
    mine = core == scal[H]
    return mine, jnp.where(scal[H] == 0, chip, GX - 1 - chip)


def pack_small(owner, slot, depth, traces, out):
    for tt in range(4):
        out[tt] = jnp.concatenate([traces[2 * tt], traces[2 * tt + 1]], axis=1)
    low = half_lanes((1, 128))
    ids = owner[...] * 1024 + slot[...]
    rows = []
    for x in range(BX):
        pair = ids[:, (x // 2) * 128 : (x // 2 + 1) * 128].astype(F32)
        rows.append(roll_half(pair) if x % 2 else pair)
    rows = jnp.concatenate(rows, axis=0)
    depths = depth[...].astype(F32)
    depths = jnp.concatenate([depths, depths], axis=1)
    out[4] = jnp.where(half_lanes((8, 128)), rows, depths)


def pack_table(scal, table, keep, give):
    first = scal[SHOT] * 1024
    for q in range(4):
        for comp in range(2):
            turned = table[pl.ds(first + q * 256 + comp, 128, stride=2), :].T
            at = q * 32 + comp * ZS
            for chunk in range(8):
                mine, g = place(scal, chunk)
                piece = turned[chunk * ZS : (chunk + 1) * ZS][None]

                @pl.when(mine)
                def _():
                    keep[pl.ds(g, 1), at : at + ZS, :] = piece

                @pl.when(jnp.logical_not(mine))
                def _():
                    give[pl.ds(g, 1), at : at + ZS, :] = piece


def assemble(scal, keep, got, small, out):
    h = scal[H]
    for ix in range(GX):
        out[pl.ds(ix * GY + h, 1), 0:128, :] = keep[ix][None]
        out[pl.ds(ix * GY + 1 - h, 1), 0:128, :] = got[ix][None]
    for n in range(GX * GY):
        out[n, 128:, :] = small[...].reshape(40, 128)


def pack_fields(scal, *refs):
    fields, (keep, give) = refs[:4], refs[4:]
    for f in range(4):
        for i in range(4):
            pair = fields[f][2 * i : 2 * i + 2].reshape(128, 128)
            turned = pair.T
            for chunk in range(8):
                mine, g = place(scal, chunk)
                piece = turned[chunk * ZS : (chunk + 1) * ZS][None]

                @pl.when(mine)
                def _():
                    keep[pl.ds(g, 1), f, i] = piece

                @pl.when(jnp.logical_not(mine))
                def _():
                    give[pl.ds(g, 1), f, i] = piece


def unpack_small(scal, wavelet, mine, other, ids_slab, ids_owner, depth, traces, pulse, pulse_depth, place):
    low = half_lanes((8, 128))
    h = scal[H]
    x_at = lax.broadcasted_iota(jnp.int32, (NXA, 128), 0)
    y_at = lax.broadcasted_iota(jnp.int32, (NXA, 128), 1)
    at_source = (x_at == scal[SX]) & (y_at == scal[SY])
    for t in range(STEPS):
        pulse[t] = jnp.where(at_source, wavelet[t], 0.0)
    pulse_depth[...] = jnp.full((NXA, 128), scal[SZ], jnp.int32)
    place[0] = jnp.full((8, 128), h, jnp.int32)
    place[1] = jnp.full((8, 128), jnp.where(is_edge(scal), 1, 0), jnp.int32)
    place[2] = jnp.full((8, 128), scal[LINE] * ZS - HALO, jnp.int32)
    for ix in range(GX):
        rows = slice(ix * BX, (ix + 1) * BX)
        for ref, is_mine in ((mine, True), (other, False)):
            a, b = ref[ix * GY], ref[ix * GY + 1]
            core = h if is_mine else 1 - h
            for tt in range(4):
                even = jnp.where(low, a[tt], roll_half(b[tt]))
                odd = jnp.where(low, roll_half(a[tt]), b[tt])
                traces[pl.ds(core * 8 + 2 * tt, 1), rows, :] = even[None]
                traces[pl.ds(core * 8 + 2 * tt + 1, 1), rows, :] = odd[None]
            ids = jnp.where(low, a[4], roll_half(b[4])).astype(jnp.int32)
            if is_mine:
                ids_owner[rows, :] = ids
                depth[rows, :] = jnp.where(low, roll_half(a[4]), b[4]).astype(jnp.int32)

            @pl.when(core == scal[IY])
            def _():
                ids_slab[rows, :] = ids


def gather_half(second, scal, table, ids, *refs):
    if second:
        before, out, sib, off = refs
    else:
        (out,) = refs
    half = 1 - scal[SHOT] if second else scal[SHOT]

    def column(x, carry):
        row = ids[pl.ds(x, 1), :]
        lane = jnp.broadcast_to(row & 127, (8, 128))
        chunk = jnp.broadcast_to(row >> 7, (8, 128))
        if second:
            totals = [before[x, 8 * t : 8 * t + 8, :] for t in range(4)]
        else:
            totals = [jnp.zeros((8, 128), F32) for t in range(4)]
        for j in range(32):
            hit = chunk == (j // 4) * 8 + half * 4 + j % 4
            for t in range(4):
                value = jnp.take_along_axis(
                    table[j // 4, j % 4, 8 * t : 8 * t + 8, :], lane, axis=1, mode="promise_in_bounds"
                )
                totals[t] = jnp.where(hit, value, totals[t])
        for t in range(4):
            out[x, 8 * t : 8 * t + 8, :] = totals[t]
        return carry

    lax.fori_loop(0, NXA, column, 0, unroll=4)
    if second:
        h = scal[H]
        for comp in range(2):
            rows = slice(comp * HALO, (comp + 1) * HALO)
            sib[:, rows, :] = out[:, pl.ds(comp * ZS + HALO * (1 - h), HALO), :]
            off[:, rows, :] = out[:, pl.ds(comp * ZS + HALO * h, HALO), :]


def is_edge(scal):
    return (scal[LINE] == 0) | (scal[LINE] == 2 * GX * GY - 1)


def extend_coefs(scal, coefs, sib, off, slow, aniso):
    sib_at = (ZE - HALO) * (1 - scal[H])
    off_at = (ZE - HALO) * scal[H]
    inside = jnp.where(is_edge(scal), 0.0, 1.0)
    slow[:, OWN, :] = coefs[:, 0:ZS, :] * UNSCALE
    slow[:, pl.ds(sib_at, HALO), :] = sib[:, 0:HALO, :] * UNSCALE
    slow[:, pl.ds(off_at, HALO), :] = off[:, 0:HALO, :] * (inside * UNSCALE)
    aniso[:, OWN, :] = 1.0 + 2.0 * coefs[:, ZS:, :]
    aniso[:, pl.ds(sib_at, HALO), :] = 1.0 + 2.0 * sib[:, HALO:, :]
    aniso[:, pl.ds(off_at, HALO), :] = 1.0 + 2.0 * off[:, HALO:, :]


def unpack_fields(scal, got, *outs):
    low = half_lanes((ZS, 128))
    h = scal[H]
    for kind in range(2):
        prev, now, sib, off = outs[4 * kind : 4 * kind + 4]
        for step, own in ((0, prev), (1, now)):
            f = 2 * kind + step
            for ix in range(GX):
                for i in range(4):
                    a, b = got[ix * GY, f, i], got[ix * GY + 1, f, i]
                    x = ix * BX + 2 * i
                    own[x] = jnp.where(low, a, roll_half(b))
                    own[x + 1] = jnp.where(low, roll_half(a), b)
        sib[0:NXA] = now[:, pl.ds(HALO * (1 - h), HALO), :]
        off[0:NXA] = now[:, pl.ds(HALO * h, HALO), :]
        upper = lax.broadcasted_iota(jnp.int32, (HALO, 128), 0) < HALO // 2
        for x in range(NXA // 2):
            one, two = prev[x], prev[x + NXA // 2]
            start = jnp.where(upper, one[:HALO], roll_tile(two[:HALO]))
            end = jnp.where(upper, roll_tile(one[HALO:]), two[HALO:])
            sib[NXA + x] = jnp.where(h == 0, end, start)
            off[NXA + x] = jnp.where(h == 0, start, end)


def index_kernel(scal, ids_slab, ids_owner, out):
    me = scal[IX] * GY + scal[IY]
    sub = lax.broadcasted_iota(jnp.int32, (8, 128), 0)
    lane = lax.broadcasted_iota(jnp.int32, (8, 128), 1)
    slots = []
    masks = [(jnp.broadcast_to(ids_slab[x : x + 1, :] >> 10, (8, 128)) == sub).astype(F32) for x in range(NXA)]
    for x in range(BX):
        rows = jnp.concatenate([ids_owner[s * BX + x : s * BX + x + 1, :] for s in range(GX)] * 2, axis=0)
        masks.append((((rows >> 10) == me) & (sub < GX)).astype(F32))
        slots.append((rows & 1023).astype(F32))
    bits = jnp.concatenate(masks, axis=0).astype(BF16)
    first = lax.broadcasted_iota(jnp.int32, (128, 128), 0)
    second = lax.broadcasted_iota(jnp.int32, (128, 128), 1)
    upto = (first <= second).astype(F32).astype(BF16)
    along = jnp.dot(bits, upto, preferred_element_type=F32)
    sums = jnp.dot(bits, jnp.ones((128, 128), BF16), preferred_element_type=F32)
    r0 = lax.broadcasted_iota(jnp.int32, (64, 64), 0)
    r1 = lax.broadcasted_iota(jnp.int32, (64, 64), 1)
    earlier = (((r0 & 7) == (r1 & 7)) & (r1 < r0)).astype(F32).astype(BF16)
    for group in range(GX + 1):
        rows = slice(64 * group, 64 * group + 64)
        above = jnp.dot(earlier, sums[rows].astype(BF16), preferred_element_type=F32)
        counts = along[rows] + above
        ends = sums[rows] + above
        for part in range(2):
            r = (lane + 128 * part).astype(F32)
            at_x = jnp.zeros((8, 128), jnp.int32)
            for x in range(BX):
                at_x = at_x + (ends[8 * x : 8 * x + 8] <= r).astype(jnp.int32)

            def pick(tables, at):
                value = jnp.zeros((8, 128), F32)
                for x in range(BX):
                    taken = jnp.take_along_axis(tables[x], at, axis=1, mode="promise_in_bounds")
                    value = jnp.where(at_x == x, taken, value)
                return value

            tables = [counts[8 * x : 8 * x + 8] for x in range(BX)]
            at_y = jnp.zeros((8, 128), jnp.int32)
            for step in (64, 32, 16, 8, 4, 2, 1):
                at_y = jnp.where(pick(tables, at_y + (step - 1)) <= r, at_y + step, at_y)
            at_y = jnp.minimum(at_y, 127)
            if group < GX:
                found = at_x * 128 + at_y
            else:
                found = pick(slots, at_y).astype(jnp.int32)
            out[part, 8 * group : 8 * group + 8] = jnp.where(at_x < BX, found, -1)


def bands_of(field, g, along_y, along_z, own):
    first = PADX + 8 * g
    depth = ZS if own else ZE
    whole = field[first : first + 8].reshape(8 * ZE, 128)
    high = whole.astype(BF16)
    rest = (whole - high.astype(F32)).astype(BF16)
    my = jnp.dot(jnp.concatenate([high, rest], axis=1), along_y[...], preferred_element_type=F32)
    mz = jnp.dot(along_z[...], jnp.concatenate([high, rest], axis=0), preferred_element_type=F32)
    return my.reshape(8, ZE, 128), mz.reshape(8, depth, 128)


def round_scratch():
    return [pltpu.VMEM(EXT_SHAPE, F32)]


def round_kernel(kind, r, *refs):
    refs = list(refs)
    take = lambda n: [refs.pop(0) for _ in range(n)]
    first, later, last = r == 0, r >= ROUNDS // 2, r == ROUNDS - 1
    place, drive, depth, own, sib, off, prev, slow, aniso, along_y, along_z, along_z_own = take(12)
    if later:
        if kind == "u":
            partner_mid, partner_end = take(2)
        else:
            (partner,) = take(1)
        if r > ROUNDS // 2:
            (total_in,) = take(1)
    out_own, out_mid = take(2)
    if not last:
        out_sib, out_off = take(2)
    if later:
        (total,) = take(1)
    elif kind == "u":
        (history,) = take(1)
    (e0,) = take(1)
    e1 = out_mid

    core_0 = place[0] == 0
    inside = place[1] == 0
    zero = jnp.zeros((PADX, ZE, 128), F32)
    for e in (e0, e1):
        e[0:PADX] = zero
        e[PADX + NXA :] = zero

    def extend(e, own, shared):
        for x in range(NXA):
            at = NXA + x % (NXA // 2) if shared else x
            near, far = sib[at], jnp.where(inside, off[at], 0.0)
            low, high = jnp.where(core_0, far, near), jnp.where(core_0, near, far)
            if shared and x < NXA // 2:
                low = roll_tile(low)
            elif shared:
                high = roll_tile(high)
            e[PADX + x, 0:HALO] = low
            e[PADX + x, OWN] = own[x]
            e[PADX + x, HALO + ZS :] = high

    extend(e0, own, False)
    if first:
        extend(e1, prev, True)
        prev = e1
    base = jnp.concatenate([place[2]] * (ZE // 8), axis=0) + lax.broadcasted_iota(jnp.int32, (ZE, 128), 0)

    def bands(step, g):
        if step:
            return bands_of(e1, g, along_y, along_z_own, True)
        return bands_of(e0, g, along_y, along_z, False)

    items = [(step, g) for step in range(2) for g in range(4)]
    ahead = bands(*items[0])
    for k, (step, g) in enumerate(items):
        my, mz = ahead
        if k + 1 < len(items):
            ahead = bands(*items[k + 1])
        t = 2 * r + step if kind == "u" else STEPS - 1 - (2 * r + step)
        field = e1 if step else e0
        zs = OWN if step else slice(0, ZE)
        count = ZS if step else ZE
        z = base[zs]
        for n in range(8):
            x = 8 * g + n
            at = PADX + x
            center = field[at, zs, :]
            hor = my[n, zs] + (2.0 * SCALE * STENCIL[0]) * center
            for i in range(1, 5):
                hor = hor + (SCALE * STENCIL[i]) * (field[at + i, zs, :] + field[at - i, zs, :])
            ver = mz[n] + (SCALE * STENCIL[0]) * center
            before = e0[at, OWN, :] if step else prev[at]
            lap = aniso[x, zs, :] * hor + ver
            following = 2.0 * center - before + slow[x, zs, :] * lap
            at_z = jnp.broadcast_to(depth[x : x + 1, :], (count, 128))
            value = jnp.broadcast_to(drive[t, x : x + 1, :], (count, 128))
            following = following + jnp.where(z == at_z, value, 0.0)
            if step:
                out_own[x] = following
                if not last:
                    low, high = following[:HALO], following[HALO:]
                    out_sib[x] = jnp.where(core_0, high, low)
                    out_off[x] = jnp.where(core_0, low, high)
            else:
                e1[at] = following
                hor, ver = hor[OWN], ver[OWN]
            if kind == "u" and not later:
                history[2 * step, x] = hor
                history[2 * step + 1, x] = ver
            if later:
                if kind == "u":
                    other = partner_mid[at, OWN, :] if step else partner_end[x]
                else:
                    other = following if step else following[OWN]
                    hor = partner[2 * (1 - step), x]
                    ver = partner[2 * (1 - step) + 1, x]
                sum_h, sum_v = other * hor, other * ver
                if step:
                    sum_h, sum_v = total[0, x] + sum_h, total[1, x] + sum_v
                elif r > ROUNDS // 2:
                    sum_h, sum_v = total_in[0, x] + sum_h, total_in[1, x] + sum_v
                total[0, x] = sum_h
                total[1, x] = sum_v


def pack_final(scal, u, a, *outs):
    low = half_lanes((ZS, 128))
    for n, out in enumerate(outs):
        block = block_of(scal, FAR_FIRST[n])
        for f, field in enumerate((u, a)):
            for i in range(4):
                x = (block >> 1) * BX + 2 * i
                x0 = field[pl.ds(x, 1)].reshape(ZS, 128)
                x1 = field[pl.ds(x + 1, 1)].reshape(ZS, 128)
                piece = jnp.where(low, x0, roll_half(x1))
                upper = jnp.where(low, roll_half(x0), x1)
                out[f, i] = jnp.where((block & 1) == 0, piece, upper)


def pack_grads(scal, index, total_u, total_a, coefs, *refs):
    outs, grads = refs[:8], refs[8]
    for x in range(NXA):
        gh = (total_u[0, x] + total_a[0, x]) * UNSCALE
        gv = (total_u[1, x] + total_a[1, x]) * UNSCALE
        slow, aniso = coefs[x, 0:ZS, :], coefs[x, ZS:, :]
        grads[x, 0:ZS, :] = (1.0 + 2.0 * aniso) * gh + gv
        grads[x, ZS:, :] = (2.0 * slow) * gh
    for n, out in enumerate(outs):
        block = block_of(scal, FAR_FIRST[n])

        def stripe(ix, carry, out=out, block=block):
            for part in range(2):
                row = index[part, pl.ds(ix * 8 + block, 1), :]
                lane = jnp.broadcast_to(row & 127, (8, 128))
                which = jnp.broadcast_to(row >> 7, (8, 128))
                totals = [jnp.zeros((8, 128), F32) for t in range(4)]
                for x in range(BX):
                    hit = which == x
                    for t in range(4):
                        value = jnp.take_along_axis(
                            grads[ix * BX + x, 8 * t : 8 * t + 8, :], lane, axis=1, mode="promise_in_bounds"
                        )
                        totals[t] = jnp.where(hit, value, totals[t])
                for t in range(4):
                    out[ix * 2 + part, 8 * t : 8 * t + 8, :] = totals[t]
            return carry

        lax.fori_loop(0, GX, stripe, 0, unroll=4)


def name_slots(index, picks):
    named = jnp.concatenate([index[n % 2, 32 + n // 2 : 33 + n // 2, :] for n in range(8)], axis=1)
    for block in range(4):
        slot = lax.broadcasted_iota(jnp.int32, (256, 1024), 0) + block * 256
        pick = slot == jnp.broadcast_to(named, (256, 1024))
        picks[block * 256 : (block + 1) * 256, :] = pick.astype(F32).astype(BF16)


def finish_fields(scal, *refs):
    gots, (u_out, a_out, turned) = refs[:8], refs[8:]
    for f, out in enumerate((u_out, a_out)):
        for i in range(4):
            for n, e in enumerate(FAR_FIRST):
                turned[f * 4 + i, pl.ds(slab_of(scal, e), ZS), :] = gots[n][f, i]
            out[2 * i : 2 * i + 2] = turned[f * 4 + i].T.reshape(2, BY, 128)


def finish_model(scal, picks, *refs):
    gots, (out, columns, model, sems) = refs[:8], refs[8:]
    for n, e in enumerate(FAR_FIRST):
        for comp in range(2):
            rows = pl.ds(pl.multiple_of(comp * 128 + slab_of(scal, e), ZS), ZS)
            for m in range(8):
                columns[rows, m * 128 : (m + 1) * 128] = gots[n][m, comp * ZS : (comp + 1) * ZS, :]
    values = columns[...].T
    high = values.astype(BF16)
    rest = (values - high.astype(F32)).astype(BF16)
    both = jnp.concatenate([high, rest], axis=1)
    copies = []
    for block in range(4):
        sums = jnp.dot(picks[block * 256 : (block + 1) * 256, :], both, preferred_element_type=F32)
        sums = sums[:, :256] + sums[:, 256:]
        for comp in range(2):
            model[pl.ds(block * 512 + comp, 256, stride=2), :] = sums[:, comp * 128 : (comp + 1) * 128]
        rows = pl.ds(block * 512, 512)
        copies.append(pltpu.make_async_copy(model.at[rows], out.at[rows], sems.at[block]))
        copies[-1].start()
    for copy in copies:
        copy.wait()


def by_half(h, mine, other):
    first = jnp.where(h == 0, mine, other)
    second = jnp.where(h == 0, other, mine)
    both = jnp.stack([first, second], axis=1)
    return both.reshape((GX * GY,) + mine.shape[1:])


def exchange(x):
    return lax.all_to_all(x, ("gx", "gy"), split_axis=0, concat_axis=0, tiled=True)


def slab_body(
    forward_prev,
    forward_now,
    adjoint_prev,
    adjoint_now,
    model_table,
    tile_owner,
    tile_slot,
    source_index,
    wavelet,
    receiver_depth,
    traces,
):
    h = lax.axis_index("gz")
    ix, iy = lax.axis_index("gx"), lax.axis_index("gy")
    chip = jnp.where(iy == 0, ix, 2 * GX - 1 - ix)
    line = 2 * chip + h
    scal = jnp.stack(
        [h, ix, iy, lax.axis_index("shots"), line, source_index[0], source_index[1], source_index[2]]
    ).astype(jnp.int32)

    trace_half = lax.dynamic_slice_in_dim(traces, h * 8, 8, axis=0)
    (small,) = call(pack_small, [((5, BX, 128), F32)], vmem(4), moved=MIB // 16, flops=1 << 16)(
        tile_owner.reshape(1, BX * BY), tile_slot.reshape(1, BX * BY), receiver_depth, trace_half
    )
    keep, give = call(
        pack_table, [((GX, 128, 128), F32)] * 2, [SMEM] + vmem(1), moved=2 * MIB, flops=1 << 20
    )(scal, model_table.reshape(2048, 128))
    (sent,) = call(assemble, [((GX * GY, 168, 128), F32)], [SMEM] + vmem(3), moved=2 * MIB, flops=1 << 20)(
        scal, keep, to_sibling(give), small
    )
    arrived = exchange(sent)
    table_mine = arrived[:, :128].reshape(8, 4, 32, 128)
    small_mine = arrived[:, 128:].reshape(8, 5, BX, 128)
    table_other = lax.ppermute(table_mine, "shots", SWAP)
    small_other = to_sibling(small_mine)

    keep, give = call(
        pack_fields, [((4, 4, 4, ZS, 128), F32)] * 2, [SMEM] + vmem(4), moved=2 * MIB, flops=1 << 20
    )(scal, forward_prev, forward_now, adjoint_prev, adjoint_now)
    fields = exchange(by_half(h, keep, to_sibling(give)))

    plane, drive = ((NXA, 128), jnp.int32), ((STEPS, NXA, 128), F32)
    ids_slab, ids_owner, depth, traces, pulse, pulse_depth, place_info = call(
        unpack_small,
        [plane] * 3 + [drive, drive, plane, ((3, 8, 128), jnp.int32)],
        [SMEM] * 2 + vmem(2),
        moved=MIB // 2,
        flops=1 << 20,
    )(scal, wavelet, small_mine, small_other)
    coef_shape = ((NXA, 2 * ZS, 128), F32)
    half_shape = ((NXA, 2 * HALO, 128), F32)
    (coefs,) = call(
        functools.partial(gather_half, False), [coef_shape], [SMEM] + vmem(2), moved=MIB, flops=1 << 24
    )(scal, table_mine, ids_slab)
    coefs, coefs_sib, coefs_off = call(
        functools.partial(gather_half, True),
        [coef_shape, half_shape, half_shape],
        [SMEM] + vmem(3),
        moved=2 * MIB,
        flops=1 << 24,
    )(scal, table_other, ids_slab, coefs)
    ext_shape = ((NXA, ZE, 128), F32)
    own_shape = ((NXA, ZS, 128), F32)
    slow, aniso = call(extend_coefs, [ext_shape] * 2, [SMEM] + vmem(3), moved=2 * MIB, flops=1 << 20)(
        scal, coefs, to_sibling(coefs_sib), to_off_chip(coefs_off)
    )
    (index,) = call(
        index_kernel,
        [((2, 40, 128), jnp.int32)],
        [SMEM] + vmem(2),
        moved=MIB // 4,
        flops=1 << 24,
    )(scal, ids_slab, ids_owner)

    fields, index = lax.optimization_barrier((fields, index))
    first_halo = ((NXA + NXA // 2, HALO, 128), F32)
    unpacked = call(
        unpack_fields,
        [own_shape, own_shape, first_halo, first_halo] * 2,
        [SMEM] + vmem(1),
        moved=4 * MIB,
        flops=1 << 20,
    )(scal, fields)
    bands = matrices()
    halo = ((NXA, HALO, 128), F32)
    state = {}
    for n, kind in enumerate("ua"):
        prev, now, sib, off = unpacked[4 * n : 4 * n + 4]
        state[kind] = [now, to_sibling(sib), to_off_chip(off), prev]
    history, mids, ends, totals = {}, {}, {}, {}
    for r in range(ROUNDS):
        for kind in "ua":
            later, last = r >= ROUNDS // 2, r == ROUNDS - 1
            args = [place_info] + ([pulse, pulse_depth] if kind == "u" else [traces, depth])
            args += state[kind] + [slow, aniso] + bands
            if later:
                partner = ROUNDS - 1 - r
                args += [mids[partner], ends[partner]] if kind == "u" else [history[partner]]
                if r > ROUNDS // 2:
                    args += [totals[kind]]
            outs = [own_shape, (EXT_SHAPE, F32)] + ([] if last else [halo, halo])
            if later:
                outs.append(((2, NXA, ZS, 128), F32))
            elif kind == "u":
                outs.append(((4, NXA, ZS, 128), F32))
            res = call(
                functools.partial(round_kernel, kind, r),
                outs,
                vmem(len(args)),
                round_scratch(),
                moved=4 * MIB,
                flops=1 << 24,
            )(*args)
            own, mid = res[0], res[1]
            if later:
                totals[kind] = res[-1]
            elif kind == "u":
                history[r] = res[-1]
            if kind == "a":
                mids[r], ends[r] = mid, own
            if last:
                state[kind] = [own]
            else:
                state[kind] = [own, to_sibling(res[2]), to_off_chip(res[3]), mid]

    final = call(
        pack_final, [((2, 4, ZS, 128), F32)] * 8, [SMEM] + vmem(2), moved=MIB, flops=1 << 20
    )(scal, state["u"][0], state["a"][0])
    final = [to_blocks(x, e) for x, e in zip(final, FAR_FIRST)]
    columns = call(
        pack_grads,
        [((8, 2 * ZS, 128), F32)] * 8,
        [SMEM] + vmem(4),
        [pltpu.VMEM((NXA, 2 * ZS, 128), F32)],
        moved=16 * MIB,
        flops=1 << 22,
    )(scal, index, totals["u"], totals["a"], coefs)
    index, _ = lax.optimization_barrier((index, columns[7]))
    (picks,) = call(name_slots, [((1024, 1024), BF16)], vmem(1), moved=4 * MIB, flops=1 << 22)(index)
    columns = [to_blocks(x, e) for x, e in zip(columns, FAR_FIRST)]
    u, a = call(
        finish_fields,
        [((BX, BY, BZ), F32)] * 2,
        [SMEM] + vmem(8),
        [pltpu.VMEM((8, 128, 128), F32)],
        moved=MIB,
        flops=1 << 20,
    )(scal, *final)
    model = pl.pallas_call(
        finish_model,
        out_shape=jax.ShapeDtypeStruct((2048, 128), F32),
        in_specs=[SMEM] + vmem(9),
        out_specs=pl.BlockSpec(memory_space=pl.ANY),
        scratch_shapes=[
            pltpu.VMEM((256, 1024), F32),
            pltpu.VMEM((2048, 128), F32),
            pltpu.SemaphoreType.DMA((4,)),
        ],
        compiler_params=pltpu.CompilerParams(vmem_limit_bytes=24 * MIB),
        cost_estimate=pl.CostEstimate(flops=1 << 28, bytes_accessed=4 * MIB, transcendentals=0),
    )(scal, picks, *columns)
    return (u, a, model.reshape(1, 1024, 2, 128))


def solution(mesh):
    in_specs = (
        P(("shots", "gx"), "gy", "gz"),
        P(("shots", "gx"), "gy", "gz"),
        P(("shots", "gx"), "gy", "gz"),
        P(("shots", "gx"), "gy", "gz"),
        P("gz", ("gx", "gy"), None, None),
        P(("shots", "gz"), "gx", "gy", None, None),
        P(("shots", "gz"), "gx", "gy", None),
        P("shots"),
        P("shots"),
        P(("shots", "gx"), "gy"),
        P(None, ("shots", "gx"), "gy"),
    )
    out_specs = (
        P(("shots", "gx"), "gy", "gz"),
        P(("shots", "gx"), "gy", "gz"),
        P("gz", ("shots", "gx", "gy"), None, None),
    )
    body = slab_body if slabs_fit(mesh) else block_body
    return jax.shard_map(body, mesh=mesh, in_specs=in_specs, out_specs=out_specs, check_vma=False)
```
